512 devices in a mesh: dp: 32 (over y, x), feat: 16 (over z, core).
Axes of the slice: x: 4, y: 8, z: 8, core: 2. Of those that a mesh axis runs over, the one named last changes fastest.
Arguments:
- features: bfloat16 [65536, 1024], P('dp', 'feat'), may hold values from -6 to 6
- request_rows: int32 [32, 32, 512], P('dp'), may hold values from 0 to 2047
- self_slots: int32 [32, 704], P('dp'), may hold values from 0 to 16383
- adj_one: int32 [32, 704, 10], P('dp'), may hold values from 0 to 16383
- deg_one: int32 [32, 704], P('dp'), may hold values from 1 to 10
- adj_two: int32 [32, 64, 10], P('dp'), may hold values from 0 to 703
- deg_two: int32 [32, 64], P('dp'), may hold values from 1 to 10
- w1_self: bfloat16 [1024, 256], P('feat'), may hold values from -0.1875 to 0.1875
- w1_neigh: bfloat16 [1024, 256], P('feat'), may hold values from -0.1875 to 0.1875
- w2_self: bfloat16 [256, 256], replicated, may hold values from -0.375 to 0.375
- w2_neigh: bfloat16 [256, 256], replicated, may hold values from -0.375 to 0.375
- out_grad: bfloat16 [2048, 256], P('dp'), may hold values from -0.078125 to 0.078125
Outputs:
- embeddings: bfloat16 [2048, 256], P('dp')
- grad_w1_self: float32 [1024, 256], P('feat')
- grad_w1_neigh: float32 [1024, 256], P('feat')
- grad_w2_self: float32 [256, 256], replicated
- grad_w2_neigh: float32 [256, 256], replicated
The draws below stay inside these ranges and needn't reach their ends.
Inputs may be any that keep to these rules, and one draw needn't show every extreme that they name: `adj_one`: entries of a padded list past its count are arbitrary valid slots and must not be used.
All inputs are finite; a program needn't handle non-finite values.
Results may differ from the reference program's by a relative error of at most 0.006.
Values may be sent and summed in bfloat16 or wider, within the bound.
A program may use at most 64 MiB of HBM per device.

```python
import jax
import jax.numpy as jnp
from jax import lax

F = 1024
HID = 256
OUT = 256
K = 10
TGT_DEV = 64
NODE_DEV = 2048
SLOTS = 16384
CAP = 512
H1 = 704
NODES = 65536
TARGETS = 2048
N_DP = 32


def plant(entries, rng, low, largest):
    longest = entries.shape.index(max(entries.shape))
    spots = []
    for shift in (0, 1):
        where = [jax.random.randint(jax.random.fold_in(rng, axis), (), 0, length) for axis, length in enumerate(entries.shape)]
        where[longest] = (where[longest] + shift) % entries.shape[longest]
        spots.append(tuple(where))
    return entries.at[spots[0]].set(low).at[spots[1]].set(largest)


def block_scale(key, dims, shards, smallest, largest):
    def one(axis_at, parts):
        draws = jax.random.uniform(jax.random.fold_in(jax.random.fold_in(key, 6), axis_at), (parts,), jnp.float32, smallest / len(shards), largest / len(shards))
        return jnp.repeat(jnp.exp(draws), dims[axis_at] // parts).reshape((-1,) + (1,) * (len(dims) - axis_at - 1))

    level = one(*shards[0])
    for cut in shards[1:]:
        level = level * one(*cut)
    return level


def noise(stream_key, shape, deviation, bound, shards=(), kind=jnp.bfloat16):
    array = jax.random.normal(stream_key, shape, jnp.float32) * deviation
    if len(shards) > 0:
        array = block_scale(stream_key, shape, shards, -0.22, 0.18) * array
    return jnp.clip(array, min=-bound, max=bound).astype(kind)


def setup_inputs(seed: int = 0) -> dict:
    seeds = jax.random.split(jax.random.key(seed), 13)
    features = noise(seeds[0], (NODES, F), 1.0, 6.0, ((0, 32), (1, 16)))
    request_rows = plant(jax.random.randint(seeds[1], (N_DP, N_DP, CAP), 0, NODE_DEV), jax.random.fold_in(seeds[1], 1), 0, NODE_DEV - 1).astype(jnp.int32)
    self_slots = plant(jax.random.randint(seeds[2], (N_DP, H1), 0, SLOTS), jax.random.fold_in(seeds[2], 1), 0, SLOTS - 1).astype(jnp.int32)
    adj_one = plant(jax.random.randint(seeds[3], (N_DP, H1, K), 0, SLOTS), jax.random.fold_in(seeds[3], 1), 0, SLOTS - 1).astype(jnp.int32)
    deg_one = plant(jax.random.randint(seeds[4], (N_DP, H1), 1, K + 1), jax.random.fold_in(seeds[4], 1), 1, K).astype(jnp.int32)
    adj_two = plant(jax.random.randint(seeds[5], (N_DP, TGT_DEV, K), 0, H1), jax.random.fold_in(seeds[5], 1), 0, H1 - 1).astype(jnp.int32)
    deg_two = plant(jax.random.randint(seeds[6], (N_DP, TGT_DEV), 1, K + 1), jax.random.fold_in(seeds[6], 1), 1, K).astype(jnp.int32)
    w1_self = noise(seeds[7], (F, HID), F ** -0.5, 0.1875, ((0, 16),))
    w1_neigh = noise(seeds[8], (F, HID), F ** -0.5, 0.1875, ((0, 16),))
    w2_self = noise(seeds[9], (HID, OUT), HID ** -0.5, 0.375)
    w2_neigh = noise(seeds[10], (HID, OUT), HID ** -0.5, 0.375)
    out_grad = noise(seeds[11], (TARGETS, OUT), (TARGETS * (1 + K) // 4) ** -0.5, 0.078125, ((0, 32),))
    return {"features": features, "request_rows": request_rows, "self_slots": self_slots, "adj_one": adj_one, "deg_one": deg_one, "adj_two": adj_two, "deg_two": deg_two, "w1_self": w1_self, "w1_neigh": w1_neigh, "w2_self": w2_self, "w2_neigh": w2_neigh, "out_grad": out_grad}


def slot_weights(neighbours, degrees):
    fanout = neighbours.shape[-1]
    present = jnp.arange(fanout, dtype=jnp.int32)[None, :] < degrees[:, None]
    return present.astype(jnp.float32) / degrees[:, None].astype(jnp.float32)


def neighbour_mean(source, neighbours, degrees):
    weights = slot_weights(neighbours, degrees)
    gathered = source[neighbours].astype(jnp.float32)
    return jnp.sum(gathered * weights[:, :, None], axis=1).astype(jnp.bfloat16)


def mixing_matrix(neighbours, degrees, row_count):
    weights = slot_weights(neighbours, degrees)
    columns = jnp.arange(row_count, dtype=jnp.int32)[None, :]
    accumulated = jnp.zeros((neighbours.shape[0], row_count), jnp.float32)
    for position in range(neighbours.shape[1]):
        match = (neighbours[:, position:position + 1] == columns).astype(jnp.float32)
        accumulated = accumulated + weights[:, position:position + 1] * match
    return accumulated


def silu_slope(pre):
    sigmoid_part = jax.nn.sigmoid(pre)
    return sigmoid_part * (1.0 + pre * (1.0 - sigmoid_part))


def reference(features, request_rows, self_slots, adj_one, deg_one, adj_two, deg_two, w1_self, w1_neigh, w2_self, w2_neigh, out_grad):
    owner_base = jnp.arange(N_DP, dtype=jnp.int32)[:, None] * NODE_DEV

    def one_group(inputs):
        requests, selfs, neigh_one, count_one, neigh_two, count_two, cotangent = inputs
        sampled = features[(owner_base + requests).reshape(-1)]
        own_rows = sampled[selfs]
        agg_one = neighbour_mean(sampled, neigh_one, count_one)
        pre_one = jnp.dot(own_rows, w1_self, preferred_element_type=jnp.float32) + jnp.dot(agg_one, w1_neigh, preferred_element_type=jnp.float32)
        hidden = jax.nn.silu(pre_one).astype(jnp.bfloat16)
        mixing = mixing_matrix(neigh_two, count_two, H1)
        agg_two = jnp.dot(mixing, hidden.astype(jnp.float32), precision=lax.Precision.HIGHEST).astype(jnp.bfloat16)
        summed = jnp.dot(hidden[:TGT_DEV], w2_self, preferred_element_type=jnp.float32) + jnp.dot(agg_two, w2_neigh, preferred_element_type=jnp.float32)
        embeddings = summed.astype(jnp.bfloat16)
        grad_w2_self = jnp.dot(hidden[:TGT_DEV].T, cotangent, preferred_element_type=jnp.float32)
        grad_w2_neigh = jnp.dot(agg_two.T, cotangent, preferred_element_type=jnp.float32)
        grad_agg = jnp.dot(cotangent, w2_neigh.T, preferred_element_type=jnp.float32)
        grad_hidden = jnp.dot(mixing.T, grad_agg, precision=lax.Precision.HIGHEST)
        grad_hidden = grad_hidden.at[:TGT_DEV].add(jnp.dot(cotangent, w2_self.T, preferred_element_type=jnp.float32))
        grad_pre = (grad_hidden * silu_slope(pre_one)).astype(jnp.bfloat16)
        grad_w1_self = jnp.dot(own_rows.T, grad_pre, preferred_element_type=jnp.float32)
        grad_w1_neigh = jnp.dot(agg_one.T, grad_pre, preferred_element_type=jnp.float32)
        return embeddings, grad_w1_self, grad_w1_neigh, grad_w2_self, grad_w2_neigh

    results = lax.map(one_group, (request_rows, self_slots, adj_one, deg_one, adj_two, deg_two, out_grad.reshape(N_DP, TGT_DEV, OUT)))
    embeddings = results[0].reshape(N_DP * TGT_DEV, OUT)
    return (embeddings, jnp.sum(results[1], axis=0), jnp.sum(results[2], axis=0), jnp.sum(results[3], axis=0), jnp.sum(results[4], axis=0))
```

```python
import functools

import jax
import jax.numpy as jnp
from jax import lax
from jax.experimental import pallas as pl
from jax.experimental.pallas import tpu as pltpu
from jax.sharding import PartitionSpec as P

MESH = pl.DeviceIdType.MESH
ROWS = 768


def slot_weights(neighbours, degrees):
    fanout = neighbours.shape[-1]
    present = jnp.arange(fanout, dtype=jnp.int32)[None, :] < degrees[:, None]
    return present.astype(jnp.float32) / degrees[:, None].astype(jnp.float32)


def neighbour_mean(source, neighbours, degrees):
    weights = slot_weights(neighbours, degrees)
    gathered = source[neighbours].astype(jnp.float32)
    return jnp.sum(gathered * weights[:, :, None], axis=1).astype(jnp.bfloat16)


def contract_rows(a, b):
    return lax.dot_general(a, b, (((0,), (0,)), ((), ())), preferred_element_type=jnp.float32)


def contract_lanes(a, b):
    return lax.dot_general(a, b, (((1,), (1,)), ((), ())), preferred_element_type=jnp.float32)


def each(count, body):
    def step(k, carry):
        body(k)
        return carry

    lax.fori_loop(1, count, step, 0)


def tail_kernel(
    nd, nf,
    oa_ref, w1_ref, w2s_ref, w2n_ref, grad_ref, adj_ref, deg_ref,
    emb_ref, gw1_ref, gw2_ref,
    rows_buf, gh_buf, hg_buf, part1, part2, in1, in2, sum1, sum2, slice2,
    send_a, recv_a, send_h, recv_h, send_r, recv_r, send_q, recv_q,
    send_g, recv_g, send_b, recv_b, send_f, recv_f,
):
    d = lax.axis_index("dp")
    f = lax.axis_index("feat")
    block = ROWS // nf

    def feat_peer(k):
        return lax.rem(f + k, nf)

    def dp_peer(k):
        return lax.rem(d + k, nd)

    barrier = pltpu.get_barrier_semaphore()

    def greet_feat(k):
        pl.semaphore_signal(barrier, inc=1, device_id=(d, feat_peer(k)), device_id_type=MESH)

    def greet_dp(k):
        pl.semaphore_signal(barrier, inc=1, device_id=(dp_peer(k), f), device_id_type=MESH)

    each(nf, greet_feat)
    each(nd, greet_dp)
    pl.semaphore_wait(barrier, nf - 1 + nd - 1)

    def rows_at(index):
        return pl.ds(pl.multiple_of(index * block, 16), block)

    my_columns = pl.ds(pl.multiple_of(f * 128, 128), 128)

    def row_copy(k):
        to = feat_peer(k)
        return pltpu.make_async_remote_copy(
            src_ref=oa_ref.at[rows_at(to), :],
            dst_ref=rows_buf.at[:, my_columns],
            send_sem=send_a.at[k], recv_sem=recv_a.at[k],
            device_id=(d, to), device_id_type=MESH,
        )

    each(nf, lambda k: row_copy(k).start())
    rows_buf[:, my_columns] = oa_ref[rows_at(f), :]

    out_grad = grad_ref[...]
    degree = deg_ref[...].astype(jnp.float32)
    targets = degree.shape[0]
    column = lax.broadcasted_iota(jnp.int32, (targets, ROWS), 1)
    counts = jnp.zeros((targets, ROWS), jnp.float32)
    for j in range(adj_ref.shape[1]):
        match = (adj_ref[:, j:j + 1] == column) & (deg_ref[...] > j)
        counts = counts + jnp.where(match, 1.0, 0.0)
    grad_agg = contract_lanes(out_grad, w2n_ref[...]) / degree
    gh_buf[...] = lax.dot_general(
        counts, grad_agg, (((0,), (0,)), ((), ())),
        precision=lax.Precision.HIGHEST, preferred_element_type=jnp.float32,
    )
    gh_buf[:targets, :] += contract_lanes(out_grad, w2s_ref[...])

    each(nf, lambda k: row_copy(k).wait())
    pre = jnp.dot(rows_buf[...], w1_ref[...], preferred_element_type=jnp.float32)
    sig = 1.0 / (1.0 + jnp.exp(-pre))
    grad_pre = gh_buf[rows_at(f), :] * (sig * (1.0 + pre * (1.0 - sig)))
    hg_buf[rows_at(f), :256] = (pre * sig).astype(jnp.bfloat16)
    hg_buf[rows_at(f), 256:] = grad_pre.astype(jnp.bfloat16)

    def hidden_copy(k):
        return pltpu.make_async_remote_copy(
            src_ref=hg_buf.at[rows_at(f), :],
            dst_ref=hg_buf.at[rows_at(f), :],
            send_sem=send_h.at[k], recv_sem=recv_h.at[k],
            device_id=(d, feat_peer(k)), device_id_type=MESH,
        )

    def hidden_arrived(k):
        here = lax.rem(f - k + nf, nf)
        pltpu.make_async_remote_copy(
            src_ref=hg_buf.at[rows_at(f), :],
            dst_ref=hg_buf.at[rows_at(here), :],
            send_sem=send_h.at[k], recv_sem=recv_h.at[k],
            device_id=(d, feat_peer(k)), device_id_type=MESH,
        ).wait_recv()

    each(nf, lambda k: hidden_copy(k).start())
    each(nf, hidden_arrived)

    part1[...] = contract_rows(oa_ref[...], hg_buf[:, 256:])
    self_hidden = hg_buf[:targets, :256]
    agg_two = jnp.dot(counts.astype(jnp.bfloat16), hg_buf[:, :256], preferred_element_type=jnp.float32)
    agg_two = (agg_two / degree).astype(jnp.bfloat16)
    part2[0] = contract_rows(self_hidden, out_grad)
    part2[1] = contract_rows(agg_two, out_grad)

    def tile_of(part):
        return (
            pl.ds(pl.multiple_of(lax.div(part, 2) * 8, 8), 8),
            pl.ds(pl.multiple_of(lax.rem(part, 2) * 128, 128), 128),
        )

    def w1_copy(k):
        to = dp_peer(k)
        rows, lanes = tile_of(to)
        return pltpu.make_async_remote_copy(
            src_ref=part1.at[rows, lanes],
            dst_ref=in1.at[d],
            send_sem=send_r.at[k], recv_sem=recv_r.at[k],
            device_id=(to, f), device_id_type=MESH,
        )

    def w2_tile(part):
        return (
            lax.div(part, 4),
            pl.ds(pl.multiple_of(f * 16 + lax.rem(lax.div(part, 2), 2) * 8, 8), 8),
            pl.ds(pl.multiple_of(lax.rem(part, 2) * 128, 128), 128),
        )

    def keeper(part):
        return part * 4 + lax.rem(part, 4)

    my_part = lax.div(d, 4)
    keeping = keeper(my_part) == d

    def w2_copy(part):
        to = keeper(part)
        which, rows, lanes = w2_tile(part)
        return pltpu.make_async_remote_copy(
            src_ref=part2.at[which, rows, lanes],
            dst_ref=in2.at[d],
            send_sem=send_q.at[part], recv_sem=recv_q.at[d],
            device_id=(to, f), device_id_type=MESH,
        )

    def w2_send(part):
        @pl.when(keeper(part) != d)
        def _():
            w2_copy(part).start()

    lax.fori_loop(0, 8, lambda k, c: (w2_send(k), c)[1], 0)
    each(nd, lambda k: w1_copy(k).start())

    emb = jnp.dot(self_hidden, w2s_ref[...], preferred_element_type=jnp.float32)
    emb = emb + jnp.dot(agg_two, w2n_ref[...], preferred_element_type=jnp.float32)
    emb_ref[...] = emb.astype(jnp.bfloat16)

    def w2_in(k):
        here = lax.rem(d - k + nd, nd)
        pltpu.make_async_remote_copy(
            src_ref=in2.at[here], dst_ref=in2.at[here],
            send_sem=send_q.at[0], recv_sem=recv_q.at[here],
            device_id=(here, f), device_id_type=MESH,
        ).wait_recv()

    mine2 = pl.ds(pl.multiple_of(my_part // 2 * 8, 8), 8)
    lanes2 = pl.ds(pl.multiple_of(lax.rem(my_part, 2) * 128, 128), 128)

    def w2_out(k):
        return pltpu.make_async_remote_copy(
            src_ref=sum2, dst_ref=slice2.at[mine2, lanes2],
            send_sem=send_b.at[k], recv_sem=recv_b.at[my_part],
            device_id=(dp_peer(k), f), device_id_type=MESH,
        )

    @pl.when(keeping)
    def _():
        which, rows, lanes = w2_tile(my_part)
        in2[d] = part2[which, rows, lanes]
        each(nd, w2_in)
        sum2[...] = jnp.sum(in2[...], axis=0)
        each(nd, lambda k: w2_out(k).start())
        slice2[mine2, lanes2] = sum2[...]

    my_rows, my_lanes = tile_of(d)
    in1[d] = part1[my_rows, my_lanes]

    def w1_in(k):
        here = lax.rem(d - k + nd, nd)
        pltpu.make_async_remote_copy(
            src_ref=in1.at[here], dst_ref=in1.at[here],
            send_sem=send_r.at[k], recv_sem=recv_r.at[k],
            device_id=(here, f), device_id_type=MESH,
        ).wait_recv()

    each(nd, w1_in)
    sum1[...] = jnp.sum(in1[...], axis=0)
    gw1_ref[my_rows, my_lanes] = sum1[...]

    def w1_out(k):
        return pltpu.make_async_remote_copy(
            src_ref=sum1, dst_ref=gw1_ref.at[my_rows, my_lanes],
            send_sem=send_g.at[k], recv_sem=recv_g.at[k],
            device_id=(dp_peer(k), f), device_id_type=MESH,
        )

    each(nd, lambda k: w1_out(k).start())

    def w2_back(part):
        @pl.when(keeper(part) != d)
        def _():
            rows = pl.ds(pl.multiple_of(lax.div(part, 2) * 8, 8), 8)
            lanes = pl.ds(pl.multiple_of(lax.rem(part, 2) * 128, 128), 128)
            pltpu.make_async_remote_copy(
                src_ref=sum2, dst_ref=slice2.at[rows, lanes],
                send_sem=send_b.at[0], recv_sem=recv_b.at[part],
                device_id=(keeper(part), f), device_id_type=MESH,
            ).wait_recv()

    lax.fori_loop(0, 8, lambda k, c: (w2_back(k), c)[1], 0)
    gw2_ref[f] = slice2[...]

    def slice_copy(k):
        return pltpu.make_async_remote_copy(
            src_ref=slice2, dst_ref=gw2_ref.at[f],
            send_sem=send_f.at[k], recv_sem=recv_f.at[k],
            device_id=(d, feat_peer(k)), device_id_type=MESH,
        )

    each(nf, lambda k: slice_copy(k).start())

    def w1_back(k):
        rows, lanes = tile_of(lax.rem(d - k + nd, nd))
        pltpu.make_async_remote_copy(
            src_ref=sum1, dst_ref=gw1_ref.at[rows, lanes],
            send_sem=send_g.at[k], recv_sem=recv_g.at[k],
            device_id=(dp_peer(k), f), device_id_type=MESH,
        ).wait_recv()

    each(nd, w1_back)

    def slice_back(k):
        here = lax.rem(f - k + nf, nf)
        pltpu.make_async_remote_copy(
            src_ref=slice2, dst_ref=gw2_ref.at[here],
            send_sem=send_f.at[k], recv_sem=recv_f.at[k],
            device_id=(d, feat_peer(k)), device_id_type=MESH,
        ).wait_recv()

    each(nf, slice_back)

    each(nf, lambda k: hidden_copy(k).wait_send())
    each(nd, lambda k: w1_copy(k).wait_send())

    def w2_sent(part):
        @pl.when(keeper(part) != d)
        def _():
            w2_copy(part).wait_send()

    lax.fori_loop(0, 8, lambda k, c: (w2_sent(k), c)[1], 0)

    @pl.when(keeping)
    def _():
        each(nd, lambda k: w2_out(k).wait_send())

    each(nd, lambda k: w1_out(k).wait_send())
    each(nf, lambda k: slice_copy(k).wait_send())


def finish_kernel(emb_ref, gw1_ref, gw2_ref, out_emb, out_1s, out_1n, out_2s, out_2n):
    out_emb[...] = emb_ref[...]
    out_1s[...] = gw1_ref[:64, :]
    out_1n[...] = gw1_ref[64:, :]
    for i in range(gw2_ref.shape[0]):
        out_2s[16 * i:16 * i + 16, :] = gw2_ref[i, :16, :]
        out_2n[16 * i:16 * i + 16, :] = gw2_ref[i, 16:, :]


def tail(nd, nf, oa, w1, w2s, w2n, out_grad, adj_two, deg_two):
    vmem = pl.BlockSpec(memory_space=pltpu.VMEM)
    f32, bf16 = jnp.float32, jnp.bfloat16
    dma = pltpu.SemaphoreType.DMA
    emb, gw1, gw2 = pl.pallas_call(
        functools.partial(tail_kernel, nd, nf),
        out_shape=(
            jax.ShapeDtypeStruct((64, 256), bf16),
            jax.ShapeDtypeStruct((128, 256), f32),
            jax.ShapeDtypeStruct((nf, 32, 256), f32),
        ),
        in_specs=[vmem] * 7,
        out_specs=(vmem,) * 3,
        scratch_shapes=[
            pltpu.VMEM((ROWS // nf, nf * 128), bf16),
            pltpu.VMEM((ROWS, 256), f32),
            pltpu.VMEM((ROWS, 512), bf16),
            pltpu.VMEM((128, 256), f32),
            pltpu.VMEM((2, 256, 256), f32),
            pltpu.VMEM((nd, 8, 128), f32),
            pltpu.VMEM((nd, 8, 128), f32),
            pltpu.VMEM((8, 128), f32),
            pltpu.VMEM((8, 128), f32),
            pltpu.VMEM((32, 256), f32),
            dma((nf,)), dma((nf,)), dma((nf,)), dma((nf,)),
            dma((nd,)), dma((nd,)), dma((8,)), dma((nd,)),
            dma((nd,)), dma((nd,)), dma((nd,)), dma((8,)),
            dma((nf,)), dma((nf,)),
        ],
        compiler_params=pltpu.CompilerParams(
            collective_id=1, has_side_effects=True, vmem_limit_bytes=32 * 1024 * 1024
        ),
        name="tail",
    )(oa, w1, w2s, w2n, out_grad, adj_two, deg_two)
    return pl.pallas_call(
        finish_kernel,
        out_shape=(
            jax.ShapeDtypeStruct((64, 256), bf16),
            jax.ShapeDtypeStruct((64, 256), f32),
            jax.ShapeDtypeStruct((64, 256), f32),
            jax.ShapeDtypeStruct((256, 256), f32),
            jax.ShapeDtypeStruct((256, 256), f32),
        ),
        in_specs=[vmem] * 3,
        out_specs=(vmem,) * 5,
        name="finish",
    )(emb, gw1, gw2)


def local(
    nd, nf,
    features, request_rows, self_slots, adj_one, deg_one, adj_two, deg_two,
    w1_self, w1_neigh, w2_self, w2_neigh, out_grad,
):
    columns_here = features.shape[1]
    w1 = lax.all_gather(jnp.concatenate([w1_self, w1_neigh], axis=0), "feat", tiled=True)
    asked_rows = lax.all_to_all(request_rows, "dp", split_axis=1, concat_axis=0, tiled=True)
    picked = features[asked_rows.reshape(-1)].reshape(asked_rows.shape + (columns_here,))
    replies = lax.all_to_all(picked, "dp", split_axis=0, concat_axis=1, tiled=True)
    sampled = replies.reshape(-1, columns_here)
    own_rows = sampled[self_slots[0]]
    agg_one = neighbour_mean(sampled, adj_one[0], deg_one[0])
    oa = jnp.concatenate([own_rows, agg_one], axis=1)
    oa = jnp.pad(oa, ((0, ROWS - oa.shape[0]), (0, 0)))
    return tail(nd, nf, oa, w1, w2_self, w2_neigh, out_grad, adj_two[0], deg_two[0][:, None])


def solution(mesh):
    return jax.shard_map(
        functools.partial(local, mesh.shape["dp"], mesh.shape["feat"]),
        mesh=mesh,
        in_specs=(
            P("dp", "feat"),
            P("dp", None, None),
            P("dp", None),
            P("dp", None, None),
            P("dp", None),
            P("dp", None, None),
            P("dp", None),
            P("feat", None),
            P("feat", None),
            P(),
            P(),
            P("dp", None),
        ),
        out_specs=(P("dp", None), P("feat", None), P("feat", None), P(), P()),
        check_vma=False,
    )
```

```python
import functools

import jax
import jax.numpy as jnp
from jax import lax
from jax.experimental import pallas as pl
from jax.experimental.pallas import tpu as pltpu
from jax.sharding import PartitionSpec as P

MESH = pl.DeviceIdType.MESH
ROWS = 768


def contract_rows(a, b):
    return lax.dot_general(a, b, (((0,), (0,)), ((), ())), preferred_element_type=jnp.float32)


def contract_lanes(a, b):
    return lax.dot_general(a, b, (((1,), (1,)), ((), ())), preferred_element_type=jnp.float32)


def each(count, body):
    def step(k, carry):
        body(k)
        return carry

    lax.fori_loop(1, count, step, 0)


def tail_kernel(
    nd, nf,
    oa_ref, w1_ref, w2s_ref, w2n_ref, grad_ref, adj_ref, deg_ref,
    emb_ref, gw1_ref, gw2_ref,
    rows_buf, gh_buf, hg_buf, part1, part2, in1, in2, sum1, sum2, slice2,
    send_a, recv_a, send_h, recv_h, send_r, recv_r, send_q, recv_q,
    send_g, recv_g, send_b, recv_b, send_f, recv_f,
):
    d = lax.axis_index("dp")
    f = lax.axis_index("feat")
    block = ROWS // nf

    def feat_peer(k):
        return lax.rem(f + k, nf)

    def dp_peer(k):
        return lax.rem(d + k, nd)

    barrier = pltpu.get_barrier_semaphore()

    def greet_feat(k):
        pl.semaphore_signal(barrier, inc=1, device_id=(d, feat_peer(k)), device_id_type=MESH)

    def greet_dp(k):
        pl.semaphore_signal(barrier, inc=1, device_id=(dp_peer(k), f), device_id_type=MESH)

    each(nf, greet_feat)
    each(nd, greet_dp)
    pl.semaphore_wait(barrier, nf - 1 + nd - 1)

    def rows_at(index):
        return pl.ds(pl.multiple_of(index * block, 16), block)

    my_columns = pl.ds(pl.multiple_of(f * 128, 128), 128)

    def row_copy(k):
        to = feat_peer(k)
        return pltpu.make_async_remote_copy(
            src_ref=oa_ref.at[rows_at(to), :],
            dst_ref=rows_buf.at[:, my_columns],
            send_sem=send_a.at[k], recv_sem=recv_a.at[k],
            device_id=(d, to), device_id_type=MESH,
        )

    each(nf, lambda k: row_copy(k).start())
    rows_buf[:, my_columns] = oa_ref[rows_at(f), :]

    out_grad = grad_ref[...]
    degree = deg_ref[...].astype(jnp.float32)
    targets = degree.shape[0]
    column = lax.broadcasted_iota(jnp.int32, (targets, ROWS), 1)
    counts = jnp.zeros((targets, ROWS), jnp.float32)
    for j in range(adj_ref.shape[1]):
        match = (adj_ref[:, j:j + 1] == column) & (deg_ref[...] > j)
        counts = counts + jnp.where(match, 1.0, 0.0)
    grad_agg = contract_lanes(out_grad, w2n_ref[...]) / degree
    gh_buf[...] = lax.dot_general(
        counts, grad_agg, (((0,), (0,)), ((), ())),
        precision=lax.Precision.HIGHEST, preferred_element_type=jnp.float32,
    )
    gh_buf[:targets, :] += contract_lanes(out_grad, w2s_ref[...])

    each(nf, lambda k: row_copy(k).wait())
    pre = jnp.dot(rows_buf[...], w1_ref[...], preferred_element_type=jnp.float32)
    sig = 1.0 / (1.0 + jnp.exp(-pre))
    grad_pre = gh_buf[rows_at(f), :] * (sig * (1.0 + pre * (1.0 - sig)))
    hg_buf[rows_at(f), :256] = (pre * sig).astype(jnp.bfloat16)
    hg_buf[rows_at(f), 256:] = grad_pre.astype(jnp.bfloat16)

    def hidden_copy(k):
        return pltpu.make_async_remote_copy(
            src_ref=hg_buf.at[rows_at(f), :],
            dst_ref=hg_buf.at[rows_at(f), :],
            send_sem=send_h.at[k], recv_sem=recv_h.at[k],
            device_id=(d, feat_peer(k)), device_id_type=MESH,
        )

    def hidden_arrived(k):
        here = lax.rem(f - k + nf, nf)
        pltpu.make_async_remote_copy(
            src_ref=hg_buf.at[rows_at(f), :],
            dst_ref=hg_buf.at[rows_at(here), :],
            send_sem=send_h.at[k], recv_sem=recv_h.at[k],
            device_id=(d, feat_peer(k)), device_id_type=MESH,
        ).wait_recv()

    each(nf, lambda k: hidden_copy(k).start())
    each(nf, hidden_arrived)

    part1[...] = contract_rows(oa_ref[...], hg_buf[:, 256:])
    self_hidden = hg_buf[:targets, :256]
    agg_two = jnp.dot(counts.astype(jnp.bfloat16), hg_buf[:, :256], preferred_element_type=jnp.float32)
    agg_two = (agg_two / degree).astype(jnp.bfloat16)
    part2[0] = contract_rows(self_hidden, out_grad)
    part2[1] = contract_rows(agg_two, out_grad)

    def tile_of(part):
        return (
            pl.ds(pl.multiple_of(lax.div(part, 2) * 8, 8), 8),
            pl.ds(pl.multiple_of(lax.rem(part, 2) * 128, 128), 128),
        )

    def w1_copy(k):
        to = dp_peer(k)
        rows, lanes = tile_of(to)
        return pltpu.make_async_remote_copy(
            src_ref=part1.at[rows, lanes],
            dst_ref=in1.at[d],
            send_sem=send_r.at[k], recv_sem=recv_r.at[k],
            device_id=(to, f), device_id_type=MESH,
        )

    def w2_tile(part):
        return (
            lax.div(part, 4),
            pl.ds(pl.multiple_of(f * 16 + lax.rem(lax.div(part, 2), 2) * 8, 8), 8),
            pl.ds(pl.multiple_of(lax.rem(part, 2) * 128, 128), 128),
        )

    def keeper(part):
        return part * 4 + lax.rem(part, 4)

    my_part = lax.div(d, 4)
    keeping = keeper(my_part) == d

    def w2_copy(part):
        to = keeper(part)
        which, rows, lanes = w2_tile(part)
        return pltpu.make_async_remote_copy(
            src_ref=part2.at[which, rows, lanes],
            dst_ref=in2.at[d],
            send_sem=send_q.at[part], recv_sem=recv_q.at[d],
            device_id=(to, f), device_id_type=MESH,
        )

    def w2_send(part):
        @pl.when(keeper(part) != d)
        def _():
            w2_copy(part).start()

    lax.fori_loop(0, 8, lambda k, c: (w2_send(k), c)[1], 0)
    each(nd, lambda k: w1_copy(k).start())

    emb = jnp.dot(self_hidden, w2s_ref[...], preferred_element_type=jnp.float32)
    emb = emb + jnp.dot(agg_two, w2n_ref[...], preferred_element_type=jnp.float32)
    emb_ref[...] = emb.astype(jnp.bfloat16)

    def w2_in(k):
        here = lax.rem(d - k + nd, nd)
        pltpu.make_async_remote_copy(
            src_ref=in2.at[here], dst_ref=in2.at[here],
            send_sem=send_q.at[0], recv_sem=recv_q.at[here],
            device_id=(here, f), device_id_type=MESH,
        ).wait_recv()

    mine2 = pl.ds(pl.multiple_of(my_part // 2 * 8, 8), 8)
    lanes2 = pl.ds(pl.multiple_of(lax.rem(my_part, 2) * 128, 128), 128)

    def w2_out(k):
        return pltpu.make_async_remote_copy(
            src_ref=sum2, dst_ref=slice2.at[mine2, lanes2],
            send_sem=send_b.at[k], recv_sem=recv_b.at[my_part],
            device_id=(dp_peer(k), f), device_id_type=MESH,
        )

    @pl.when(keeping)
    def _():
        which, rows, lanes = w2_tile(my_part)
        in2[d] = part2[which, rows, lanes]
        each(nd, w2_in)
        sum2[...] = jnp.sum(in2[...], axis=0)
        each(nd, lambda k: w2_out(k).start())
        slice2[mine2, lanes2] = sum2[...]

    my_rows, my_lanes = tile_of(d)
    in1[d] = part1[my_rows, my_lanes]

    def w1_in(k):
        here = lax.rem(d - k + nd, nd)
        pltpu.make_async_remote_copy(
            src_ref=in1.at[here], dst_ref=in1.at[here],
            send_sem=send_r.at[k], recv_sem=recv_r.at[k],
            device_id=(here, f), device_id_type=MESH,
        ).wait_recv()

    each(nd, w1_in)
    sum1[...] = jnp.sum(in1[...], axis=0)
    gw1_ref[my_rows, my_lanes] = sum1[...]

    def w1_out(k):
        return pltpu.make_async_remote_copy(
            src_ref=sum1, dst_ref=gw1_ref.at[my_rows, my_lanes],
            send_sem=send_g.at[k], recv_sem=recv_g.at[k],
            device_id=(dp_peer(k), f), device_id_type=MESH,
        )

    each(nd, lambda k: w1_out(k).start())

    def w2_back(part):
        @pl.when(keeper(part) != d)
        def _():
            rows = pl.ds(pl.multiple_of(lax.div(part, 2) * 8, 8), 8)
            lanes = pl.ds(pl.multiple_of(lax.rem(part, 2) * 128, 128), 128)
            pltpu.make_async_remote_copy(
                src_ref=sum2, dst_ref=slice2.at[rows, lanes],
                send_sem=send_b.at[0], recv_sem=recv_b.at[part],
                device_id=(keeper(part), f), device_id_type=MESH,
            ).wait_recv()

    lax.fori_loop(0, 8, lambda k, c: (w2_back(k), c)[1], 0)
    gw2_ref[f] = slice2[...]

    def slice_copy(k):
        return pltpu.make_async_remote_copy(
            src_ref=slice2, dst_ref=gw2_ref.at[f],
            send_sem=send_f.at[k], recv_sem=recv_f.at[k],
            device_id=(d, feat_peer(k)), device_id_type=MESH,
        )

    each(nf, lambda k: slice_copy(k).start())

    def w1_back(k):
        rows, lanes = tile_of(lax.rem(d - k + nd, nd))
        pltpu.make_async_remote_copy(
            src_ref=sum1, dst_ref=gw1_ref.at[rows, lanes],
            send_sem=send_g.at[k], recv_sem=recv_g.at[k],
            device_id=(dp_peer(k), f), device_id_type=MESH,
        ).wait_recv()

    each(nd, w1_back)

    def slice_back(k):
        here = lax.rem(f - k + nf, nf)
        pltpu.make_async_remote_copy(
            src_ref=slice2, dst_ref=gw2_ref.at[here],
            send_sem=send_f.at[k], recv_sem=recv_f.at[k],
            device_id=(d, feat_peer(k)), device_id_type=MESH,
        ).wait_recv()

    each(nf, slice_back)

    each(nf, lambda k: hidden_copy(k).wait_send())
    each(nd, lambda k: w1_copy(k).wait_send())

    def w2_sent(part):
        @pl.when(keeper(part) != d)
        def _():
            w2_copy(part).wait_send()

    lax.fori_loop(0, 8, lambda k, c: (w2_sent(k), c)[1], 0)

    @pl.when(keeping)
    def _():
        each(nd, lambda k: w2_out(k).wait_send())

    each(nd, lambda k: w1_out(k).wait_send())
    each(nf, lambda k: slice_copy(k).wait_send())


def finish_kernel(emb_ref, gw1_ref, gw2_ref, out_emb, out_1s, out_1n, out_2s, out_2n):
    out_emb[...] = emb_ref[...]
    out_1s[...] = gw1_ref[:64, :]
    out_1n[...] = gw1_ref[64:, :]
    for i in range(gw2_ref.shape[0]):
        out_2s[16 * i:16 * i + 16, :] = gw2_ref[i, :16, :]
        out_2n[16 * i:16 * i + 16, :] = gw2_ref[i, 16:, :]


def tail(nd, nf, oa, w1, w2s, w2n, out_grad, adj_two, deg_two):
    vmem = pl.BlockSpec(memory_space=pltpu.VMEM)
    f32, bf16 = jnp.float32, jnp.bfloat16
    dma = pltpu.SemaphoreType.DMA
    emb, gw1, gw2 = pl.pallas_call(
        functools.partial(tail_kernel, nd, nf),
        out_shape=(
            jax.ShapeDtypeStruct((64, 256), bf16),
            jax.ShapeDtypeStruct((128, 256), f32),
            jax.ShapeDtypeStruct((nf, 32, 256), f32),
        ),
        in_specs=[vmem] * 7,
        out_specs=(vmem,) * 3,
        scratch_shapes=[
            pltpu.VMEM((ROWS // nf, nf * 128), bf16),
            pltpu.VMEM((ROWS, 256), f32),
            pltpu.VMEM((ROWS, 512), bf16),
            pltpu.VMEM((128, 256), f32),
            pltpu.VMEM((2, 256, 256), f32),
            pltpu.VMEM((nd, 8, 128), f32),
            pltpu.VMEM((nd, 8, 128), f32),
            pltpu.VMEM((8, 128), f32),
            pltpu.VMEM((8, 128), f32),
            pltpu.VMEM((32, 256), f32),
            dma((nf,)), dma((nf,)), dma((nf,)), dma((nf,)),
            dma((nd,)), dma((nd,)), dma((8,)), dma((nd,)),
            dma((nd,)), dma((nd,)), dma((nd,)), dma((8,)),
            dma((nf,)), dma((nf,)),
        ],
        compiler_params=pltpu.CompilerParams(
            collective_id=1, has_side_effects=True, vmem_limit_bytes=32 * 1024 * 1024
        ),
        name="tail",
    )(oa, w1, w2s, w2n, out_grad, adj_two, deg_two)
    return pl.pallas_call(
        finish_kernel,
        out_shape=(
            jax.ShapeDtypeStruct((64, 256), bf16),
            jax.ShapeDtypeStruct((64, 256), f32),
            jax.ShapeDtypeStruct((64, 256), f32),
            jax.ShapeDtypeStruct((256, 256), f32),
            jax.ShapeDtypeStruct((256, 256), f32),
        ),
        in_specs=[vmem] * 3,
        out_specs=(vmem,) * 5,
        name="finish",
    )(emb, gw1, gw2)


def front_kernel(
    nd, nf, feat_ref, req_ref, w1_ref, samp_ref, w1_out,
    blocks, req_by_x, req_in, stage,
    up_send, up_recv, down_send, down_recv, req_send, req_recv,
    x_send, x_recv, w1_send, w1_recv, local_sem,
):
    d = lax.axis_index("dp")
    f = lax.axis_index("feat")
    nx, ny = 4, nd // 4
    x, y = lax.rem(d, nx), lax.div(d, nx)

    def at_x(j):
        return lax.rem(x + j, nx)

    def at_y(s):
        return lax.rem(y + s + ny, ny)

    def feat_peer(k):
        return lax.rem(f + k, nf)

    barrier = pltpu.get_barrier_semaphore()

    def greet(to):
        pl.semaphore_signal(barrier, inc=1, device_id=to, device_id_type=MESH)

    for j in range(1, nx):
        greet((y * nx + at_x(j), f))
    greet((at_y(1) * nx + x, f))
    greet((at_y(-1) * nx + x, f))
    each(nf, lambda k: greet((d, feat_peer(k))))

    for q in range(4):
        blocks[y, 64 * q:64 * q + 64, :] = feat_ref[:, 512 * q:512 * q + 512]
    for owner in range(nd):
        req_by_x[owner % nx, owner // nx:owner // nx + 1, :] = req_ref[owner:owner + 1, :]

    pl.semaphore_wait(barrier, nx - 1 + 2 + nf - 1)

    def req_copy(j):
        to = at_x(j)
        return pltpu.make_async_remote_copy(
            src_ref=req_by_x.at[to], dst_ref=req_in.at[x],
            send_sem=req_send.at[j], recv_sem=req_recv.at[x],
            device_id=(y * nx + to, f), device_id_type=MESH,
        )

    def half(source, h):
        return blocks.at[source, pl.ds(128 * h, 128), :]

    def up_copy(t, source):
        return pltpu.make_async_remote_copy(
            src_ref=half(source, t % 2), dst_ref=half(source, t % 2),
            send_sem=up_send.at[t], recv_sem=up_recv.at[t],
            device_id=(at_y(1) * nx + x, f), device_id_type=MESH,
        )

    def down_copy(t, source):
        return pltpu.make_async_remote_copy(
            src_ref=half(source, 1 - t % 2), dst_ref=half(source, 1 - t % 2),
            send_sem=down_send.at[t], recv_sem=down_recv.at[t],
            device_id=(at_y(-1) * nx + x, f), device_id_type=MESH,
        )

    def w1_copy(k):
        return pltpu.make_async_remote_copy(
            src_ref=w1_ref, dst_ref=w1_out.at[f],
            send_sem=w1_send.at[k], recv_sem=w1_recv.at[k],
            device_id=(d, feat_peer(k)), device_id_type=MESH,
        )

    for j in range(1, nx):
        req_copy(j).start()
    for t in range(2):
        up_copy(t, y).start()
        down_copy(t, y).start()
    each(nf, lambda k: w1_copy(k).start())
    own_w1 = pltpu.make_async_copy(w1_ref, w1_out.at[f], local_sem.at[ny])
    own_w1.start()
    req_in[x] = req_by_x[x]
    for j in range(1, nx):
        source = at_x(j)
        pltpu.make_async_remote_copy(
            src_ref=req_by_x.at[source], dst_ref=req_in.at[source],
            send_sem=req_send.at[j], recv_sem=req_recv.at[source],
            device_id=(y * nx + source, f), device_id_type=MESH,
        ).wait_recv()

    def x_copy(source, j):
        slot = source * nx + x
        return pltpu.make_async_remote_copy(
            src_ref=stage.at[source, j], dst_ref=samp_ref.at[slot],
            send_sem=x_send.at[source * nx + j], recv_sem=x_recv.at[slot],
            device_id=(y * nx + at_x(j), f), device_id_type=MESH,
        )

    def own_copy(source):
        return pltpu.make_async_copy(
            stage.at[source, 0], samp_ref.at[source * nx + x], local_sem.at[source]
        )

    node = lax.broadcasted_iota(jnp.int32, (512, 512), 0)

    def pick(source, j):
        asked = req_in[at_x(j), pl.ds(source, 1), :]
        low, quarter = asked & 511, asked >> 9
        one_hot = jnp.where(node == low, 1.0, 0.0).astype(jnp.bfloat16)
        rows = jnp.dot(blocks[source], one_hot, preferred_element_type=jnp.float32)
        chosen = rows[192:256, :]
        for q in range(3):
            chosen = jnp.where(quarter == q, rows[64 * q:64 * q + 64, :], chosen)
        stage[source, j] = chosen.astype(jnp.bfloat16)

    def process(count, source_of):
        def step(k, carry):
            source = source_of(lax.div(k, nx))
            j = lax.rem(k + 1, nx)
            pick(source, j)

            @pl.when(j > 0)
            def _():
                x_copy(source, j).start()

            @pl.when(j == 0)
            def _():
                own_copy(source).start()

            return carry

        lax.fori_loop(0, count * nx, step, 0)

    process(1, lambda i: y)
    for s in range(ny // 2):
        below, above = at_y(-1 - s), at_y(1 + s)
        for h in range(2 if s < ny // 2 - 1 else 1):
            t = 2 * s + h
            up_copy(t, below).wait_recv()
            if t + 2 < ny - 1:
                up_copy(t + 2, below).start()
            down_copy(t, above).wait_recv()
            if t + 2 < ny - 1:
                down_copy(t + 2, above).start()
        if s < ny // 2 - 1:
            process(2, lambda i: lax.rem(y + (2 * i - 1) * (1 + s) + ny, ny))
        else:
            process(1, lambda i: below)

    def x_back(source):
        for j in range(1, nx):
            slot = source * nx + at_x(j)
            pltpu.make_async_remote_copy(
                src_ref=stage.at[source, j], dst_ref=samp_ref.at[slot],
                send_sem=x_send.at[source * nx + j], recv_sem=x_recv.at[slot],
                device_id=(y * nx + at_x(j), f), device_id_type=MESH,
            ).wait_recv()
            x_copy(source, j).wait_send()
        own_copy(source).wait()

    lax.fori_loop(0, ny, lambda k, c: (x_back(k), c)[1], 0)

    def w1_back(k):
        here = lax.rem(f - k + nf, nf)
        pltpu.make_async_remote_copy(
            src_ref=w1_ref, dst_ref=w1_out.at[here],
            send_sem=w1_send.at[k], recv_sem=w1_recv.at[k],
            device_id=(d, here), device_id_type=MESH,
        ).wait_recv()
        w1_copy(k).wait_send()

    each(nf, w1_back)
    own_w1.wait()
    for j in range(1, nx):
        req_copy(j).wait_send()
    for t in range(ny - 1):
        up_copy(t, at_y(-(t // 2))).wait_send()
        down_copy(t, at_y(t // 2)).wait_send()


def front(nd, nf, features, request_rows, w1):
    vmem = pl.BlockSpec(memory_space=pltpu.VMEM)
    anywhere = pl.BlockSpec(memory_space=pl.ANY)
    bf16, i32 = jnp.bfloat16, jnp.int32
    dma = pltpu.SemaphoreType.DMA
    ny = nd // 4
    return pl.pallas_call(
        functools.partial(front_kernel, nd, nf),
        out_shape=(
            jax.ShapeDtypeStruct((nd, 64, 512), bf16),
            jax.ShapeDtypeStruct((nf, 128, 256), bf16),
        ),
        in_specs=[vmem] * 3,
        out_specs=(anywhere, anywhere),
        scratch_shapes=[
            pltpu.VMEM((ny, 256, 512), bf16),
            pltpu.VMEM((4, ny, 512), i32),
            pltpu.VMEM((4, ny, 512), i32),
            pltpu.VMEM((ny, 4, 64, 512), bf16),
            dma((ny - 1,)), dma((ny - 1,)), dma((ny - 1,)), dma((ny - 1,)),
            dma((4,)), dma((4,)), dma((nd,)), dma((nd,)),
            dma((nf,)), dma((nf,)), dma((ny + 1,)),
        ],
        compiler_params=pltpu.CompilerParams(
            collective_id=2, has_side_effects=True, vmem_limit_bytes=32 * 1024 * 1024
        ),
        name="front",
    )(features.T, request_rows, w1)


def mean_kernel(slots_ref, samp_ref, scale_ref, out_ref, table, own, total):
    pairs, width, cap = samp_ref.shape

    def unpack(p, carry):
        both = samp_ref[p].astype(jnp.float32).T
        table[pl.ds(pl.multiple_of(2 * cap * p, 8), cap), :] = both
        table[pl.ds(pl.multiple_of(2 * cap * p + cap, 8), cap), :] = pltpu.roll(both, 64, 1)
        return carry

    lax.fori_loop(0, pairs, unpack, 0)
    table[2 * cap * pairs:, :] = jnp.zeros((8, width), jnp.float32)
    rows = scale_ref.shape[0]
    lists = slots_ref.shape[0] // rows

    def gather(block, carry):
        for r in range(8):
            i = block * 8 + r
            own[pl.ds(i, 1), :] = table[pl.ds(slots_ref[i], 1), :]
            terms = [table[pl.ds(slots_ref[j * rows + i], 1), :] for j in range(1, lists)]
            while len(terms) > 1:
                terms = [sum(terms[k:k + 2][1:], terms[k]) for k in range(0, len(terms), 2)]
            total[pl.ds(i, 1), :] = terms[0]
        return carry

    lax.fori_loop(0, rows // 8, gather, 0)
    lane = lax.broadcasted_iota(jnp.int32, (rows, width), 1)
    mean = pltpu.roll(total[...] * scale_ref[...], 64, 1)
    out_ref[:rows, :] = jnp.where(lane < 64, own[...], mean).astype(jnp.bfloat16)
    out_ref[rows:, :] = jnp.zeros((ROWS - rows, width), jnp.bfloat16)


def neighbour_mean(sampled, self_slots, neighbours, degrees):
    nd, columns, cap = sampled.shape
    rows, fanout = neighbours.shape
    order = jnp.arange(fanout, dtype=jnp.int32)[:, None]
    listed = jnp.where(order < degrees[None, :], neighbours.T, nd * cap)
    slots = jnp.concatenate([self_slots[None, :], listed], axis=0).reshape(-1)
    scale = 1.0 / degrees.astype(jnp.float32)[:, None]
    vmem = pl.BlockSpec(memory_space=pltpu.VMEM)
    return pl.pallas_call(
        mean_kernel,
        out_shape=jax.ShapeDtypeStruct((ROWS, 2 * columns), jnp.bfloat16),
        in_specs=[pl.BlockSpec(memory_space=pltpu.SMEM), vmem, vmem],
        out_specs=vmem,
        scratch_shapes=[
            pltpu.VMEM((nd * cap + 8, 2 * columns), jnp.float32),
            pltpu.VMEM((rows, 2 * columns), jnp.float32),
            pltpu.VMEM((rows, 2 * columns), jnp.float32),
        ],
        compiler_params=pltpu.CompilerParams(vmem_limit_bytes=32 * 1024 * 1024),
        name="mean",
    )(slots, sampled.reshape(nd // 2, 2 * columns, cap), scale)


def local(
    nd, nf,
    features, request_rows, self_slots, adj_one, deg_one, adj_two, deg_two,
    w1_self, w1_neigh, w2_self, w2_neigh, out_grad,
):
    w1 = jnp.concatenate([w1_self, w1_neigh], axis=0)
    sampled, w1 = front(nd, nf, features, request_rows[0], w1)
    oa = neighbour_mean(sampled, self_slots[0], adj_one[0], deg_one[0])
    w1 = w1.reshape(-1, w1.shape[-1])
    return tail(nd, nf, oa, w1, w2_self, w2_neigh, out_grad, adj_two[0], deg_two[0][:, None])


def solution(mesh):
    return jax.shard_map(
        functools.partial(local, mesh.shape["dp"], mesh.shape["feat"]),
        mesh=mesh,
        in_specs=(
            P("dp", "feat"),
            P("dp", None, None),
            P("dp", None),
            P("dp", None, None),
            P("dp", None),
            P("dp", None, None),
            P("dp", None),
            P("feat", None),
            P("feat", None),
            P(),
            P(),
            P("dp", None),
        ),
        out_specs=(P("dp", None), P("feat", None), P("feat", None), P(), P()),
        check_vma=False,
    )
```

```python
import functools

import jax
import jax.numpy as jnp
from jax import lax
from jax.experimental import pallas as pl
from jax.experimental.pallas import tpu as pltpu
from jax.sharding import PartitionSpec as P

MESH = pl.DeviceIdType.MESH
ROWS = 768


def contract_rows(a, b):
    return lax.dot_general(a, b, (((0,), (0,)), ((), ())), preferred_element_type=jnp.float32)


def contract_lanes(a, b):
    return lax.dot_general(a, b, (((1,), (1,)), ((), ())), preferred_element_type=jnp.float32)


def each(count, body):
    def step(k, carry):
        body(k)
        return carry

    lax.fori_loop(1, count, step, 0)


Z_ORDER = (4, 3, 5, 2, 6, 1, 7)


def tail_kernel(
    nd, nf,
    oa_ref, w1_any, w2s_any, w2n_any, grad_any, adj_any, deg_any,
    emb_ref, gw1_ref, gw2_ref,
    w1, w2s, w2n, grad_ref, adj_ref, deg_ref, both, x_in, gh_buf, hid, gpre, grads, turned, w2_in, part1, in1, sum1,
    fetch, sib_send, sib_recv, a_send, a_recv, h_send, h_recv, p_send, p_recv,
    g_send, g_recv, q_send, q_recv, r_send, r_recv, b_send, b_recv, f_send, f_recv,
):
    d = lax.axis_index("dp")
    f = lax.axis_index("feat")
    nz = nf // 2
    z, c = lax.div(f, 2), lax.rem(f, 2)
    block = ROWS // nf
    half = ROWS // 2
    mine = c * nz + z
    sibling = (d, 2 * z + 1 - c)

    def along_z(k):
        to = lax.rem(z + k, nz)
        return to, (d, 2 * to + c)

    def dp_peer(k):
        return lax.rem(d + k, nd)

    def remote(src, dst, send_sem, recv_sem, to):
        return pltpu.make_async_remote_copy(
            src_ref=src, dst_ref=dst, send_sem=send_sem, recv_sem=recv_sem,
            device_id=to, device_id_type=MESH,
        )

    fetches = [
        pltpu.make_async_copy(w1_any, w1, fetch.at[0]),
        pltpu.make_async_copy(w2s_any, w2s, fetch.at[1]),
        pltpu.make_async_copy(w2n_any, w2n, fetch.at[2]),
        pltpu.make_async_copy(adj_any, adj_ref, fetch.at[3]),
        pltpu.make_async_copy(deg_any, deg_ref, fetch.at[4]),
        pltpu.make_async_copy(grad_any, grad_ref, fetch.at[5]),
    ]
    for copy in reversed(fetches):
        copy.start()

    barrier = pltpu.get_barrier_semaphore()

    def greet(to):
        pl.semaphore_signal(barrier, inc=1, device_id=to, device_id_type=MESH)

    greet(sibling)
    for k in range(1, nz):
        greet(along_z(k)[1])
    each(nd, lambda k: greet((dp_peer(k), f)))
    mine_c = pl.ds(pl.multiple_of(c * half, 16), half)
    other_c = pl.ds(pl.multiple_of((1 - c) * half, 16), half)
    both[c] = oa_ref[mine_c, :]
    g_rows = pl.ds(pl.multiple_of(c * 32, 16), 32)
    for copy in fetches[1:]:
        copy.wait()
    grads[d, g_rows, :] = grad_ref[g_rows, :]
    pl.semaphore_wait(barrier, 1 + nz - 1 + nd - 1)

    swap = remote(oa_ref.at[other_c, :], both.at[c], sib_send.at[0], sib_recv.at[0], sibling)
    swap.start()
    swap.wait()

    def rows_of(index):
        return pl.ds(pl.multiple_of(index * block, 16), block)

    def row_copy(k):
        to, device = along_z(k)
        return remote(both.at[:, rows_of(to), :], x_in.at[z], a_send.at[k], a_recv.at[z], device)

    def row_back(k):
        source, device = along_z(k)
        return remote(both.at[:, rows_of(source), :], x_in.at[source], a_send.at[k], a_recv.at[source], device)

    for k in Z_ORDER:
        row_copy(k).start()

    def grad_copy(k):
        to = (dp_peer(k), f)
        return remote(grad_ref.at[g_rows, :], grads.at[d, g_rows, :], g_send.at[k], g_recv.at[k], to)

    each(nd, lambda k: grad_copy(k).start())
    x_in[z] = both[:, rows_of(z), :]

    out_grad = grad_ref[...]
    degree_row = deg_ref[...]
    targets = degree_row.shape[1]
    row = lax.broadcasted_iota(jnp.int32, (ROWS, targets), 0)
    counts = jnp.zeros((ROWS, targets), jnp.float32)
    for j in range(adj_ref.shape[0]):
        listed = jnp.where(degree_row > j, adj_ref[j], -1)
        counts = counts + jnp.where(row == listed, 1.0, 0.0)
    degree_row = degree_row.astype(jnp.float32)
    degree = jnp.broadcast_to(degree_row, (8, targets)).T[:, :1]
    grad_agg = contract_lanes(out_grad, w2n[...]) / degree
    gh_buf[...] = jnp.dot(
        counts, grad_agg, precision=lax.Precision.HIGHEST, preferred_element_type=jnp.float32
    )
    gh_buf[:targets, :] += contract_lanes(out_grad, w2s[...])
    counts = counts.T.astype(jnp.bfloat16)
    fetches[0].wait()

    for k in Z_ORDER:
        row_back(k).wait_recv()
    pre = jnp.zeros((block, w1.shape[-1]), jnp.float32)
    for source in range(nz):
        for core in range(2):
            pre = pre + jnp.dot(x_in[source, core], w1[core, source], preferred_element_type=jnp.float32)
    sig = 1.0 / (1.0 + jnp.exp(-pre))
    grad_pre = gh_buf[rows_of(mine), :] * (sig * (1.0 + pre * (1.0 - sig)))
    hid[mine] = (pre * sig).astype(jnp.bfloat16)
    gpre[mine] = grad_pre.astype(jnp.bfloat16)

    def spread(buf, send_sem, recv_sem, k):
        return remote(buf.at[mine], buf.at[mine], send_sem.at[k], recv_sem.at[z], along_z(k)[1])

    def spread_back(buf, send_sem, recv_sem, k):
        source, device = along_z(k)
        slot = c * nz + source
        return remote(buf.at[slot], buf.at[slot], send_sem.at[k], recv_sem.at[source], device)

    def hand_over(buf, i):
        ours = buf.at[pl.ds(c * nz, nz)]
        return remote(ours, ours, sib_send.at[i], sib_recv.at[i], sibling)

    def handed(buf, i):
        theirs = buf.at[pl.ds((1 - c) * nz, nz)]
        return remote(theirs, theirs, sib_send.at[i], sib_recv.at[i], sibling)

    for k in Z_ORDER:
        spread(hid, h_send, h_recv, k).start()
    for k in Z_ORDER:
        spread(gpre, p_send, p_recv, k).start()

    def grad_in(k):
        here = lax.rem(d - k + nd, nd)
        return remote(
            grads.at[here, g_rows, :], grads.at[here, g_rows, :], g_send.at[k], g_recv.at[k], (here, f)
        )

    each(nd, lambda k: grad_in(k).wait_recv())
    grads_over = remote(
        grads.at[:, g_rows, :], grads.at[:, g_rows, :], sib_send.at[1], sib_recv.at[1], sibling
    )
    grads_over.start()

    for k in Z_ORDER:
        spread_back(hid, h_send, h_recv, k).wait_recv()
    hand_over(hid, 2).start()
    handed(hid, 2).wait_recv()

    hidden = hid[...].reshape(ROWS, hid.shape[-1])
    self_hidden = hidden[:targets, :]
    agg_two = jnp.dot(counts, hidden, preferred_element_type=jnp.float32) / degree
    agg_two = agg_two.astype(jnp.bfloat16)
    pair = jnp.concatenate([self_hidden, agg_two], axis=0)
    turned[...] = pair.astype(jnp.float32).T.astype(jnp.bfloat16)
    columns = pl.ds(pl.multiple_of(f * 16, 16), 16)
    w2_in[d] = turned[columns, :]

    def w2_copy(k):
        return remote(turned.at[columns, :], w2_in.at[d], q_send.at[k], q_recv.at[k], (dp_peer(k), f))

    def w2_back(k):
        here = lax.rem(d - k + nd, nd)
        return remote(w2_in.at[here], w2_in.at[here], q_send.at[k], q_recv.at[k], (here, f))

    each(nd, lambda k: w2_copy(k).start())

    for k in Z_ORDER:
        spread_back(gpre, p_send, p_recv, k).wait_recv()
    hand_over(gpre, 3).start()
    handed(gpre, 3).wait_recv()
    part1[...] = contract_rows(oa_ref[...], gpre[...].reshape(ROWS, gpre.shape[-1]))

    def tile_of(part):
        return (
            pl.ds(pl.multiple_of(lax.div(part, 2) * 8, 8), 8),
            pl.ds(pl.multiple_of(lax.rem(part, 2) * 128, 128), 128),
        )

    my_rows, my_lanes = tile_of(d)

    def w1_copy(k):
        to = dp_peer(k)
        rows, lanes = tile_of(to)
        return remote(part1.at[rows, lanes], in1.at[d], r_send.at[k], r_recv.at[k], (to, f))

    def w1_in(k):
        here = lax.rem(d - k + nd, nd)
        return remote(in1.at[here], in1.at[here], r_send.at[k], r_recv.at[k], (here, f))

    each(nd, lambda k: w1_copy(k).start())
    in1[d] = part1[my_rows, my_lanes]
    emb = jnp.dot(self_hidden, w2s[...], preferred_element_type=jnp.float32)
    emb = emb + jnp.dot(agg_two, w2n[...], preferred_element_type=jnp.float32)
    emb_ref[...] = emb.astype(jnp.bfloat16)

    grads_over.wait_send()
    remote(
        grads.at[:, pl.ds(pl.multiple_of((1 - c) * 32, 16), 32), :],
        grads.at[:, pl.ds(pl.multiple_of((1 - c) * 32, 16), 32), :],
        sib_send.at[1], sib_recv.at[1], sibling,
    ).wait_recv()
    each(nd, lambda k: w2_back(k).wait_recv())
    lane = lax.broadcasted_iota(jnp.int32, (16, 128), 1)
    total2 = jnp.zeros((32, out_grad.shape[-1]), jnp.float32)
    for p in range(nd // 2):
        first, second = w2_in[2 * p].astype(jnp.float32), w2_in[2 * p + 1].astype(jnp.float32)
        selfs = jnp.where(lane < 64, first, pltpu.roll(second, 64, 1))
        neighs = jnp.where(lane < 64, pltpu.roll(first, 64, 1), second)
        left = jnp.concatenate([selfs, neighs], axis=0).astype(jnp.bfloat16)
        right = grads[2 * p:2 * p + 2].reshape(128, out_grad.shape[-1])
        total2 = total2 + jnp.dot(left, right, preferred_element_type=jnp.float32)
    gw2_ref[mine] = total2.astype(jnp.bfloat16)
    for k in Z_ORDER:
        spread(gw2_ref, f_send, f_recv, k).start()

    each(nd, lambda k: w1_in(k).wait_recv())
    sum1[...] = jnp.sum(in1[...], axis=0)
    gw1_ref[my_rows, my_lanes] = sum1[...]

    def w1_out(k):
        return remote(sum1, gw1_ref.at[my_rows, my_lanes], b_send.at[k], b_recv.at[k], (dp_peer(k), f))

    def w1_back(k):
        here = lax.rem(d - k + nd, nd)
        rows, lanes = tile_of(here)
        return remote(sum1, gw1_ref.at[rows, lanes], b_send.at[k], b_recv.at[k], (here, f))

    each(nd, lambda k: w1_out(k).start())
    for k in Z_ORDER:
        spread_back(gw2_ref, f_send, f_recv, k).wait_recv()
    hand_over(gw2_ref, 4).start()

    for k in Z_ORDER:
        row_copy(k).wait_send()
        spread(hid, h_send, h_recv, k).wait_send()
        spread(gpre, p_send, p_recv, k).wait_send()
        spread(gw2_ref, f_send, f_recv, k).wait_send()
    hand_over(hid, 2).wait_send()
    hand_over(gpre, 3).wait_send()

    def sent(k):
        grad_copy(k).wait_send()
        w2_copy(k).wait_send()
        w1_copy(k).wait_send()

    each(nd, sent)
    handed(gw2_ref, 4).wait_recv()
    hand_over(gw2_ref, 4).wait_send()

    def finished(k):
        w1_back(k).wait_recv()
        w1_out(k).wait_send()

    each(nd, finished)


def finish_kernel(
    emb_any, gw1_any, gw2_ref, out_emb, out_1s, out_1n, out_2s, out_2n, sem
):
    copies = [
        pltpu.make_async_copy(emb_any, out_emb, sem.at[0]),
        pltpu.make_async_copy(gw1_any.at[:64, :], out_1s, sem.at[1]),
        pltpu.make_async_copy(gw1_any.at[64:, :], out_1n, sem.at[2]),
    ]
    for copy in copies:
        copy.start()
    nz = gw2_ref.shape[0] // 2
    for i in range(2 * nz):
        f = 2 * (i % nz) + i // nz
        out_2s[16 * f:16 * f + 16, :] = gw2_ref[i, :16, :].astype(jnp.float32)
        out_2n[16 * f:16 * f + 16, :] = gw2_ref[i, 16:, :].astype(jnp.float32)
    for copy in copies:
        copy.wait()


def tail(nd, nf, oa, w1, w2s, w2n, out_grad, adj_two, deg_two):
    vmem = pl.BlockSpec(memory_space=pltpu.VMEM)
    anywhere = pl.BlockSpec(memory_space=pltpu.HBM)
    f32, bf16 = jnp.float32, jnp.bfloat16
    dma = pltpu.SemaphoreType.DMA
    nz = nf // 2
    emb, gw1, gw2 = pl.pallas_call(
        functools.partial(tail_kernel, nd, nf),
        out_shape=(
            jax.ShapeDtypeStruct((64, 256), bf16),
            jax.ShapeDtypeStruct((128, 256), f32),
            jax.ShapeDtypeStruct((nf, 32, 256), bf16),
        ),
        in_specs=[vmem] + [anywhere] * 6,
        out_specs=(vmem,) * 3,
        scratch_shapes=[
            pltpu.VMEM((2, nz, 128, 256), bf16),
            pltpu.VMEM((256, 256), bf16),
            pltpu.VMEM((256, 256), bf16),
            pltpu.VMEM(out_grad.shape, bf16),
            pltpu.VMEM(adj_two.shape, jnp.int32),
            pltpu.VMEM(deg_two.shape, jnp.int32),
            pltpu.VMEM((2, ROWS // 2, 128), bf16),
            pltpu.VMEM((nz, 2, ROWS // nf, 128), bf16),
            pltpu.VMEM((ROWS, 256), f32),
            pltpu.VMEM((nf, ROWS // nf, 256), bf16),
            pltpu.VMEM((nf, ROWS // nf, 256), bf16),
            pltpu.VMEM((nd, 64, 256), bf16),
            pltpu.VMEM((256, 128), bf16),
            pltpu.VMEM((nd, 16, 128), bf16),
            pltpu.VMEM((128, 256), f32),
            pltpu.VMEM((nd, 8, 128), f32),
            pltpu.VMEM((8, 128), f32),
            dma((6,)), dma((5,)), dma((5,)),
            dma((nz,)), dma((nz,)), dma((nz,)), dma((nz,)), dma((nz,)), dma((nz,)),
            dma((nd,)), dma((nd,)), dma((nd,)), dma((nd,)), dma((nd,)), dma((nd,)),
            dma((nd,)), dma((nd,)), dma((nz,)), dma((nz,)),
        ],
        compiler_params=pltpu.CompilerParams(
            collective_id=1, has_side_effects=True, vmem_limit_bytes=60 * 1024 * 1024
        ),
        name="tail",
    )(oa, w1, w2s, w2n, out_grad, adj_two, deg_two)
    return pl.pallas_call(
        finish_kernel,
        out_shape=(
            jax.ShapeDtypeStruct((64, 256), bf16),
            jax.ShapeDtypeStruct((64, 256), f32),
            jax.ShapeDtypeStruct((64, 256), f32),
            jax.ShapeDtypeStruct((256, 256), f32),
            jax.ShapeDtypeStruct((256, 256), f32),
        ),
        in_specs=[anywhere, anywhere, vmem],
        out_specs=(anywhere, anywhere, anywhere, vmem, vmem),
        scratch_shapes=[dma((3,))],
        compiler_params=pltpu.CompilerParams(vmem_limit_bytes=60 * 1024 * 1024),
        name="finish",
    )(emb, gw1, gw2)


def front_kernel(
    nd, nf, feat_any, req_any, w1s_any, w1n_any, adj_any, deg_any, self_any,
    samp_ref, w1_out, slots_ref, scale_ref,
    blocks, req_ref, w1_ref, adj_ref, deg_ref, self_ref, req_by_x, req_in, stage,
    up_send, up_recv, down_send, down_recv, req_send, req_recv,
    x_send, x_recv, w1_send, w1_recv, local_sem, fetch, sib_send, sib_recv,
):
    d = lax.axis_index("dp")
    f = lax.axis_index("feat")
    nx, ny = 4, nd // 4
    x, y = lax.rem(d, nx), lax.div(d, nx)

    def at_x(j):
        return lax.rem(x + j, nx)

    def at_y(s):
        return lax.rem(y + s + ny, ny)

    nz = nf // 2
    z, c = lax.div(f, 2), lax.rem(f, 2)
    sibling = (d, 2 * z + 1 - c)

    def along_z(k):
        to = lax.rem(z + k, nz)
        return to, (d, 2 * to + c)

    fetches = [
        pltpu.make_async_copy(feat_any.at[:, 512 * q:512 * q + 512], blocks.at[y, 64 * q:64 * q + 64, :], fetch.at[q])
        for q in range(4)
    ] + [
        pltpu.make_async_copy(req_any, req_ref, fetch.at[4]),
        pltpu.make_async_copy(w1s_any, w1_ref.at[:64, :], fetch.at[5]),
        pltpu.make_async_copy(w1n_any, w1_ref.at[64:, :], fetch.at[6]),
        pltpu.make_async_copy(adj_any, adj_ref, fetch.at[7]),
        pltpu.make_async_copy(deg_any, deg_ref, fetch.at[8]),
        pltpu.make_async_copy(self_any, self_ref, fetch.at[9]),
    ]
    for copy in fetches:
        copy.start()

    barrier = pltpu.get_barrier_semaphore()

    def greet(to):
        pl.semaphore_signal(barrier, inc=1, device_id=to, device_id_type=MESH)

    for j in range(1, nx):
        greet((y * nx + at_x(j), f))
    greet((at_y(1) * nx + x, f))
    greet((at_y(-1) * nx + x, f))
    greet(sibling)
    for k in range(1, nz):
        greet(along_z(k)[1])

    fetches[4].wait()
    for owner in range(nd):
        req_by_x[owner % nx, owner // nx:owner // nx + 1, :] = req_ref[owner:owner + 1, :]

    for copy in fetches[:4] + fetches[5:]:
        copy.wait()
    pl.semaphore_wait(barrier, nx - 1 + 2 + 1 + nz - 1)

    def req_copy(j):
        to = at_x(j)
        return pltpu.make_async_remote_copy(
            src_ref=req_by_x.at[to], dst_ref=req_in.at[x],
            send_sem=req_send.at[j], recv_sem=req_recv.at[x],
            device_id=(y * nx + to, f), device_id_type=MESH,
        )

    def half(source, h):
        return blocks.at[source, pl.ds(128 * h, 128), :]

    def up_copy(t, source):
        return pltpu.make_async_remote_copy(
            src_ref=half(source, t % 2), dst_ref=half(source, t % 2),
            send_sem=up_send.at[t], recv_sem=up_recv.at[t],
            device_id=(at_y(1) * nx + x, f), device_id_type=MESH,
        )

    def down_copy(t, source):
        return pltpu.make_async_remote_copy(
            src_ref=half(source, 1 - t % 2), dst_ref=half(source, 1 - t % 2),
            send_sem=down_send.at[t], recv_sem=down_recv.at[t],
            device_id=(at_y(-1) * nx + x, f), device_id_type=MESH,
        )

    def w1_copy(k):
        return pltpu.make_async_remote_copy(
            src_ref=w1_ref, dst_ref=w1_out.at[c, z],
            send_sem=w1_send.at[k], recv_sem=w1_recv.at[z],
            device_id=along_z(k)[1], device_id_type=MESH,
        )

    for j in range(1, nx):
        req_copy(j).start()
    for t in range(2):
        up_copy(t, y).start()
        down_copy(t, y).start()
    for k in Z_ORDER:
        w1_copy(k).start()
    own_w1 = pltpu.make_async_copy(w1_ref, w1_out.at[c, z], local_sem.at[ny])
    own_w1.start()
    req_in[x] = req_by_x[x]
    for j in range(1, nx):
        source = at_x(j)
        pltpu.make_async_remote_copy(
            src_ref=req_by_x.at[source], dst_ref=req_in.at[source],
            send_sem=req_send.at[j], recv_sem=req_recv.at[source],
            device_id=(y * nx + source, f), device_id_type=MESH,
        ).wait_recv()

    def x_copy(source, j):
        slot = source * nx + x
        return pltpu.make_async_remote_copy(
            src_ref=stage.at[source, j], dst_ref=samp_ref.at[slot],
            send_sem=x_send.at[source * nx + j], recv_sem=x_recv.at[slot],
            device_id=(y * nx + at_x(j), f), device_id_type=MESH,
        )

    def own_copy(source):
        return pltpu.make_async_copy(
            stage.at[source, 0], samp_ref.at[source * nx + x], local_sem.at[source]
        )

    node = lax.broadcasted_iota(jnp.int32, (512, 512), 0)

    def pick(source, j):
        asked = req_in[at_x(j), pl.ds(source, 1), :]
        low, quarter = asked & 511, asked >> 9
        one_hot = jnp.where(node == low, 1.0, 0.0).astype(jnp.bfloat16)
        rows = jnp.dot(blocks[source], one_hot, preferred_element_type=jnp.float32)
        chosen = rows[192:256, :]
        for q in range(3):
            chosen = jnp.where(quarter == q, rows[64 * q:64 * q + 64, :], chosen)
        stage[source, j] = chosen.astype(jnp.bfloat16)

    def process(count, source_of):
        def step(k, carry):
            source = source_of(lax.div(k, nx))
            j = lax.rem(k + 1, nx)
            pick(source, j)

            @pl.when(j > 0)
            def _():
                x_copy(source, j).start()

            @pl.when(j == 0)
            def _():
                own_copy(source).start()

            return carry

        lax.fori_loop(0, count * nx, step, 0)

    def w1_over(core):
        return pltpu.make_async_remote_copy(
            src_ref=w1_out.at[core], dst_ref=w1_out.at[core],
            send_sem=sib_send.at[0], recv_sem=sib_recv.at[0],
            device_id=sibling, device_id_type=MESH,
        )

    process(1, lambda i: y)
    fanout = adj_ref.shape[0]
    for j in range(fanout):
        slots_ref[j:j + 1, :] = jnp.where(deg_ref[...] > j, adj_ref[j], nd * 512)
    slots_ref[fanout:, :] = self_ref[...]
    scale_ref[...] = 1.0 / deg_ref[...].astype(jnp.float32)
    for s in range(ny // 2):
        below, above = at_y(-1 - s), at_y(1 + s)
        for h in range(2 if s < ny // 2 - 1 else 1):
            t = 2 * s + h
            up_copy(t, below).wait_recv()
            if t + 2 < ny - 1:
                up_copy(t + 2, below).start()
            down_copy(t, above).wait_recv()
            if t + 2 < ny - 1:
                down_copy(t + 2, above).start()
        if s == ny // 2 - 1:
            own_w1.wait()
            for k in Z_ORDER:
                source, device = along_z(k)
                pltpu.make_async_remote_copy(
                    src_ref=w1_ref, dst_ref=w1_out.at[c, source],
                    send_sem=w1_send.at[k], recv_sem=w1_recv.at[source],
                    device_id=device, device_id_type=MESH,
                ).wait_recv()
            w1_given = w1_over(c)
            w1_taken = w1_over(1 - c)
            w1_given.start()
        if s < ny // 2 - 1:
            process(2, lambda i: lax.rem(y + (2 * i - 1) * (1 + s) + ny, ny))
        else:
            process(1, lambda i: below)

    def x_back(source):
        for j in range(1, nx):
            slot = source * nx + at_x(j)
            pltpu.make_async_remote_copy(
                src_ref=stage.at[source, j], dst_ref=samp_ref.at[slot],
                send_sem=x_send.at[source * nx + j], recv_sem=x_recv.at[slot],
                device_id=(y * nx + at_x(j), f), device_id_type=MESH,
            ).wait_recv()
            x_copy(source, j).wait_send()
        own_copy(source).wait()

    lax.fori_loop(0, ny, lambda k, c: (x_back(k), c)[1], 0)

    for k in Z_ORDER:
        w1_copy(k).wait_send()
    w1_given.wait_send()
    w1_taken.wait_recv()
    for j in range(1, nx):
        req_copy(j).wait_send()
    for t in range(ny - 1):
        up_copy(t, at_y(-(t // 2))).wait_send()
        down_copy(t, at_y(t // 2)).wait_send()


def front(nd, nf, features, request_rows, w1_self, w1_neigh, adj_one, deg_one, self_slots):
    vmem = pl.BlockSpec(memory_space=pltpu.VMEM)
    anywhere = pl.BlockSpec(memory_space=pltpu.HBM)
    bf16, i32 = jnp.bfloat16, jnp.int32
    dma = pltpu.SemaphoreType.DMA
    ny = nd // 4
    return pl.pallas_call(
        functools.partial(front_kernel, nd, nf),
        out_shape=(
            jax.ShapeDtypeStruct((nd, 64, 512), bf16),
            jax.ShapeDtypeStruct((2, nf // 2, 128, 256), bf16),
            jax.ShapeDtypeStruct((adj_one.shape[0] + 1, adj_one.shape[2]), i32),
            jax.ShapeDtypeStruct(deg_one.shape, jnp.float32),
        ),
        in_specs=[anywhere] * 7,
        out_specs=(anywhere, anywhere, vmem, vmem),
        scratch_shapes=[
            pltpu.VMEM((ny, 256, 512), bf16),
            pltpu.VMEM((nd, 512), i32),
            pltpu.VMEM((128, 256), bf16),
            pltpu.VMEM(adj_one.shape, i32),
            pltpu.VMEM(deg_one.shape, i32),
            pltpu.VMEM(self_slots.shape, i32),
            pltpu.VMEM((4, ny, 512), i32),
            pltpu.VMEM((4, ny, 512), i32),
            pltpu.VMEM((ny, 4, 64, 512), bf16),
            dma((ny - 1,)), dma((ny - 1,)), dma((ny - 1,)), dma((ny - 1,)),
            dma((4,)), dma((4,)), dma((nd,)), dma((nd,)),
            dma((nf // 2,)), dma((nf // 2,)), dma((ny + 1,)), dma((10,)), dma((1,)), dma((1,)),
        ],
        compiler_params=pltpu.CompilerParams(
            collective_id=2, has_side_effects=True, vmem_limit_bytes=60 * 1024 * 1024
        ),
        name="front",
    )(features.T, request_rows, w1_self, w1_neigh, adj_one, deg_one, self_slots)


def mean_kernel(slots_ref, scale_ref, samp_any, out_ref, samp, table, own, total, sem):
    pairs, width, cap = samp.shape
    pieces = sem.shape[0]
    step = pairs // pieces
    fetches = [
        pltpu.make_async_copy(samp_any.at[pl.ds(i * step, step)], samp.at[pl.ds(i * step, step)], sem.at[i])
        for i in range(pieces)
    ]
    for copy in fetches:
        copy.start()
    table[2 * cap * pairs:, :] = jnp.zeros((8, width), jnp.float32)

    def unpack(p, carry):
        turned = samp[p].astype(jnp.float32).T
        table[pl.ds(pl.multiple_of(2 * cap * p, 8), cap), :] = turned
        table[pl.ds(pl.multiple_of(2 * cap * p + cap, 8), cap), :] = pltpu.roll(turned, 64, 1)
        return carry

    for i in range(pieces):
        fetches[i].wait()
        lax.fori_loop(i * step, (i + 1) * step, unpack, 0)
    lists, rows = slots_ref.shape

    def gather(block, carry):
        for r in range(8):
            i = block * 8 + r
            own[pl.ds(i, 1), :] = table[pl.ds(slots_ref[lists - 1, i], 1), :]
            terms = [table[pl.ds(slots_ref[j, i], 1), :] for j in range(lists - 1)]
            while len(terms) > 1:
                terms = [sum(terms[k:k + 2][1:], terms[k]) for k in range(0, len(terms), 2)]
            total[pl.ds(i, 1), :] = terms[0] * scale_ref[0, i]
        return carry

    lax.fori_loop(0, rows // 8, gather, 0)
    lane = lax.broadcasted_iota(jnp.int32, (rows, width), 1)
    mean = pltpu.roll(total[...], 64, 1)
    out_ref[:rows, :] = jnp.where(lane < 64, own[...], mean).astype(jnp.bfloat16)
    out_ref[rows:, :] = jnp.zeros((ROWS - rows, width), jnp.bfloat16)


def neighbour_mean(sampled, slots, scale):
    nd, columns, cap = sampled.shape
    rows = slots.shape[1]
    smem = pl.BlockSpec(memory_space=pltpu.SMEM)
    return pl.pallas_call(
        mean_kernel,
        out_shape=jax.ShapeDtypeStruct((ROWS, 2 * columns), jnp.bfloat16),
        in_specs=[smem, smem, pl.BlockSpec(memory_space=pltpu.HBM)],
        out_specs=pl.BlockSpec(memory_space=pltpu.VMEM),
        scratch_shapes=[
            pltpu.VMEM((nd // 2, 2 * columns, cap), jnp.bfloat16),
            pltpu.VMEM((nd * cap + 8, 2 * columns), jnp.float32),
            pltpu.VMEM((rows, 2 * columns), jnp.float32),
            pltpu.VMEM((rows, 2 * columns), jnp.float32),
            pltpu.SemaphoreType.DMA((4,)),
        ],
        compiler_params=pltpu.CompilerParams(vmem_limit_bytes=60 * 1024 * 1024),
        name="mean",
    )(slots, scale, sampled.reshape(nd // 2, 2 * columns, cap))


def local(
    nd, nf,
    features, request_rows, self_slots, adj_one, deg_one, adj_two, deg_two,
    w1_self, w1_neigh, w2_self, w2_neigh, out_grad,
):
    sampled, w1, slots, scale = front(
        nd, nf, features, request_rows[0], w1_self, w1_neigh, adj_one.transpose(2, 0, 1), deg_one, self_slots
    )
    oa = neighbour_mean(sampled, slots, scale)
    return tail(nd, nf, oa, w1, w2_self, w2_neigh, out_grad, adj_two.transpose(2, 0, 1), deg_two)


def solution(mesh):
    return jax.shard_map(
        functools.partial(local, mesh.shape["dp"], mesh.shape["feat"]),
        mesh=mesh,
        in_specs=(
            P("dp", "feat"),
            P("dp", None, None),
            P("dp", None),
            P("dp", None, None),
            P("dp", None),
            P("dp", None, None),
            P("dp", None),
            P("feat", None),
            P("feat", None),
            P(),
            P(),
            P("dp", None),
        ),
        out_specs=(P("dp", None), P("feat", None), P("feat", None), P(), P()),
        check_vma=False,
    )
```

```python
import functools

import jax
import jax.numpy as jnp
from jax import lax
from jax.experimental import pallas as pl
from jax.experimental.pallas import tpu as pltpu
from jax.sharding import PartitionSpec as P

MESH = pl.DeviceIdType.MESH
ROWS = 768


def contract_rows(a, b):
    return lax.dot_general(a, b, (((0,), (0,)), ((), ())), preferred_element_type=jnp.float32)


def contract_lanes(a, b):
    return lax.dot_general(a, b, (((1,), (1,)), ((), ())), preferred_element_type=jnp.float32)


def each(count, body):
    def step(k, carry):
        body(k)
        return carry

    lax.fori_loop(1, count, step, 0)


Z_ORDER = (4, 3, 5, 2, 6, 1, 7)


def step_kernel(
    nd, nf,
    feat_any, req_any, w1s_any, w1n_any, adj_any, deg_any, self_any,
    adj_two_any, deg_two_any, w2s_any, w2n_any, grad_any,
    emb_ref, gw1_ref, gw2_ref,
    blocks, req_ref, req_by_x, req_in, stage, samp, table, w1,
    adj_ref, deg_ref, self_ref, padded, lists, slots, scale, own, total,
    adj_two, deg_two, w2s, w2n, grad_ref,
    x_out, x_in, gh_buf, hid, gpre, grads, turned, rows_t, w2_in, part, part_in, part1, in1, sum1,
    fetch, up_send, up_recv, down_send, down_recv, req_send, req_recv, x_send, x_recv,
    pair_send, pair_recv, w1_send, w1_recv, sib_send, sib_recv, a_send, a_recv, h_send, h_recv,
    p_send, p_recv, g_send, g_recv, q_send, q_recv, r_send, r_recv, b_send, b_recv,
    f_send, f_recv, smem_sem,
):
    d = lax.axis_index("dp")
    f = lax.axis_index("feat")
    nx, ny, nz = 4, nd // 4, nf // 2
    cap = 512
    x, y = lax.rem(d, nx), lax.div(d, nx)
    z, c = lax.div(f, 2), lax.rem(f, 2)
    block, half_rows = ROWS // nf, ROWS // 2
    mine = c * nz + z
    sibling = (d, 2 * z + 1 - c)

    def at_x(j):
        return lax.rem(x + j, nx)

    def at_y(s):
        return lax.rem(y + s + ny, ny)

    def along_z(k):
        to = lax.rem(z + k, nz)
        return to, (d, 2 * to + c)

    def dp_peer(k):
        return lax.rem(d + k, nd)

    def dp_from(k):
        return lax.rem(d - k + nd, nd)

    def remote(src, dst, send_sem, recv_sem, to):
        return pltpu.make_async_remote_copy(
            src_ref=src, dst_ref=dst, send_sem=send_sem, recv_sem=recv_sem,
            device_id=to, device_id_type=MESH,
        )

    def core_rows(core, size):
        return pl.ds(pl.multiple_of(core * size, 16), size)

    sources = [
        (feat_any.at[:, 512 * q:512 * q + 512], blocks.at[y, 64 * q:64 * q + 64, :]) for q in range(4)
    ] + [
        (req_any, req_ref),
        (w1s_any, w1.at[0, z, core_rows(c, 64), :]),
        (w1n_any, w1.at[1, z, core_rows(c, 64), :]),
        (adj_any, adj_ref), (deg_any, deg_ref), (self_any, self_ref),
        (adj_two_any, adj_two), (deg_two_any, deg_two),
        (w2s_any, w2s), (w2n_any, w2n), (grad_any, grad_ref),
    ]
    fetches = [pltpu.make_async_copy(src, dst, fetch.at[i]) for i, (src, dst) in enumerate(sources)]
    for copy in fetches:
        copy.start()

    barrier = pltpu.get_barrier_semaphore()

    def greet(to):
        pl.semaphore_signal(barrier, inc=1, device_id=to, device_id_type=MESH)

    greet(sibling)
    for k in range(1, nz):
        greet(along_z(k)[1])
    each(nd, lambda k: greet((dp_peer(k), f)))
    fetches[4].wait()
    for owner in range(nd):
        req_by_x[owner % nx, owner // nx:owner // nx + 1, :] = req_ref[owner:owner + 1, :]
    for copy in fetches[:4] + fetches[5:7]:
        copy.wait()
    pl.semaphore_wait(barrier, 1 + nz - 1 + nd - 1)

    def req_copy(j):
        to = at_x(j)
        return remote(req_by_x.at[to], req_in.at[x], req_send.at[j], req_recv.at[x], (y * nx + to, f))

    def req_back(j):
        here = at_x(j)
        return remote(req_by_x.at[here], req_in.at[here], req_send.at[j], req_recv.at[here], (y * nx + here, f))

    def half(source, h):
        return blocks.at[source, pl.ds(128 * h, 128), :]

    def up_copy(t, source):
        part = half(source, t % 2)
        return remote(part, part, up_send.at[t], up_recv.at[t], (at_y(1) * nx + x, f))

    def down_copy(t, source):
        part = half(source, 1 - t % 2)
        return remote(part, part, down_send.at[t], down_recv.at[t], (at_y(-1) * nx + x, f))

    def w1_part(source):
        return w1.at[:, source, core_rows(c, 64), :]

    def w1_copy(k):
        return remote(w1_part(z), w1_part(z), w1_send.at[k], w1_recv.at[z], along_z(k)[1])

    def w1_back(k):
        source, device = along_z(k)
        return remote(w1_part(source), w1_part(source), w1_send.at[k], w1_recv.at[source], device)

    def w1_over(core):
        ours = w1.at[:, :, core_rows(core, 64), :]
        return remote(ours, ours, sib_send.at[0], sib_recv.at[0], sibling)

    for j in range(1, nx):
        req_copy(j).start()
    for t in range(2):
        up_copy(t, y).start()
        down_copy(t, y).start()
    for k in Z_ORDER:
        w1_copy(k).start()
    req_in[x] = req_by_x[x]
    for j in range(1, nx):
        req_back(j).wait_recv()

    def x_copy(source, j):
        slot = source * nx + x
        return remote(
            stage.at[source, j], samp.at[slot, core_rows(c, 64), :],
            x_send.at[source * nx + j], x_recv.at[slot], (y * nx + at_x(j), f),
        )

    def x_back(source, j):
        slot = source * nx + at_x(j)
        return remote(
            stage.at[source, j], samp.at[slot, core_rows(c, 64), :],
            x_send.at[source * nx + j], x_recv.at[slot], (y * nx + at_x(j), f),
        )

    def pair_copy(slot, core):
        ours = samp.at[slot, core_rows(core, 64), :]
        return remote(ours, ours, pair_send.at[slot], pair_recv.at[slot], sibling)

    node = lax.broadcasted_iota(jnp.int32, (512, cap), 0)

    def pick(source, j):
        asked = req_in[at_x(j), pl.ds(source, 1), :]
        low, quarter = asked & 511, asked >> 9
        one_hot = jnp.where(node == low, 1.0, 0.0).astype(jnp.bfloat16)
        rows = jnp.dot(blocks[source], one_hot, preferred_element_type=jnp.float32)
        chosen = rows[192:256, :]
        for q in range(3):
            chosen = jnp.where(quarter == q, rows[64 * q:64 * q + 64, :], chosen)
        return chosen.astype(jnp.bfloat16)

    def process(count, source_of):
        def step(k, carry):
            source = source_of(lax.div(k, nx))
            j = lax.rem(k + 1, nx)
            stage[source, j] = pick(source, j)

            @pl.when(j > 0)
            def _():
                x_copy(source, j).start()

            return carry

        lax.fori_loop(0, count * nx, step, 0)

    def collect(count, source_of):
        def step(k, carry):
            source = source_of(lax.div(k, nx))
            j = lax.rem(k, nx)

            @pl.when(j > 0)
            def _():
                x_back(source, j).wait_recv()

            @pl.when(j == 0)
            def _():
                samp[source * nx + x, core_rows(c, 64), :] = stage[source, 0]

            pair_copy(source * nx + at_x(j), c).start()
            return carry

        lax.fori_loop(0, count * nx, step, 0)

    def absorb(count, source_of):
        def step(k, carry):
            source = source_of(lax.div(k, nx))
            slot = source * nx + at_x(lax.rem(k, nx))
            pair_copy(slot, 1 - c).wait_recv()
            here = pl.ds(pl.multiple_of(slot * cap, 8), cap)
            table[here, :] = samp[slot].astype(jnp.float32).T
            return carry

        lax.fori_loop(0, count * nx, step, 0)

    process(1, lambda i: y)

    for copy in fetches[7:]:
        copy.wait()
    fanout = adj_ref.shape[0]
    present = self_ref.shape[1]
    table[nd * cap:, :] = jnp.zeros((8, 128), jnp.float32)
    padded[...] = jnp.full(padded.shape, nd * cap, jnp.int32)
    for j in range(fanout):
        padded[j:j + 1, :present] = jnp.where(deg_ref[...] > j, adj_ref[j], nd * cap)
    padded[fanout:fanout + 1, :present] = self_ref[...]
    my_lanes_half = pl.ds(pl.multiple_of(c * half_rows, 128), half_rows)
    for j in range(fanout + 1):
        line = padded[j:j + 1, my_lanes_half]
        for to in range(nz):
            at = to * (fanout + 1) + j
            lists[at:at + 1, :block] = line[:, block * to:block * to + block]
    to_smem = pltpu.make_async_copy(lists, slots, smem_sem.at[0])
    to_smem.start()
    padded[:1, :] = jnp.ones((1, ROWS), jnp.int32)
    padded[:1, :present] = deg_ref[...]
    inverse = 1.0 / padded[:1, my_lanes_half].astype(jnp.float32)
    scale[...] = jnp.broadcast_to(jnp.broadcast_to(inverse, (8, half_rows)).T[:, :1], scale.shape)

    out_grad = grad_ref[...]
    degree_row = deg_two[...]
    targets = degree_row.shape[1]
    row = lax.broadcasted_iota(jnp.int32, (ROWS, targets), 0)
    counts = jnp.zeros((ROWS, targets), jnp.float32)
    for j in range(fanout):
        listed = jnp.where(degree_row > j, adj_two[j], -1)
        counts = counts + jnp.where(row == listed, 1.0, 0.0)
    degree_row = degree_row.astype(jnp.float32)
    degree = jnp.broadcast_to(degree_row, (8, targets)).T[:, :1]
    grad_agg = contract_lanes(out_grad, w2n[...]) / degree
    gh_buf[...] = jnp.dot(
        counts, grad_agg, precision=lax.Precision.HIGHEST, preferred_element_type=jnp.float32
    )
    gh_buf[:targets, :] += contract_lanes(out_grad, w2s[...])
    counts = counts.T.astype(jnp.bfloat16)

    def around(s):
        return lambda i: lax.rem(y + (2 * i - 1) * (1 + s) + ny, ny)

    steps = ny // 2
    for s in range(steps):
        below, above = at_y(-1 - s), at_y(1 + s)
        for h in range(2 if s < steps - 1 else 1):
            t = 2 * s + h
            up_copy(t, below).wait_recv()
            if t + 2 < ny - 1:
                up_copy(t + 2, below).start()
            down_copy(t, above).wait_recv()
            if t + 2 < ny - 1:
                down_copy(t + 2, above).start()
        process(2 if s < steps - 1 else 1, around(s))
        if s == 0:
            collect(1, lambda i: y)
        else:
            collect(2, around(s - 1))
        if s == 1:
            absorb(1, lambda i: y)
        if s > 1:
            absorb(2, around(s - 2))

    g_rows = core_rows(c, 32)

    def grad_copy(k):
        return remote(grad_ref.at[g_rows, :], grads.at[d, g_rows, :], g_send.at[k], g_recv.at[k], (dp_peer(k), f))

    def grad_in(k):
        here = grads.at[dp_from(k), g_rows, :]
        return remote(here, here, g_send.at[k], g_recv.at[k], (dp_from(k), f))

    for k in Z_ORDER:
        w1_back(k).wait_recv()
    w1_over(c).start()
    absorb(2, around(steps - 2))
    collect(1, around(steps - 1))
    each(nd, lambda k: grad_copy(k).start())
    grads[d, g_rows, :] = grad_ref[g_rows, :]
    absorb(1, around(steps - 1))
    to_smem.wait()

    def row_copy(k):
        to, device = along_z(k)
        return remote(x_out.at[to], x_in.at[z], a_send.at[k], a_recv.at[z], device)

    def row_back(k):
        source, device = along_z(k)
        return remote(x_out.at[source], x_in.at[source], a_send.at[k], a_recv.at[source], device)

    def sum_rows(t, carry):
        k = lax.rem(t + nz // 2, nz)
        to = lax.rem(z + k, nz)
        base = to * (fanout + 1)

        def eight(m, inner):
            for r in range(8):
                i = m * 8 + r
                own[pl.ds(i, 1), :] = table[pl.ds(slots[base + fanout, i], 1), :]
                terms = [table[pl.ds(slots[base + j, i], 1), :] for j in range(fanout)]
                while len(terms) > 1:
                    terms = [sum(terms[n:n + 2][1:], terms[n]) for n in range(0, len(terms), 2)]
                total[pl.ds(i, 1), :] = terms[0]
            return inner

        lax.fori_loop(0, block // 8, eight, 0)
        x_out[to, 0] = own[...].astype(jnp.bfloat16)
        mean = total[...] * scale[pl.ds(pl.multiple_of(to * block, 8), block), :]
        x_out[to, 1] = mean.astype(jnp.bfloat16)

        @pl.when(k > 0)
        def _():
            row_copy(k).start()

        return carry

    lax.fori_loop(0, nz, sum_rows, 0)
    x_in[z] = x_out[z]
    for kind in range(2):
        rows_t[128 * kind:128 * kind + 128, :] = (
            x_out[:, kind].reshape(half_rows, 128).astype(jnp.float32).T.astype(jnp.bfloat16)
        )
    w1_over(1 - c).wait_recv()

    pre = jnp.zeros((block, w1.shape[-1]), jnp.float32)
    for k in (0,) + tuple(reversed(Z_ORDER)):
        if k > 0:
            row_back(k).wait_recv()
        source = lax.rem(z + k, nz)
        for kind in range(2):
            pre = pre + jnp.dot(x_in[source, kind], w1[kind, source], preferred_element_type=jnp.float32)
    sig = 1.0 / (1.0 + jnp.exp(-pre))
    my_gh = gh_buf[pl.ds(pl.multiple_of(mine * block, 8), block), :]
    hid[mine] = (pre * sig).astype(jnp.bfloat16)
    gpre[z] = (my_gh * (sig * (1.0 + pre * (1.0 - sig)))).astype(jnp.bfloat16)

    def spread(buf, send_sem, recv_sem, k):
        return remote(buf.at[mine], buf.at[mine], send_sem.at[k], recv_sem.at[z], along_z(k)[1])

    def spread_back(buf, send_sem, recv_sem, k):
        source, device = along_z(k)
        slot = buf.at[c * nz + source]
        return remote(slot, slot, send_sem.at[k], recv_sem.at[source], device)

    def hand_over(buf, core, i):
        ours = buf.at[pl.ds(core * nz, nz)]
        return remote(ours, ours, sib_send.at[i], sib_recv.at[i], sibling)

    def gpre_copy(k):
        return remote(gpre.at[z], gpre.at[z], p_send.at[k], p_recv.at[z], along_z(k)[1])

    def gpre_back(k):
        source, device = along_z(k)
        return remote(gpre.at[source], gpre.at[source], p_send.at[k], p_recv.at[source], device)

    for k in Z_ORDER:
        spread(hid, h_send, h_recv, k).start()
    for k in Z_ORDER:
        gpre_copy(k).start()
    for k in Z_ORDER:
        spread_back(hid, h_send, h_recv, k).wait_recv()
    hand_over(hid, c, 1).start()
    hand_over(hid, 1 - c, 1).wait_recv()

    hidden = hid[...].reshape(ROWS, hid.shape[-1])
    self_hidden = hidden[:targets, :]
    agg_two = jnp.dot(counts, hidden, preferred_element_type=jnp.float32) / degree
    agg_two = agg_two.astype(jnp.bfloat16)
    pair = jnp.concatenate([self_hidden, agg_two], axis=0)
    turned[...] = pair.astype(jnp.float32).T.astype(jnp.bfloat16)
    columns = core_rows(f, 16)

    def w2_copy(k):
        return remote(turned.at[columns, :], w2_in.at[d], q_send.at[k], q_recv.at[k], (dp_peer(k), f))

    def w2_back(k):
        here = w2_in.at[dp_from(k)]
        return remote(here, here, q_send.at[k], q_recv.at[k], (dp_from(k), f))

    each(nd, lambda k: w2_copy(k).start())
    w2_in[d] = turned[columns, :]

    for k in Z_ORDER:
        gpre_back(k).wait_recv()
    sums = jnp.dot(
        rows_t[...], gpre[...].reshape(half_rows, gpre.shape[-1]), preferred_element_type=jnp.float32
    )
    part[...] = sums.reshape(part.shape)

    def part_copy(core):
        return remote(part.at[:, core], part_in, sib_send.at[2], sib_recv.at[2], sibling)

    part_copy(1 - c).start()
    part_copy(c).wait_recv()
    part1[...] = (part[:, c] + part_in[...]).reshape(part1.shape)

    def tile_of(index):
        return (
            pl.ds(pl.multiple_of(lax.div(index, 2) * 8, 8), 8),
            pl.ds(pl.multiple_of(lax.rem(index, 2) * 128, 128), 128),
        )

    my_rows, my_lanes = tile_of(d)

    def w1_sum_copy(k):
        to = dp_peer(k)
        rows, lanes = tile_of(to)
        return remote(part1.at[rows, lanes], in1.at[d], r_send.at[k], r_recv.at[k], (to, f))

    def w1_sum_back(k):
        here = in1.at[dp_from(k)]
        return remote(here, here, r_send.at[k], r_recv.at[k], (dp_from(k), f))

    each(nd, lambda k: w1_sum_copy(k).start())
    in1[d] = part1[my_rows, my_lanes]

    each(nd, lambda k: grad_in(k).wait_recv())

    def grads_over(core):
        ours = grads.at[:, core_rows(core, 32), :]
        return remote(ours, ours, sib_send.at[3], sib_recv.at[3], sibling)

    grads_over(c).start()
    emb = jnp.dot(self_hidden, w2s[...], preferred_element_type=jnp.float32)
    emb = emb + jnp.dot(agg_two, w2n[...], preferred_element_type=jnp.float32)
    emb_ref[...] = emb.astype(jnp.bfloat16)
    grads_over(1 - c).wait_recv()
    each(nd, lambda k: w2_back(k).wait_recv())
    lane = lax.broadcasted_iota(jnp.int32, (16, 128), 1)
    total2 = jnp.zeros((32, out_grad.shape[-1]), jnp.float32)
    for p in range(nd // 2):
        first, second = w2_in[2 * p].astype(jnp.float32), w2_in[2 * p + 1].astype(jnp.float32)
        selfs = jnp.where(lane < 64, first, pltpu.roll(second, 64, 1))
        neighs = jnp.where(lane < 64, pltpu.roll(first, 64, 1), second)
        left = jnp.concatenate([selfs, neighs], axis=0).astype(jnp.bfloat16)
        right = grads[2 * p:2 * p + 2].reshape(128, out_grad.shape[-1])
        total2 = total2 + jnp.dot(left, right, preferred_element_type=jnp.float32)
    gw2_ref[mine] = total2.astype(jnp.bfloat16)
    for k in Z_ORDER:
        spread(gw2_ref, f_send, f_recv, k).start()

    each(nd, lambda k: w1_sum_back(k).wait_recv())
    sum1[...] = jnp.sum(in1[...], axis=0)
    gw1_ref[my_rows, my_lanes] = sum1[...]

    def w1_out(k):
        return remote(sum1, gw1_ref.at[my_rows, my_lanes], b_send.at[k], b_recv.at[k], (dp_peer(k), f))

    def w1_done(k):
        rows, lanes = tile_of(dp_from(k))
        return remote(sum1, gw1_ref.at[rows, lanes], b_send.at[k], b_recv.at[k], (dp_from(k), f))

    each(nd, lambda k: w1_out(k).start())
    for k in Z_ORDER:
        spread_back(gw2_ref, f_send, f_recv, k).wait_recv()
    hand_over(gw2_ref, c, 4).start()

    for j in range(1, nx):
        req_copy(j).wait_send()
    for t in range(ny - 1):
        up_copy(t, at_y(-(t // 2))).wait_send()
        down_copy(t, at_y(t // 2)).wait_send()
    for k in Z_ORDER:
        w1_copy(k).wait_send()
        row_copy(k).wait_send()
        spread(hid, h_send, h_recv, k).wait_send()
        gpre_copy(k).wait_send()
        spread(gw2_ref, f_send, f_recv, k).wait_send()
    w1_over(c).wait_send()
    hand_over(hid, c, 1).wait_send()
    part_copy(1 - c).wait_send()
    grads_over(c).wait_send()

    def picked_sent(source, carry):
        for j in range(nx):
            if j > 0:
                x_copy(source, j).wait_send()
            pair_copy(source * nx + at_x(j), c).wait_send()
        return carry

    lax.fori_loop(0, ny, picked_sent, 0)

    def sent(k):
        grad_copy(k).wait_send()
        w2_copy(k).wait_send()
        w1_sum_copy(k).wait_send()

    each(nd, sent)
    hand_over(gw2_ref, 1 - c, 4).wait_recv()
    hand_over(gw2_ref, c, 4).wait_send()

    def finished(k):
        w1_done(k).wait_recv()
        w1_out(k).wait_send()

    each(nd, finished)


def finish_kernel(emb_ref, gw1_ref, gw2_ref, out_emb, out_1s, out_1n, out_2s, out_2n):
    out_emb[...] = emb_ref[...]
    out_1s[...] = gw1_ref[:64, :]
    out_1n[...] = gw1_ref[64:, :]
    nz = gw2_ref.shape[0] // 2
    for i in range(2 * nz):
        f = 2 * (i % nz) + i // nz
        out_2s[16 * f:16 * f + 16, :] = gw2_ref[i, :16, :].astype(jnp.float32)
        out_2n[16 * f:16 * f + 16, :] = gw2_ref[i, 16:, :].astype(jnp.float32)


def local(
    nd, nf,
    features, request_rows, self_slots, adj_one, deg_one, adj_two, deg_two,
    w1_self, w1_neigh, w2_self, w2_neigh, out_grad,
):
    vmem = pl.BlockSpec(memory_space=pltpu.VMEM)
    anywhere = pl.BlockSpec(memory_space=pltpu.HBM)
    f32, bf16, i32 = jnp.float32, jnp.bfloat16, jnp.int32
    dma = pltpu.SemaphoreType.DMA
    nx, ny, nz = 4, nd // 4, nf // 2
    block, half = ROWS // nf, ROWS // 2
    adj_one = adj_one.transpose(2, 0, 1)
    adj_two = adj_two.transpose(2, 0, 1)
    lists = nz * (adj_one.shape[0] + 1)
    emb, gw1, gw2 = pl.pallas_call(
        functools.partial(step_kernel, nd, nf),
        out_shape=(
            jax.ShapeDtypeStruct((64, 256), bf16),
            jax.ShapeDtypeStruct((128, 256), f32),
            jax.ShapeDtypeStruct((nf, 32, 256), bf16),
        ),
        in_specs=[anywhere] * 12,
        out_specs=(vmem,) * 3,
        scratch_shapes=[
            pltpu.VMEM((ny, 256, 512), bf16),
            pltpu.VMEM((nd, 512), i32),
            pltpu.VMEM((nx, ny, 512), i32),
            pltpu.VMEM((nx, ny, 512), i32),
            pltpu.VMEM((ny, nx, 64, 512), bf16),
            pltpu.VMEM((nd, 128, 512), bf16),
            pltpu.VMEM((nd * 512 + 8, 128), f32),
            pltpu.VMEM((2, nz, 128, 256), bf16),
            pltpu.VMEM(adj_one.shape, i32),
            pltpu.VMEM(deg_one.shape, i32),
            pltpu.VMEM(self_slots.shape, i32),
            pltpu.VMEM((16, ROWS), i32),
            pltpu.VMEM((lists, 128), i32),
            pltpu.SMEM((lists, 128), i32),
            pltpu.VMEM((half, 128), f32),
            pltpu.VMEM((block, 128), f32),
            pltpu.VMEM((block, 128), f32),
            pltpu.VMEM(adj_two.shape, i32),
            pltpu.VMEM(deg_two.shape, i32),
            pltpu.VMEM((256, 256), bf16),
            pltpu.VMEM((256, 256), bf16),
            pltpu.VMEM(out_grad.shape, bf16),
            pltpu.VMEM((nz, 2, block, 128), bf16),
            pltpu.VMEM((nz, 2, block, 128), bf16),
            pltpu.VMEM((ROWS, 256), f32),
            pltpu.VMEM((nf, block, 256), bf16),
            pltpu.VMEM((nz, block, 256), bf16),
            pltpu.VMEM((nd, 64, 256), bf16),
            pltpu.VMEM((256, 128), bf16),
            pltpu.VMEM((256, half), bf16),
            pltpu.VMEM((nd, 16, 128), bf16),
            pltpu.VMEM((2, 2, 64, 256), f32),
            pltpu.VMEM((2, 64, 256), f32),
            pltpu.VMEM((128, 256), f32),
            pltpu.VMEM((nd, 8, 128), f32),
            pltpu.VMEM((8, 128), f32),
            dma((15,)),
            dma((ny - 1,)), dma((ny - 1,)), dma((ny - 1,)), dma((ny - 1,)),
            dma((nx,)), dma((nx,)), dma((nd,)), dma((nd,)), dma((nd,)), dma((nd,)),
            dma((nz,)), dma((nz,)), dma((5,)), dma((5,)),
            dma((nz,)), dma((nz,)), dma((nz,)), dma((nz,)), dma((nz,)), dma((nz,)),
            dma((nd,)), dma((nd,)), dma((nd,)), dma((nd,)),
            dma((nd,)), dma((nd,)), dma((nd,)), dma((nd,)),
            dma((nz,)), dma((nz,)), dma((1,)),
        ],
        compiler_params=pltpu.CompilerParams(
            collective_id=1, has_side_effects=True, vmem_limit_bytes=60 * 1024 * 1024
        ),
        name="train_step",
    )(
        features.T, request_rows[0], w1_self, w1_neigh, adj_one, deg_one, self_slots,
        adj_two, deg_two, w2_self, w2_neigh, out_grad,
    )
    return pl.pallas_call(
        finish_kernel,
        out_shape=(
            jax.ShapeDtypeStruct((64, 256), bf16),
            jax.ShapeDtypeStruct((64, 256), f32),
            jax.ShapeDtypeStruct((64, 256), f32),
            jax.ShapeDtypeStruct((256, 256), f32),
            jax.ShapeDtypeStruct((256, 256), f32),
        ),
        in_specs=[vmem] * 3,
        out_specs=(vmem,) * 5,
        compiler_params=pltpu.CompilerParams(vmem_limit_bytes=60 * 1024 * 1024),
        name="finish",
    )(emb, gw1, gw2)


def solution(mesh):
    return jax.shard_map(
        functools.partial(local, mesh.shape["dp"], mesh.shape["feat"]),
        mesh=mesh,
        in_specs=(
            P("dp", "feat"),
            P("dp", None, None),
            P("dp", None),
            P("dp", None, None),
            P("dp", None),
            P("dp", None, None),
            P("dp", None),
            P("feat", None),
            P("feat", None),
            P(),
            P(),
            P("dp", None),
        ),
        out_specs=(P("dp", None), P("feat", None), P("feat", None), P(), P()),
        check_vma=False,
    )
```

```python
import functools

import jax
import jax.numpy as jnp
from jax import lax
from jax.experimental import pallas as pl
from jax.experimental.pallas import tpu as pltpu
from jax.sharding import PartitionSpec as P

MESH = pl.DeviceIdType.MESH
ROWS = 768


def contract_rows(a, b):
    return lax.dot_general(a, b, (((0,), (0,)), ((), ())), preferred_element_type=jnp.float32)


def contract_lanes(a, b):
    return lax.dot_general(a, b, (((1,), (1,)), ((), ())), preferred_element_type=jnp.float32)


def each(count, body):
    def step(k, carry):
        body(k)
        return carry

    lax.fori_loop(1, count, step, 0)


Z_ORDER = (4, 3, 5, 2, 6, 1, 7)


def step_kernel(
    nd, nf,
    feat_any, req_any, w1s_any, w1n_any, adj_any, deg_any, self_any,
    adj_two_any, deg_two_any, w2s_any, w2n_any, grad_any,
    emb_ref, gw1_ref, gw2_ref,
    blocks, req_ref, req_by_x, req_in, stage, samp, table, w1,
    adj_ref, deg_ref, self_ref, padded, lists, slots, scale, own, total,
    adj_two, deg_two, w2s, w2n, grad_ref,
    x_out, x_in, gh_buf, hid, gpre, grads, turned, rows_t, w2_in, part, part_in, part1, in1, sum1,
    fetch, up_send, up_recv, down_send, down_recv, req_send, req_recv, x_send, x_recv,
    pair_send, pair_recv, w1_send, w1_recv, sib_send, sib_recv, a_send, a_recv, h_send, h_recv,
    p_send, p_recv, g_send, g_recv, q_send, q_recv, r_send, r_recv, b_send, b_recv,
    f_send, f_recv, smem_sem,
):
    d = lax.axis_index("dp")
    f = lax.axis_index("feat")
    nx, ny, nz = 4, nd // 4, nf // 2
    cap = 512
    x, y = lax.rem(d, nx), lax.div(d, nx)
    z, c = lax.div(f, 2), lax.rem(f, 2)
    block, half_rows = ROWS // nf, ROWS // 2
    mine = c * nz + z
    sibling = (d, 2 * z + 1 - c)

    def at_x(j):
        return lax.rem(x + j, nx)

    def at_y(s):
        return lax.rem(y + s + ny, ny)

    def along_z(k):
        to = lax.rem(z + k, nz)
        return to, (d, 2 * to + c)

    def dp_peer(k):
        return lax.rem(d + k, nd)

    def dp_from(k):
        return lax.rem(d - k + nd, nd)

    def remote(src, dst, send_sem, recv_sem, to):
        return pltpu.make_async_remote_copy(
            src_ref=src, dst_ref=dst, send_sem=send_sem, recv_sem=recv_sem,
            device_id=to, device_id_type=MESH,
        )

    def core_rows(core, size):
        return pl.ds(pl.multiple_of(core * size, 16), size)

    barrier = pltpu.get_barrier_semaphore()

    def greet(to):
        pl.semaphore_signal(barrier, inc=1, device_id=to, device_id_type=MESH)

    sources = [
        (feat_any.at[:, 512 * q:512 * q + 512], blocks.at[y, 64 * q:64 * q + 64, :]) for q in range(4)
    ] + [
        (req_any, req_ref),
        (w1s_any, w1.at[z, 0, core_rows(c, 64), :]),
        (w1n_any, w1.at[z, 1, core_rows(c, 64), :]),
        (adj_any, adj_ref), (deg_any, deg_ref), (self_any, self_ref),
        (adj_two_any, adj_two), (deg_two_any, deg_two),
        (w2s_any, w2s), (w2n_any, w2n), (grad_any, grad_ref),
    ]
    fetches = [pltpu.make_async_copy(src, dst, fetch.at[i]) for i, (src, dst) in enumerate(sources)]
    for copy in [fetches[4]] + fetches[:4] + fetches[5:7]:
        copy.start()

    greet(sibling)
    for k in range(1, nz):
        greet(along_z(k)[1])
    each(nd, lambda k: greet((dp_peer(k), f)))
    pl.semaphore_wait(barrier, 1 + nz - 1 + nd - 1)

    def req_copy(j):
        to = at_x(j)
        return remote(req_by_x.at[to], req_in.at[x], req_send.at[j], req_recv.at[x], (y * nx + to, f))

    def req_back(j):
        here = at_x(j)
        return remote(req_by_x.at[here], req_in.at[here], req_send.at[j], req_recv.at[here], (y * nx + here, f))

    def half(source, h):
        return blocks.at[source, pl.ds(128 * h, 128), :]

    def up_copy(t, source):
        part = half(source, t % 2)
        return remote(part, part, up_send.at[t], up_recv.at[t], (at_y(1) * nx + x, f))

    def down_copy(t, source):
        part = half(source, 1 - t % 2)
        return remote(part, part, down_send.at[t], down_recv.at[t], (at_y(-1) * nx + x, f))

    def w1_part(source):
        return w1.at[source, :, core_rows(c, 64), :]

    def w1_copy(k):
        return remote(w1_part(z), w1_part(z), w1_send.at[k], w1_recv.at[z], along_z(k)[1])

    def w1_back(k):
        source, device = along_z(k)
        return remote(w1_part(source), w1_part(source), w1_send.at[k], w1_recv.at[source], device)

    def w1_over(core):
        ours = w1.at[:, :, core_rows(core, 64), :]
        return remote(ours, ours, sib_send.at[0], sib_recv.at[0], sibling)

    def first_copies(t):
        copies = []
        for up, h in ((True, t % 2), (False, 1 - t % 2)):
            for q in (2 * h, 2 * h + 1):
                copies.append(remote(
                    feat_any.at[:, 512 * q:512 * q + 512], blocks.at[y, 64 * q:64 * q + 64, :],
                    (up_send if up else down_send).at[t], (up_recv if up else down_recv).at[t],
                    (at_y(1 if up else -1) * nx + x, f),
                ))
        return copies

    for t in range(2):
        for copy in first_copies(t):
            copy.start()
    for copy in fetches[7:]:
        copy.start()
    fetches[4].wait()
    for owner in range(nd):
        req_by_x[owner % nx, owner // nx:owner // nx + 1, :] = req_ref[owner:owner + 1, :]
    for j in range(1, nx):
        req_copy(j).start()
    for copy in fetches[:4] + fetches[5:7]:
        copy.wait()
    req_in[x] = req_by_x[x]
    for j in range(1, nx):
        req_back(j).wait_recv()

    def x_copy(source, j):
        slot = source * nx + x
        return remote(
            stage.at[source, j], samp.at[slot, core_rows(c, 64), :],
            x_send.at[source * nx + j], x_recv.at[slot], (y * nx + at_x(j), f),
        )

    def x_back(source, j):
        slot = source * nx + at_x(j)
        return remote(
            stage.at[source, j], samp.at[slot, core_rows(c, 64), :],
            x_send.at[source * nx + j], x_recv.at[slot], (y * nx + at_x(j), f),
        )

    def pair_copy(slot, core):
        ours = samp.at[slot, core_rows(core, 64), :]
        return remote(ours, ours, pair_send.at[slot], pair_recv.at[slot], sibling)

    node = lax.broadcasted_iota(jnp.int32, (512, cap), 0)

    def pick(source, j):
        asked = req_in[at_x(j), pl.ds(source, 1), :]
        low, quarter = asked & 511, asked >> 9
        one_hot = jnp.where(node == low, 1.0, 0.0).astype(jnp.bfloat16)
        rows = jnp.dot(blocks[source], one_hot, preferred_element_type=jnp.float32)
        chosen = rows[192:256, :]
        for q in range(3):
            chosen = jnp.where(quarter == q, rows[64 * q:64 * q + 64, :], chosen)
        return chosen.astype(jnp.bfloat16)

    def process(count, source_of):
        def step(k, carry):
            source = source_of(lax.div(k, nx))
            j = lax.rem(k + 2, nx)
            stage[source, j] = pick(source, j)

            @pl.when(j > 0)
            def _():
                x_copy(source, j).start()

            return carry

        lax.fori_loop(0, count * nx, step, 0)

    def collect(count, source_of):
        def step(k, carry):
            source = source_of(lax.div(k, nx))
            j = lax.rem(k, nx)

            @pl.when(j > 0)
            def _():
                x_back(source, j).wait_recv()

            @pl.when(j == 0)
            def _():
                samp[source * nx + x, core_rows(c, 64), :] = stage[source, 0]

            pair_copy(source * nx + at_x(j), c).start()
            return carry

        lax.fori_loop(0, count * nx, step, 0)

    def absorb(count, source_of):
        def step(k, carry):
            source = source_of(lax.div(k, nx))
            slot = source * nx + at_x(lax.rem(k, nx))
            pair_copy(slot, 1 - c).wait_recv()
            here = pl.ds(pl.multiple_of(slot * cap, 8), cap)
            table[here, :] = samp[slot].astype(jnp.float32).T
            return carry

        lax.fori_loop(0, count * nx, step, 0)

    process(1, lambda i: y)

    for k in Z_ORDER:
        w1_copy(k).start()
    for copy in fetches[7:]:
        copy.wait()
    fanout = adj_ref.shape[0]
    present = self_ref.shape[1]
    table[nd * cap:, :] = jnp.zeros((8, 128), jnp.float32)
    padded[...] = jnp.full(padded.shape, nd * cap, jnp.int32)
    for j in range(fanout):
        padded[j:j + 1, :present] = jnp.where(deg_ref[...] > j, adj_ref[j], nd * cap)
    padded[fanout:fanout + 1, :present] = self_ref[...]
    my_lanes_half = pl.ds(pl.multiple_of(c * half_rows, 128), half_rows)
    for j in range(fanout + 1):
        line = padded[j:j + 1, my_lanes_half]
        for to in range(nz):
            at = to * (fanout + 1) + j
            lists[at:at + 1, :block] = line[:, block * to:block * to + block]
    to_smem = pltpu.make_async_copy(lists, slots, smem_sem.at[0])
    to_smem.start()
    padded[:1, :] = jnp.ones((1, ROWS), jnp.int32)
    padded[:1, :present] = deg_ref[...]
    inverse = 1.0 / padded[:1, my_lanes_half].astype(jnp.float32)
    scale[...] = jnp.broadcast_to(jnp.broadcast_to(inverse, (8, half_rows)).T[:, :1], scale.shape)

    out_grad = grad_ref[...]
    degree_row = deg_two[...]
    targets = degree_row.shape[1]
    row = lax.broadcasted_iota(jnp.int32, (ROWS, targets), 0)
    counts = jnp.zeros((ROWS, targets), jnp.float32)
    for j in range(fanout):
        listed = jnp.where(degree_row > j, adj_two[j], -1)
        counts = counts + jnp.where(row == listed, 1.0, 0.0)
    degree_row = degree_row.astype(jnp.float32)
    degree = jnp.broadcast_to(degree_row, (8, targets)).T[:, :1]
    grad_agg = contract_lanes(out_grad, w2n[...]) / degree
    gh_buf[...] = jnp.dot(
        counts, grad_agg, precision=lax.Precision.HIGHEST, preferred_element_type=jnp.float32
    )
    gh_buf[:targets, :] += contract_lanes(out_grad, w2s[...])
    counts = counts.T.astype(jnp.bfloat16)

    def around(s):
        return lambda i: lax.rem(y + (2 * i - 1) * (1 + s) + ny, ny)

    def one(offset):
        return lambda i: at_y(offset)

    steps = ny // 2
    for t in range(ny - 1):
        s = t // 2
        below, above = at_y(-1 - s), at_y(1 + s)
        up_copy(t, below).wait_recv()
        if t + 2 < ny - 1:
            up_copy(t + 2, below).start()
        down_copy(t, above).wait_recv()
        if t + 2 < ny - 1:
            down_copy(t + 2, above).start()
        if t % 2 == 1:
            process(2, around(s))
            if s == 1:
                collect(1, one(0))
            if s == 2:
                collect(2, around(0))
                absorb(1, one(0))
        elif t == ny - 2:
            process(1, one(1 + s))
    absorb(2, around(0))
    collect(2, around(1))

    g_rows = core_rows(c, 32)

    def grad_copy(k):
        return remote(grad_ref.at[g_rows, :], grads.at[d, g_rows, :], g_send.at[k], g_recv.at[k], (dp_peer(k), f))

    def grad_in(k):
        here = grads.at[dp_from(k), g_rows, :]
        return remote(here, here, g_send.at[k], g_recv.at[k], (dp_from(k), f))

    absorb(2, around(steps - 3))
    collect(2, around(steps - 2))
    absorb(2, around(steps - 2))
    collect(1, around(steps - 1))
    absorb(1, around(steps - 1))
    to_smem.wait()
    for k in Z_ORDER:
        w1_back(k).wait_recv()
    w1_over(c).start()

    def row_copy(k):
        to, device = along_z(k)
        return remote(x_out.at[to], x_in.at[z], a_send.at[k], a_recv.at[z], device)

    def row_back(k):
        source, device = along_z(k)
        return remote(x_out.at[source], x_in.at[source], a_send.at[k], a_recv.at[source], device)

    def sum_rows(t, carry):
        odd = lax.rem(t, 2)
        k = nz // 2 + lax.div(t, 2) * (1 - odd) - lax.div(t + 1, 2) * odd
        to = lax.rem(z + k, nz)
        base = to * (fanout + 1)
        for i in range(block):
            own[i:i + 1, :] = table[pl.ds(slots[base + fanout, i], 1), :]
            terms = [table[pl.ds(slots[base + j, i], 1), :] for j in range(fanout)]
            while len(terms) > 1:
                terms = [sum(terms[n:n + 2][1:], terms[n]) for n in range(0, len(terms), 2)]
            total[i:i + 1, :] = terms[0]
        x_out[to, :, :128] = own[...].astype(jnp.bfloat16)
        mean = total[...] * scale[pl.ds(pl.multiple_of(to * block, 8), block), :]
        x_out[to, :, 128:] = mean.astype(jnp.bfloat16)

        @pl.when(k > 0)
        def _():
            row_copy(k).start()

        return carry

    lax.fori_loop(0, nz, sum_rows, 0)
    each(nd, lambda k: grad_copy(k).start())
    grads[d, g_rows, :] = grad_ref[g_rows, :]
    x_in[z] = x_out[z]
    rows_t[...] = x_out[...].reshape(half_rows, 256).astype(jnp.float32).T.astype(jnp.bfloat16)
    w1_over(1 - c).wait_recv()

    pre = jnp.zeros((block, w1.shape[-1]), jnp.float32)
    for k in (0, 5, 4, 6, 3, 7, 2, 1):
        if k > 0:
            row_back(k).wait_recv()
        source = lax.rem(z + k, nz)
        pre = pre + jnp.dot(
            x_in[source], w1[source].reshape(256, w1.shape[-1]), preferred_element_type=jnp.float32
        )
    sig = 1.0 / (1.0 + jnp.exp(-pre))
    my_gh = gh_buf[pl.ds(pl.multiple_of(mine * block, 8), block), :]
    hid[mine] = (pre * sig).astype(jnp.bfloat16)
    gpre[z] = (my_gh * (sig * (1.0 + pre * (1.0 - sig)))).astype(jnp.bfloat16)

    def spread(buf, send_sem, recv_sem, k):
        return remote(buf.at[mine], buf.at[mine], send_sem.at[k], recv_sem.at[z], along_z(k)[1])

    def spread_back(buf, send_sem, recv_sem, k):
        source, device = along_z(k)
        slot = buf.at[c * nz + source]
        return remote(slot, slot, send_sem.at[k], recv_sem.at[source], device)

    def hand_over(buf, core, i):
        ours = buf.at[pl.ds(core * nz, nz)]
        return remote(ours, ours, sib_send.at[i], sib_recv.at[i], sibling)

    def gpre_copy(k):
        return remote(gpre.at[z], gpre.at[z], p_send.at[k], p_recv.at[z], along_z(k)[1])

    def gpre_back(k):
        source, device = along_z(k)
        return remote(gpre.at[source], gpre.at[source], p_send.at[k], p_recv.at[source], device)

    for k in Z_ORDER:
        spread(hid, h_send, h_recv, k).start()
    for k in Z_ORDER:
        gpre_copy(k).start()
    for k in Z_ORDER:
        spread_back(hid, h_send, h_recv, k).wait_recv()
    hand_over(hid, c, 1).start()
    for k in Z_ORDER:
        gpre_back(k).wait_recv()
    sums = jnp.dot(
        rows_t[...], gpre[...].reshape(half_rows, gpre.shape[-1]), preferred_element_type=jnp.float32
    )
    part[...] = sums.reshape(part.shape)

    def part_copy(core):
        return remote(part.at[:, core], part_in, sib_send.at[2], sib_recv.at[2], sibling)

    part_copy(1 - c).start()
    hand_over(hid, 1 - c, 1).wait_recv()

    hidden = hid[...].reshape(ROWS, hid.shape[-1])
    self_hidden = hidden[:targets, :]
    agg_two = jnp.dot(counts, hidden, preferred_element_type=jnp.float32) / degree
    agg_two = agg_two.astype(jnp.bfloat16)
    pair = jnp.concatenate([self_hidden, agg_two], axis=0)
    turned[...] = pair.astype(jnp.float32).T.astype(jnp.bfloat16)
    columns = core_rows(f, 16)

    def w2_copy(k):
        return remote(turned.at[columns, :], w2_in.at[d], q_send.at[k], q_recv.at[k], (dp_peer(k), f))

    def w2_back(k):
        here = w2_in.at[dp_from(k)]
        return remote(here, here, q_send.at[k], q_recv.at[k], (dp_from(k), f))

    each(nd, lambda k: w2_copy(k).start())
    w2_in[d] = turned[columns, :]

    part_copy(c).wait_recv()
    part1[...] = (part[:, c] + part_in[...]).reshape(part1.shape)

    def tile_of(index):
        return (
            pl.ds(pl.multiple_of(lax.div(index, 2) * 8, 8), 8),
            pl.ds(pl.multiple_of(lax.rem(index, 2) * 128, 128), 128),
        )

    my_rows, my_lanes = tile_of(d)

    def w1_sum_copy(k):
        to = dp_peer(k)
        rows, lanes = tile_of(to)
        return remote(part1.at[rows, lanes], in1.at[d], r_send.at[k], r_recv.at[k], (to, f))

    def w1_sum_back(k):
        here = in1.at[dp_from(k)]
        return remote(here, here, r_send.at[k], r_recv.at[k], (dp_from(k), f))

    each(nd, lambda k: w1_sum_copy(k).start())
    in1[d] = part1[my_rows, my_lanes]

    each(nd, lambda k: grad_in(k).wait_recv())

    def grads_over(core):
        ours = grads.at[:, core_rows(core, 32), :]
        return remote(ours, ours, sib_send.at[3], sib_recv.at[3], sibling)

    grads_over(c).start()
    emb = jnp.dot(self_hidden, w2s[...], preferred_element_type=jnp.float32)
    emb = emb + jnp.dot(agg_two, w2n[...], preferred_element_type=jnp.float32)
    emb_ref[...] = emb.astype(jnp.bfloat16)
    grads_over(1 - c).wait_recv()
    each(nd, lambda k: w2_back(k).wait_recv())
    lane = lax.broadcasted_iota(jnp.int32, (16, 128), 1)
    total2 = jnp.zeros((32, out_grad.shape[-1]), jnp.float32)
    for p in range(nd // 2):
        first, second = w2_in[2 * p].astype(jnp.float32), w2_in[2 * p + 1].astype(jnp.float32)
        selfs = jnp.where(lane < 64, first, pltpu.roll(second, 64, 1))
        neighs = jnp.where(lane < 64, pltpu.roll(first, 64, 1), second)
        left = jnp.concatenate([selfs, neighs], axis=0).astype(jnp.bfloat16)
        right = grads[2 * p:2 * p + 2].reshape(128, out_grad.shape[-1])
        total2 = total2 + jnp.dot(left, right, preferred_element_type=jnp.float32)
    gw2_ref[mine] = total2.astype(jnp.bfloat16)
    for k in Z_ORDER:
        spread(gw2_ref, f_send, f_recv, k).start()

    each(nd, lambda k: w1_sum_back(k).wait_recv())
    sum1[...] = jnp.sum(in1[...], axis=0)
    gw1_ref[my_rows, my_lanes] = sum1[...]

    def w1_out(k):
        return remote(sum1, gw1_ref.at[my_rows, my_lanes], b_send.at[k], b_recv.at[k], (dp_peer(k), f))

    def w1_done(k):
        rows, lanes = tile_of(dp_from(k))
        return remote(sum1, gw1_ref.at[rows, lanes], b_send.at[k], b_recv.at[k], (dp_from(k), f))

    each(nd, lambda k: w1_out(k).start())
    for k in Z_ORDER:
        spread_back(gw2_ref, f_send, f_recv, k).wait_recv()
    hand_over(gw2_ref, c, 4).start()

    for j in range(1, nx):
        req_copy(j).wait_send()
    for t in range(ny - 1):
        up_copy(t, at_y(-(t // 2))).wait_send()
        down_copy(t, at_y(t // 2)).wait_send()
    for k in Z_ORDER:
        w1_copy(k).wait_send()
        row_copy(k).wait_send()
        spread(hid, h_send, h_recv, k).wait_send()
        gpre_copy(k).wait_send()
        spread(gw2_ref, f_send, f_recv, k).wait_send()
    w1_over(c).wait_send()
    hand_over(hid, c, 1).wait_send()
    part_copy(1 - c).wait_send()
    grads_over(c).wait_send()

    def picked_sent(source, carry):
        for j in range(nx):
            if j > 0:
                x_copy(source, j).wait_send()
            pair_copy(source * nx + at_x(j), c).wait_send()
        return carry

    lax.fori_loop(0, ny, picked_sent, 0)

    def sent(k):
        grad_copy(k).wait_send()
        w2_copy(k).wait_send()
        w1_sum_copy(k).wait_send()

    each(nd, sent)
    hand_over(gw2_ref, 1 - c, 4).wait_recv()
    hand_over(gw2_ref, c, 4).wait_send()

    def finished(k):
        w1_done(k).wait_recv()
        w1_out(k).wait_send()

    each(nd, finished)


def finish_kernel(emb_ref, gw1_ref, gw2_ref, out_emb, out_1s, out_1n, out_2s, out_2n):
    out_emb[...] = emb_ref[...]
    out_1s[...] = gw1_ref[:64, :]
    out_1n[...] = gw1_ref[64:, :]
    nz = gw2_ref.shape[0] // 2
    for i in range(2 * nz):
        f = 2 * (i % nz) + i // nz
        out_2s[16 * f:16 * f + 16, :] = gw2_ref[i, :16, :].astype(jnp.float32)
        out_2n[16 * f:16 * f + 16, :] = gw2_ref[i, 16:, :].astype(jnp.float32)


def local(
    nd, nf,
    features, request_rows, self_slots, adj_one, deg_one, adj_two, deg_two,
    w1_self, w1_neigh, w2_self, w2_neigh, out_grad,
):
    vmem = pl.BlockSpec(memory_space=pltpu.VMEM)
    anywhere = pl.BlockSpec(memory_space=pltpu.HBM)
    f32, bf16, i32 = jnp.float32, jnp.bfloat16, jnp.int32
    dma = pltpu.SemaphoreType.DMA
    nx, ny, nz = 4, nd // 4, nf // 2
    block, half = ROWS // nf, ROWS // 2
    adj_one = adj_one.transpose(2, 0, 1)
    adj_two = adj_two.transpose(2, 0, 1)
    lists = nz * (adj_one.shape[0] + 1)
    emb, gw1, gw2 = pl.pallas_call(
        functools.partial(step_kernel, nd, nf),
        out_shape=(
            jax.ShapeDtypeStruct((64, 256), bf16),
            jax.ShapeDtypeStruct((128, 256), f32),
            jax.ShapeDtypeStruct((nf, 32, 256), bf16),
        ),
        in_specs=[anywhere] * 12,
        out_specs=(vmem,) * 3,
        scratch_shapes=[
            pltpu.VMEM((ny, 256, 512), bf16),
            pltpu.VMEM((nd, 512), i32),
            pltpu.VMEM((nx, ny, 512), i32),
            pltpu.VMEM((nx, ny, 512), i32),
            pltpu.VMEM((ny, nx, 64, 512), bf16),
            pltpu.VMEM((nd, 128, 512), bf16),
            pltpu.VMEM((nd * 512 + 8, 128), f32),
            pltpu.VMEM((nz, 2, 128, 256), bf16),
            pltpu.VMEM(adj_one.shape, i32),
            pltpu.VMEM(deg_one.shape, i32),
            pltpu.VMEM(self_slots.shape, i32),
            pltpu.VMEM((16, ROWS), i32),
            pltpu.VMEM((lists, 128), i32),
            pltpu.SMEM((lists, 128), i32),
            pltpu.VMEM((half, 128), f32),
            pltpu.VMEM((block, 128), f32),
            pltpu.VMEM((block, 128), f32),
            pltpu.VMEM(adj_two.shape, i32),
            pltpu.VMEM(deg_two.shape, i32),
            pltpu.VMEM((256, 256), bf16),
            pltpu.VMEM((256, 256), bf16),
            pltpu.VMEM(out_grad.shape, bf16),
            pltpu.VMEM((nz, block, 256), bf16),
            pltpu.VMEM((nz, block, 256), bf16),
            pltpu.VMEM((ROWS, 256), f32),
            pltpu.VMEM((nf, block, 256), bf16),
            pltpu.VMEM((nz, block, 256), bf16),
            pltpu.VMEM((nd, 64, 256), bf16),
            pltpu.VMEM((256, 128), bf16),
            pltpu.VMEM((256, half), bf16),
            pltpu.VMEM((nd, 16, 128), bf16),
            pltpu.VMEM((2, 2, 64, 256), f32),
            pltpu.VMEM((2, 64, 256), f32),
            pltpu.VMEM((128, 256), f32),
            pltpu.VMEM((nd, 8, 128), f32),
            pltpu.VMEM((8, 128), f32),
            dma((15,)),
            dma((ny - 1,)), dma((ny - 1,)), dma((ny - 1,)), dma((ny - 1,)),
            dma((nx,)), dma((nx,)), dma((nd,)), dma((nd,)), dma((nd,)), dma((nd,)),
            dma((nz,)), dma((nz,)), dma((5,)), dma((5,)),
            dma((nz,)), dma((nz,)), dma((nz,)), dma((nz,)), dma((nz,)), dma((nz,)),
            dma((nd,)), dma((nd,)), dma((nd,)), dma((nd,)),
            dma((nd,)), dma((nd,)), dma((nd,)), dma((nd,)),
            dma((nz,)), dma((nz,)), dma((1,)),
        ],
        compiler_params=pltpu.CompilerParams(
            collective_id=1, has_side_effects=True, vmem_limit_bytes=60 * 1024 * 1024
        ),
        name="train_step",
    )(
        features.T, request_rows[0], w1_self, w1_neigh, adj_one, deg_one, self_slots,
        adj_two, deg_two, w2_self, w2_neigh, out_grad,
    )
    return pl.pallas_call(
        finish_kernel,
        out_shape=(
            jax.ShapeDtypeStruct((64, 256), bf16),
            jax.ShapeDtypeStruct((64, 256), f32),
            jax.ShapeDtypeStruct((64, 256), f32),
            jax.ShapeDtypeStruct((256, 256), f32),
            jax.ShapeDtypeStruct((256, 256), f32),
        ),
        in_specs=[vmem] * 3,
        out_specs=(vmem,) * 5,
        compiler_params=pltpu.CompilerParams(vmem_limit_bytes=60 * 1024 * 1024),
        name="finish",
    )(emb, gw1, gw2)


def solution(mesh):
    return jax.shard_map(
        functools.partial(local, mesh.shape["dp"], mesh.shape["feat"]),
        mesh=mesh,
        in_specs=(
            P("dp", "feat"),
            P("dp", None, None),
            P("dp", None),
            P("dp", None, None),
            P("dp", None),
            P("dp", None, None),
            P("dp", None),
            P("feat", None),
            P("feat", None),
            P(),
            P(),
            P("dp", None),
        ),
        out_specs=(P("dp", None), P("feat", None), P("feat", None), P(), P()),
        check_vma=False,
    )
```

```python
import functools

import jax
import jax.numpy as jnp
from jax import lax
from jax.experimental import pallas as pl
from jax.experimental.pallas import tpu as pltpu
from jax.sharding import PartitionSpec as P

MESH = pl.DeviceIdType.MESH
ROWS = 768


def contract_rows(a, b):
    return lax.dot_general(a, b, (((0,), (0,)), ((), ())), preferred_element_type=jnp.float32)


def contract_lanes(a, b):
    return lax.dot_general(a, b, (((1,), (1,)), ((), ())), preferred_element_type=jnp.float32)


def each(count, body):
    def step(k, carry):
        body(k)
        return carry

    lax.fori_loop(1, count, step, 0)


Z_ORDER = (4, 3, 5, 2, 6, 1, 7)


def step_kernel(
    nd, nf,
    feat_any, req_any, w1s_any, w1n_any, adj_any, deg_any, self_any,
    adj_two_any, deg_two_any, w2s_any, w2n_any, grad_any,
    emb_ref, gw1_ref, gw2_ref,
    blocks, req_ref, req_by_x, req_in, stage, samp, table, w1,
    adj_ref, deg_ref, self_ref, padded, lists, slots, scale, own, total,
    adj_two, deg_two, w2s, w2n, grad_ref,
    x_out, x_in, gh_buf, hid, gpre, grads, turned, rows_t, w2_in, part, part_in, part1, in1, sum1,
    fetch, up_send, up_recv, down_send, down_recv, req_send, req_recv, x_send, x_recv,
    pair_send, pair_recv, w1_send, w1_recv, sib_send, sib_recv, a_send, a_recv, h_send, h_recv,
    p_send, p_recv, g_send, g_recv, q_send, q_recv, r_send, r_recv, b_send, b_recv,
    f_send, f_recv, smem_sem,
):
    d = lax.axis_index("dp")
    f = lax.axis_index("feat")
    nx, ny, nz = 4, nd // 4, nf // 2
    cap = 512
    x, y = lax.rem(d, nx), lax.div(d, nx)
    z, c = lax.div(f, 2), lax.rem(f, 2)
    block, half_rows = ROWS // nf, ROWS // 2
    mine = c * nz + z
    sibling = (d, 2 * z + 1 - c)

    def at_x(j):
        return lax.rem(x + j, nx)

    def at_y(s):
        return lax.rem(y + s + ny, ny)

    def along_z(k):
        to = lax.rem(z + k, nz)
        return to, (d, 2 * to + c)

    def dp_peer(k):
        return lax.rem(d + k, nd)

    def dp_from(k):
        return lax.rem(d - k + nd, nd)

    def remote(src, dst, send_sem, recv_sem, to):
        return pltpu.make_async_remote_copy(
            src_ref=src, dst_ref=dst, send_sem=send_sem, recv_sem=recv_sem,
            device_id=to, device_id_type=MESH,
        )

    def all_in(ref, sem):
        remote(ref, ref, sem, sem, sibling).wait_recv()

    def all_out(ref, sem):
        remote(ref, ref, sem, sem, sibling).wait_send()

    def core_rows(core, size):
        return pl.ds(pl.multiple_of(core * size, 16), size)

    barrier = pltpu.get_barrier_semaphore()

    def greet(to):
        pl.semaphore_signal(barrier, inc=1, device_id=to, device_id_type=MESH)

    sources = [
        (feat_any.at[:, 512 * q:512 * q + 512], blocks.at[y, 64 * q:64 * q + 64, :]) for q in range(4)
    ] + [
        (req_any, req_ref),
        (w1s_any, w1.at[z, 0, core_rows(c, 64), :]),
        (w1n_any, w1.at[z, 1, core_rows(c, 64), :]),
        (adj_any, adj_ref), (deg_any, deg_ref), (self_any, self_ref),
        (adj_two_any, adj_two), (deg_two_any, deg_two),
        (w2s_any, w2s), (w2n_any, w2n), (grad_any, grad_ref),
    ]
    kinds = (0, 0, 0, 0, 1, 2, 2, 3, 4, 5, 6, 7, 8, 9, 10)
    fetches = [pltpu.make_async_copy(src, dst, fetch.at[i]) for i, (src, dst) in zip(kinds, sources)]
    for copy in [fetches[4]] + fetches[:4] + fetches[5:7]:
        copy.start()

    greet(sibling)
    for k in range(1, nz):
        greet(along_z(k)[1])
    each(nd, lambda k: greet((dp_peer(k), f)))
    pl.semaphore_wait(barrier, 1 + nz - 1 + nd - 1)

    def req_copy(j):
        to = at_x(j)
        return remote(req_by_x.at[to], req_in.at[x], req_send.at[0], req_recv.at[0], (y * nx + to, f))

    def half(source, h):
        return blocks.at[source, core_rows(h, 128), :]

    def up_copy(t, source):
        part = half(source, lax.rem(t, 2))
        return remote(part, part, up_send.at[0], up_recv.at[t], (at_y(1) * nx + x, f))

    def down_copy(t, source):
        part = half(source, 1 - lax.rem(t, 2))
        return remote(part, part, down_send.at[0], down_recv.at[t], (at_y(-1) * nx + x, f))

    def w1_part(source):
        return w1.at[source, :, core_rows(c, 64), :]

    def w1_copy(k):
        return remote(w1_part(z), w1_part(z), w1_send.at[0], w1_recv.at[0], along_z(k)[1])

    def w1_over(core):
        ours = w1.at[:, :, core_rows(core, 64), :]
        return remote(ours, ours, sib_send.at[0], sib_recv.at[0], sibling)

    def first_copies(t):
        copies = []
        for up, h in ((True, t % 2), (False, 1 - t % 2)):
            for q in (2 * h, 2 * h + 1):
                copies.append(remote(
                    feat_any.at[:, 512 * q:512 * q + 512], blocks.at[y, 64 * q:64 * q + 64, :],
                    (up_send if up else down_send).at[0], (up_recv if up else down_recv).at[t],
                    (at_y(1 if up else -1) * nx + x, f),
                ))
        return copies

    for t in range(2):
        for copy in first_copies(t):
            copy.start()
    for copy in fetches[7:]:
        copy.start()
    fetches[4].wait()
    for owner in range(nd):
        req_by_x[owner % nx, owner // nx:owner // nx + 1, :] = req_ref[owner:owner + 1, :]
    for j in range(1, nx):
        req_copy(j).start()
    pltpu.make_async_copy(blocks.at[y], blocks.at[y], fetch.at[0]).wait()
    pltpu.make_async_copy(w1.at[z, :, core_rows(c, 64), :], w1.at[z, :, core_rows(c, 64), :], fetch.at[2]).wait()
    req_in[x] = req_by_x[x]
    all_in(req_in.at[pl.ds(0, nx - 1)], req_recv.at[0])

    def x_copy(source, j):
        slot = source * nx + x
        return remote(
            stage.at[source, j], samp.at[slot, core_rows(c, 64), :],
            x_send.at[0], x_recv.at[source], (y * nx + at_x(j), f),
        )

    def slots_of(source, count, core):
        return samp.at[pl.ds(source * nx, count), core_rows(core, 64), :]

    def pair_copy(source, core):
        ours = slots_of(source, nx, core)
        return remote(ours, ours, pair_send.at[0], pair_recv.at[source], sibling)

    node = lax.broadcasted_iota(jnp.int32, (512, cap), 0)

    def pick(source, j):
        asked = req_in[at_x(j), pl.ds(source, 1), :]
        low, quarter = asked & 511, asked >> 9
        one_hot = jnp.where(node == low, 1.0, 0.0).astype(jnp.bfloat16)
        rows = jnp.dot(blocks[source], one_hot, preferred_element_type=jnp.float32)
        chosen = rows[192:256, :]
        for q in range(3):
            chosen = jnp.where(quarter == q, rows[64 * q:64 * q + 64, :], chosen)
        return chosen.astype(jnp.bfloat16)

    def process(count, source_of):
        def step(k, carry):
            source = source_of(lax.div(k, nx))
            j = lax.rem(k + 2, nx)
            stage[source, j] = pick(source, j)

            @pl.when(j > 0)
            def _():
                x_copy(source, j).start()

            return carry

        lax.fori_loop(0, count * nx, step, 0)

    def collect(count, source_of):
        def step(u, carry):
            source = source_of(u)
            all_in(slots_of(source, nx - 1, c), x_recv.at[source])
            samp[source * nx + x, core_rows(c, 64), :] = stage[source, 0]
            pair_copy(source, c).start()
            return carry

        lax.fori_loop(0, count, step, 0)

    def absorb(count, source_of):
        def step(u, carry):
            source = source_of(u)
            pair_copy(source, 1 - c).wait_recv()
            for j in range(nx):
                slot = source * nx + j
                here = pl.ds(pl.multiple_of(slot * cap, 8), cap)
                table[here, :] = samp[slot].astype(jnp.float32).T
            return carry

        lax.fori_loop(0, count, step, 0)

    for k in Z_ORDER:
        w1_copy(k).start()
    steps = ny // 2

    def in_step(i):
        return 2 - lax.div(steps - i, steps) - lax.div(i, steps)

    def source_in(i):
        return lambda u: lax.rem(y + (2 * u - 1) * i + ny, ny)

    def pass_on(t, i):
        below, above = at_y(-i), at_y(i)
        more = t + 2 < ny - 1
        up_copy(t, below).wait_recv()

        @pl.when(more)
        def _():
            up_copy(t + 2, below).start()

        down_copy(t, above).wait_recv()

        @pl.when(more)
        def _():
            down_copy(t + 2, above).start()

    def gather_late(i):
        @pl.when(i >= 3)
        def _():
            absorb(in_step(i - 3), source_in(i - 3))

        @pl.when((i >= 2) & (i <= steps + 2))
        def _():
            collect(in_step(i - 2), source_in(i - 2))

    def ring_step(i, carry):
        @pl.when(i > 0)
        def _():
            pass_on(2 * i - 2, i)

        @pl.when((i > 0) & (i < steps))
        def _():
            pass_on(2 * i - 1, i)

        process(in_step(i), source_in(i))
        gather_late(i)
        return carry

    lax.fori_loop(0, steps + 1, ring_step, 0)

    for copy in fetches[7:]:
        copy.wait()
    fanout = adj_ref.shape[0]
    present = self_ref.shape[1]
    table[nd * cap:, :] = jnp.zeros((8, 128), jnp.float32)
    padded[...] = jnp.full(padded.shape, nd * cap, jnp.int32)
    for j in range(fanout):
        padded[j:j + 1, :present] = jnp.where(deg_ref[...] > j, adj_ref[j], nd * cap)
    padded[fanout:fanout + 1, :present] = self_ref[...]
    my_lanes_half = pl.ds(pl.multiple_of(c * half_rows, 128), half_rows)
    for j in range(fanout + 1):
        line = padded[j:j + 1, my_lanes_half]
        for to in range(nz):
            at = to * (fanout + 1) + j
            lists[at:at + 1, :block] = line[:, block * to:block * to + block]
    to_smem = pltpu.make_async_copy(lists, slots, smem_sem.at[0])
    to_smem.start()
    padded[:1, :] = jnp.ones((1, ROWS), jnp.int32)
    padded[:1, :present] = deg_ref[...]
    inverse = 1.0 / padded[:1, my_lanes_half].astype(jnp.float32)
    scale[...] = jnp.broadcast_to(jnp.broadcast_to(inverse, (8, half_rows)).T[:, :1], scale.shape)

    out_grad = grad_ref[...]
    degree_row = deg_two[...]
    targets = degree_row.shape[1]
    row = lax.broadcasted_iota(jnp.int32, (ROWS, targets), 0)
    counts = jnp.zeros((ROWS, targets), jnp.float32)
    for j in range(fanout):
        listed = jnp.where(degree_row > j, adj_two[j], -1)
        counts = counts + jnp.where(row == listed, 1.0, 0.0)
    degree_row = degree_row.astype(jnp.float32)
    degree = jnp.broadcast_to(degree_row, (8, targets)).T[:, :1]
    grad_agg = contract_lanes(out_grad, w2n[...]) / degree
    high = grad_agg.astype(jnp.bfloat16)
    low = (grad_agg - high.astype(jnp.float32)).astype(jnp.bfloat16)
    both = jnp.concatenate([counts, counts], axis=1).astype(jnp.bfloat16)
    gh_buf[...] = jnp.dot(both, jnp.concatenate([high, low], axis=0), preferred_element_type=jnp.float32)
    gh_buf[:targets, :] += contract_lanes(out_grad, w2s[...])
    counts = counts.T.astype(jnp.bfloat16)

    lax.fori_loop(steps + 1, steps + 4, lambda i, carry: (gather_late(i), carry)[1], 0)

    g_rows = core_rows(c, 32)

    def grad_copy(k):
        return remote(grad_ref.at[g_rows, :], grads.at[d, g_rows, :], g_send.at[0], g_recv.at[0], (dp_peer(k), f))

    some_grads = grads.at[pl.ds(0, nd - 1), pl.ds(0, 32), :]

    to_smem.wait()
    all_in(w1.at[pl.ds(0, nz - 1), :, pl.ds(0, 64), :], w1_recv.at[0])
    w1_over(c).start()

    def row_copy(k):
        to, device = along_z(k)
        return remote(x_out.at[to], x_in.at[z], a_send.at[0], a_recv.at[z], device)

    def row_back(k):
        source, device = along_z(k)
        return remote(x_out.at[source], x_in.at[source], a_send.at[0], a_recv.at[source], device)

    def sum_rows(t, carry):
        odd = lax.rem(t, 2)
        k = nz // 2 + lax.div(t, 2) * (1 - odd) - lax.div(t + 1, 2) * odd
        to = lax.rem(z + k, nz)
        base = to * (fanout + 1)
        for i in range(block):
            own[i:i + 1, :] = table[pl.ds(slots[base + fanout, i], 1), :]
            terms = [table[pl.ds(slots[base + j, i], 1), :] for j in range(fanout)]
            while len(terms) > 1:
                terms = [sum(terms[n:n + 2][1:], terms[n]) for n in range(0, len(terms), 2)]
            total[i:i + 1, :] = terms[0]
        x_out[to, :, :128] = own[...].astype(jnp.bfloat16)
        mean = total[...] * scale[pl.ds(pl.multiple_of(to * block, 8), block), :]
        x_out[to, :, 128:] = mean.astype(jnp.bfloat16)

        @pl.when(k > 0)
        def _():
            row_copy(k).start()

        return carry

    lax.fori_loop(0, nz, sum_rows, 0)
    each(nd, lambda k: grad_copy(k).start())
    grads[d, g_rows, :] = grad_ref[g_rows, :]
    x_in[z] = x_out[z]
    rows_t[...] = x_out[...].reshape(half_rows, 256).astype(jnp.float32).T.astype(jnp.bfloat16)
    w1_over(1 - c).wait_recv()

    pre = jnp.zeros((block, w1.shape[-1]), jnp.float32)
    for k in (0, 5, 4, 6, 3, 7, 2, 1):
        if k > 0:
            row_back(k).wait_recv()
        source = lax.rem(z + k, nz)
        pre = pre + jnp.dot(
            x_in[source], w1[source].reshape(256, w1.shape[-1]), preferred_element_type=jnp.float32
        )
    sig = 1.0 / (1.0 + jnp.exp(-pre))
    my_gh = gh_buf[pl.ds(pl.multiple_of(mine * block, 8), block), :]
    hid[mine] = (pre * sig).astype(jnp.bfloat16)
    gpre[z] = (my_gh * (sig * (1.0 + pre * (1.0 - sig)))).astype(jnp.bfloat16)

    def spread(buf, send_sem, recv_sem, k):
        return remote(buf.at[mine], buf.at[mine], send_sem.at[0], recv_sem.at[0], along_z(k)[1])

    def most(buf):
        return buf.at[pl.ds(0, nz - 1)]

    def hand_over(buf, core, i):
        ours = buf.at[pl.ds(core * nz, nz)]
        return remote(ours, ours, sib_send.at[i], sib_recv.at[i], sibling)

    def gpre_copy(k):
        return remote(gpre.at[z], gpre.at[z], p_send.at[0], p_recv.at[0], along_z(k)[1])

    for k in Z_ORDER:
        spread(hid, h_send, h_recv, k).start()
    for k in Z_ORDER:
        gpre_copy(k).start()
    all_in(most(hid), h_recv.at[0])
    hand_over(hid, c, 1).start()
    all_in(most(gpre), p_recv.at[0])
    sums = jnp.dot(
        rows_t[...], gpre[...].reshape(half_rows, gpre.shape[-1]), preferred_element_type=jnp.float32
    )
    part[...] = sums.reshape(part.shape)

    def part_copy(core):
        return remote(part.at[:, core], part_in, sib_send.at[2], sib_recv.at[2], sibling)

    part_copy(1 - c).start()
    hand_over(hid, 1 - c, 1).wait_recv()

    hidden = hid[...].reshape(ROWS, hid.shape[-1])
    self_hidden = hidden[:targets, :]
    agg_two = jnp.dot(counts, hidden, preferred_element_type=jnp.float32) / degree
    agg_two = agg_two.astype(jnp.bfloat16)
    pair = jnp.concatenate([self_hidden, agg_two], axis=0)
    turned[...] = pair.astype(jnp.float32).T.astype(jnp.bfloat16)
    columns = core_rows(f, 16)

    def w2_copy(k):
        return remote(turned.at[columns, :], w2_in.at[d], q_send.at[0], q_recv.at[0], (dp_peer(k), f))

    each(nd, lambda k: w2_copy(k).start())
    w2_in[d] = turned[columns, :]

    part_copy(c).wait_recv()
    part1[...] = (part[:, c] + part_in[...]).reshape(part1.shape)

    def tile_of(index):
        return (
            pl.ds(pl.multiple_of(lax.div(index, 2) * 8, 8), 8),
            pl.ds(pl.multiple_of(lax.rem(index, 2) * 128, 128), 128),
        )

    my_rows, my_lanes = tile_of(d)

    def w1_sum_copy(k):
        to = dp_peer(k)
        rows, lanes = tile_of(to)
        return remote(part1.at[rows, lanes], in1.at[d], r_send.at[0], r_recv.at[0], (to, f))

    some_tiles = in1.at[pl.ds(0, nd - 1)]
    each(nd, lambda k: w1_sum_copy(k).start())
    in1[d] = part1[my_rows, my_lanes]

    all_in(some_grads, g_recv.at[0])

    def grads_over(core):
        ours = grads.at[:, core_rows(core, 32), :]
        return remote(ours, ours, sib_send.at[3], sib_recv.at[3], sibling)

    grads_over(c).start()
    emb = jnp.dot(self_hidden, w2s[...], preferred_element_type=jnp.float32)
    emb = emb + jnp.dot(agg_two, w2n[...], preferred_element_type=jnp.float32)
    emb_ref[...] = emb.astype(jnp.bfloat16)
    grads_over(1 - c).wait_recv()
    all_in(w2_in.at[pl.ds(0, nd - 1)], q_recv.at[0])
    lane = lax.broadcasted_iota(jnp.int32, (16, 128), 1)
    total2 = jnp.zeros((32, out_grad.shape[-1]), jnp.float32)
    for p in range(nd // 2):
        first, second = w2_in[2 * p].astype(jnp.float32), w2_in[2 * p + 1].astype(jnp.float32)
        selfs = jnp.where(lane < 64, first, pltpu.roll(second, 64, 1))
        neighs = jnp.where(lane < 64, pltpu.roll(first, 64, 1), second)
        left = jnp.concatenate([selfs, neighs], axis=0).astype(jnp.bfloat16)
        right = grads[2 * p:2 * p + 2].reshape(128, out_grad.shape[-1])
        total2 = total2 + jnp.dot(left, right, preferred_element_type=jnp.float32)
    gw2_ref[mine] = total2.astype(jnp.bfloat16)
    for k in Z_ORDER:
        spread(gw2_ref, f_send, f_recv, k).start()

    all_in(some_tiles, r_recv.at[0])
    sum1[...] = jnp.sum(in1[...], axis=0)
    gw1_ref[my_rows, my_lanes] = sum1[...]

    def w1_out(k):
        return remote(sum1, gw1_ref.at[my_rows, my_lanes], b_send.at[0], b_recv.at[0], (dp_peer(k), f))

    each(nd, lambda k: w1_out(k).start())
    all_in(most(gw2_ref), f_recv.at[0])
    hand_over(gw2_ref, c, 4).start()

    all_out(req_in.at[pl.ds(0, nx - 1)], req_send.at[0])
    all_out(blocks.at[pl.ds(0, ny - 1), pl.ds(0, 128), :], up_send.at[0])
    all_out(blocks.at[pl.ds(0, ny - 1), pl.ds(0, 128), :], down_send.at[0])
    all_out(w1.at[pl.ds(0, nz - 1), :, pl.ds(0, 64), :], w1_send.at[0])
    all_out(most(x_out), a_send.at[0])
    all_out(most(hid), h_send.at[0])
    all_out(most(gpre), p_send.at[0])
    all_out(most(gw2_ref), f_send.at[0])
    w1_over(c).wait_send()
    hand_over(hid, c, 1).wait_send()
    part_copy(1 - c).wait_send()
    grads_over(c).wait_send()
    all_out(stage.at[:, pl.ds(0, nx - 1)], x_send.at[0])
    all_out(samp.at[:, core_rows(c, 64), :], pair_send.at[0])
    all_out(some_grads, g_send.at[0])
    all_out(w2_in.at[pl.ds(0, nd - 1)], q_send.at[0])
    all_out(some_tiles, r_send.at[0])
    hand_over(gw2_ref, 1 - c, 4).wait_recv()
    hand_over(gw2_ref, c, 4).wait_send()
    all_in(some_tiles, b_recv.at[0])
    all_out(some_tiles, b_send.at[0])


def finish_kernel(emb_ref, gw1_ref, gw2_ref, out_emb, out_1s, out_1n, out_2s, out_2n):
    out_emb[...] = emb_ref[...]
    out_1s[...] = gw1_ref[:64, :]
    out_1n[...] = gw1_ref[64:, :]
    nz = gw2_ref.shape[0] // 2
    for i in range(2 * nz):
        f = 2 * (i % nz) + i // nz
        out_2s[16 * f:16 * f + 16, :] = gw2_ref[i, :16, :].astype(jnp.float32)
        out_2n[16 * f:16 * f + 16, :] = gw2_ref[i, 16:, :].astype(jnp.float32)


def local(
    nd, nf,
    features, request_rows, self_slots, adj_one, deg_one, adj_two, deg_two,
    w1_self, w1_neigh, w2_self, w2_neigh, out_grad,
):
    vmem = pl.BlockSpec(memory_space=pltpu.VMEM)
    anywhere = pl.BlockSpec(memory_space=pltpu.HBM)
    f32, bf16, i32 = jnp.float32, jnp.bfloat16, jnp.int32
    dma = pltpu.SemaphoreType.DMA
    nx, ny, nz = 4, nd // 4, nf // 2
    block, half = ROWS // nf, ROWS // 2
    adj_one = adj_one.transpose(2, 0, 1)
    adj_two = adj_two.transpose(2, 0, 1)
    lists = nz * (adj_one.shape[0] + 1)
    emb, gw1, gw2 = pl.pallas_call(
        functools.partial(step_kernel, nd, nf),
        out_shape=(
            jax.ShapeDtypeStruct((64, 256), bf16),
            jax.ShapeDtypeStruct((128, 256), f32),
            jax.ShapeDtypeStruct((nf, 32, 256), bf16),
        ),
        in_specs=[anywhere] * 12,
        out_specs=(vmem,) * 3,
        scratch_shapes=[
            pltpu.VMEM((ny, 256, 512), bf16),
            pltpu.VMEM((nd, 512), i32),
            pltpu.VMEM((nx, ny, 512), i32),
            pltpu.VMEM((nx, ny, 512), i32),
            pltpu.VMEM((ny, nx, 64, 512), bf16),
            pltpu.VMEM((nd, 128, 512), bf16),
            pltpu.VMEM((nd * 512 + 8, 128), f32),
            pltpu.VMEM((nz, 2, 128, 256), bf16),
            pltpu.VMEM(adj_one.shape, i32),
            pltpu.VMEM(deg_one.shape, i32),
            pltpu.VMEM(self_slots.shape, i32),
            pltpu.VMEM((16, ROWS), i32),
            pltpu.VMEM((lists, 128), i32),
            pltpu.SMEM((lists, 128), i32),
            pltpu.VMEM((half, 128), f32),
            pltpu.VMEM((block, 128), f32),
            pltpu.VMEM((block, 128), f32),
            pltpu.VMEM(adj_two.shape, i32),
            pltpu.VMEM(deg_two.shape, i32),
            pltpu.VMEM((256, 256), bf16),
            pltpu.VMEM((256, 256), bf16),
            pltpu.VMEM(out_grad.shape, bf16),
            pltpu.VMEM((nz, block, 256), bf16),
            pltpu.VMEM((nz, block, 256), bf16),
            pltpu.VMEM((ROWS, 256), f32),
            pltpu.VMEM((nf, block, 256), bf16),
            pltpu.VMEM((nz, block, 256), bf16),
            pltpu.VMEM((nd, 64, 256), bf16),
            pltpu.VMEM((256, 128), bf16),
            pltpu.VMEM((256, half), bf16),
            pltpu.VMEM((nd, 16, 128), bf16),
            pltpu.VMEM((2, 2, 64, 256), f32),
            pltpu.VMEM((2, 64, 256), f32),
            pltpu.VMEM((128, 256), f32),
            pltpu.VMEM((nd, 8, 128), f32),
            pltpu.VMEM((8, 128), f32),
            dma((11,)),
            dma((1,)), dma((ny - 1,)), dma((1,)), dma((ny - 1,)),
            dma((1,)), dma((1,)), dma((1,)), dma((ny,)), dma((1,)), dma((ny,)),
            dma((1,)), dma((1,)), dma((5,)), dma((5,)),
            dma((1,)), dma((nz,)), dma((1,)), dma((1,)), dma((1,)), dma((1,)),
            dma((1,)), dma((1,)), dma((1,)), dma((1,)),
            dma((1,)), dma((1,)), dma((1,)), dma((1,)),
            dma((1,)), dma((1,)), dma((1,)),
        ],
        compiler_params=pltpu.CompilerParams(
            collective_id=1, has_side_effects=True, vmem_limit_bytes=60 * 1024 * 1024
        ),
        name="train_step",
    )(
        features.T, request_rows[0], w1_self, w1_neigh, adj_one, deg_one, self_slots,
        adj_two, deg_two, w2_self, w2_neigh, out_grad,
    )
    return pl.pallas_call(
        finish_kernel,
        out_shape=(
            jax.ShapeDtypeStruct((64, 256), bf16),
            jax.ShapeDtypeStruct((64, 256), f32),
            jax.ShapeDtypeStruct((64, 256), f32),
            jax.ShapeDtypeStruct((256, 256), f32),
            jax.ShapeDtypeStruct((256, 256), f32),
        ),
        in_specs=[vmem] * 3,
        out_specs=(vmem,) * 5,
        compiler_params=pltpu.CompilerParams(vmem_limit_bytes=60 * 1024 * 1024),
        name="finish",
    )(emb, gw1, gw2)


def solution(mesh):
    return jax.shard_map(
        functools.partial(local, mesh.shape["dp"], mesh.shape["feat"]),
        mesh=mesh,
        in_specs=(
            P("dp", "feat"),
            P("dp", None, None),
            P("dp", None),
            P("dp", None, None),
            P("dp", None),
            P("dp", None, None),
            P("dp", None),
            P("feat", None),
            P("feat", None),
            P(),
            P(),
            P("dp", None),
        ),
        out_specs=(P("dp", None), P("feat", None), P("feat", None), P(), P()),
        check_vma=False,
    )
```

```python
import functools

import jax
import jax.numpy as jnp
from jax import lax
from jax.experimental import pallas as pl
from jax.experimental.pallas import tpu as pltpu
from jax.sharding import PartitionSpec as P

MESH = pl.DeviceIdType.MESH
ROWS = 768


def contract_rows(a, b):
    return lax.dot_general(a, b, (((0,), (0,)), ((), ())), preferred_element_type=jnp.float32)


def contract_lanes(a, b):
    return lax.dot_general(a, b, (((1,), (1,)), ((), ())), preferred_element_type=jnp.float32)


def each(count, body):
    def step(k, carry):
        body(k)
        return carry

    lax.fori_loop(1, count, step, 0)


Z_ORDER = (4, 3, 5, 2, 6, 1, 7)


def step_kernel(
    nd, nf,
    feat_any, req_any, w1s_any, w1n_any, adj_any, deg_any, self_any,
    adj_two_any, deg_two_any, w2s_any, w2n_any, grad_any,
    emb_ref, gw1_ref, gw2_ref,
    blocks, req_ref, req_by_x, req_in, stage, samp, table, w1,
    adj_ref, deg_ref, self_ref, padded, lists, slots, scale, own, total,
    adj_two, deg_two, w2s, w2n, grad_ref,
    x_out, x_in, gh_buf, hid, gpre, grads, turned, rows_t, w2_in, left, part, part_in, part1, in1, sum1,
    fetch, up_send, up_recv, down_send, down_recv, req_send, req_recv, x_send, x_recv,
    pair_send, pair_recv, w1_send, w1_recv, sib_send, sib_recv, a_send, a_recv, h_send, h_recv,
    p_send, p_recv, g_send, g_recv, q_send, q_recv, r_send, r_recv, b_send, b_recv,
    f_send, f_recv, smem_sem,
):
    d = lax.axis_index("dp")
    f = lax.axis_index("feat")
    nx, ny, nz = 4, nd // 4, nf // 2
    cap = 512
    x, y = lax.rem(d, nx), lax.div(d, nx)
    z, c = lax.div(f, 2), lax.rem(f, 2)
    block, half_rows = ROWS // nf, ROWS // 2
    mine = c * nz + z
    sibling = (d, 2 * z + 1 - c)

    def at_x(j):
        return lax.rem(x + j, nx)

    def at_y(s):
        return lax.rem(y + s + ny, ny)

    def along_z(k):
        to = lax.rem(z + k, nz)
        return to, (d, 2 * to + c)

    def dp_peer(k):
        return lax.rem(d + k, nd)

    offsets = [(dx, dy) for dy in range(ny) for dx in range(nx) if dx + dy > 0]
    offsets.sort(key=lambda o: -min(o[0], nx - o[0]) - min(o[1], ny - o[1]))

    def to_dp_peers(copy_to):
        for dx, dy in offsets:
            copy_to(at_y(dy) * nx + at_x(dx)).start()

    def remote(src, dst, send_sem, recv_sem, to):
        return pltpu.make_async_remote_copy(
            src_ref=src, dst_ref=dst, send_sem=send_sem, recv_sem=recv_sem,
            device_id=to, device_id_type=MESH,
        )

    def all_in(ref, sem):
        remote(ref, ref, sem, sem, sibling).wait_recv()

    def all_out(ref, sem):
        remote(ref, ref, sem, sem, sibling).wait_send()

    def core_rows(core, size):
        return pl.ds(pl.multiple_of(core * size, 16), size)

    barrier = pltpu.get_barrier_semaphore()

    def greet(to):
        pl.semaphore_signal(barrier, inc=1, device_id=to, device_id_type=MESH)

    sources = [
        (feat_any.at[:, 512 * q:512 * q + 512], blocks.at[y, 64 * q:64 * q + 64, :]) for q in range(4)
    ] + [
        (req_any, req_ref),
        (w1s_any, w1.at[z, 0, core_rows(c, 64), :]),
        (w1n_any, w1.at[z, 1, core_rows(c, 64), :]),
        (adj_any, adj_ref), (deg_any, deg_ref), (self_any, self_ref),
        (adj_two_any, adj_two), (deg_two_any, deg_two),
        (w2s_any, w2s), (w2n_any, w2n), (grad_any, grad_ref),
    ]
    kinds = (0, 0, 0, 0, 1, 2, 2, 3, 4, 5, 6, 7, 8, 9, 10)
    fetches = [pltpu.make_async_copy(src, dst, fetch.at[i]) for i, (src, dst) in zip(kinds, sources)]
    for copy in [fetches[4]] + fetches[:4] + fetches[5:7]:
        copy.start()

    greet(sibling)
    for k in range(1, nz):
        greet(along_z(k)[1])
    each(nd, lambda k: greet((dp_peer(k), f)))
    pl.semaphore_wait(barrier, 1 + nz - 1 + nd - 1)

    def req_copy(j):
        to = at_x(j)
        return remote(req_by_x.at[to], req_in.at[x], req_send.at[0], req_recv.at[0], (y * nx + to, f))

    def half(source, h):
        return blocks.at[source, core_rows(h, 128), :]

    def up_copy(t, source):
        part = half(source, lax.rem(t, 2))
        return remote(part, part, up_send.at[0], up_recv.at[t], (at_y(1) * nx + x, f))

    def down_copy(t, source):
        part = half(source, 1 - lax.rem(t, 2))
        return remote(part, part, down_send.at[0], down_recv.at[t], (at_y(-1) * nx + x, f))

    def w1_part(source):
        return w1.at[source, :, core_rows(c, 64), :]

    def w1_copy(k):
        return remote(w1_part(z), w1_part(z), w1_send.at[0], w1_recv.at[0], along_z(k)[1])

    def w1_over(core):
        ours = w1.at[:, :, core_rows(core, 64), :]
        return remote(ours, ours, sib_send.at[0], sib_recv.at[0], sibling)

    def first_copies(t):
        copies = []
        for up, h in ((True, t % 2), (False, 1 - t % 2)):
            for q in (2 * h, 2 * h + 1):
                copies.append(remote(
                    feat_any.at[:, 512 * q:512 * q + 512], blocks.at[y, 64 * q:64 * q + 64, :],
                    (up_send if up else down_send).at[0], (up_recv if up else down_recv).at[t],
                    (at_y(1 if up else -1) * nx + x, f),
                ))
        return copies

    for t in range(2):
        for copy in first_copies(t):
            copy.start()
    for copy in fetches[7:]:
        copy.start()
    fetches[4].wait()
    for owner in range(nd):
        req_by_x[owner % nx, owner // nx:owner // nx + 1, :] = req_ref[owner:owner + 1, :]
    for j in range(1, nx):
        req_copy(j).start()
    pltpu.make_async_copy(blocks.at[y], blocks.at[y], fetch.at[0]).wait()
    pltpu.make_async_copy(w1.at[z, :, core_rows(c, 64), :], w1.at[z, :, core_rows(c, 64), :], fetch.at[2]).wait()
    req_in[x] = req_by_x[x]
    all_in(req_in.at[pl.ds(0, nx - 1)], req_recv.at[0])

    def x_copy(source, j):
        slot = source * nx + x
        return remote(
            stage.at[source, j], samp.at[slot, core_rows(c, 64), :],
            x_send.at[0], x_recv.at[source], (y * nx + at_x(j), f),
        )

    def slots_of(source, count, core):
        return samp.at[pl.ds(source * nx, count), core_rows(core, 64), :]

    def pair_copy(source, core):
        ours = slots_of(source, nx, core)
        return remote(ours, ours, pair_send.at[0], pair_recv.at[source], sibling)

    node = lax.broadcasted_iota(jnp.int32, (512, cap), 0)

    def pick(source, j):
        asked = req_in[at_x(j), pl.ds(source, 1), :]
        low, quarter = asked & 511, asked >> 9
        one_hot = jnp.where(node == low, 1.0, 0.0).astype(jnp.bfloat16)
        rows = jnp.dot(blocks[source], one_hot, preferred_element_type=jnp.float32)
        chosen = rows[192:256, :]
        for q in range(3):
            chosen = jnp.where(quarter == q, rows[64 * q:64 * q + 64, :], chosen)
        return chosen.astype(jnp.bfloat16)

    def process(count, source_of):
        def step(k, carry):
            source = source_of(lax.div(k, nx))
            j = lax.rem(k + 2, nx)
            stage[source, j] = pick(source, j)

            @pl.when(j > 0)
            def _():
                x_copy(source, j).start()

            return carry

        lax.fori_loop(0, count * nx, step, 0)

    def collect(count, source_of):
        def step(u, carry):
            source = source_of(u)
            all_in(slots_of(source, nx - 1, c), x_recv.at[source])
            samp[source * nx + x, core_rows(c, 64), :] = stage[source, 0]
            pair_copy(source, c).start()
            return carry

        lax.fori_loop(0, count, step, 0)

    def absorb(count, source_of):
        def step(u, carry):
            source = source_of(u)
            pair_copy(source, 1 - c).wait_recv()
            for j in range(nx):
                slot = source * nx + j
                here = pl.ds(pl.multiple_of(slot * cap, 8), cap)
                table[here, :] = samp[slot].astype(jnp.float32).T
            return carry

        lax.fori_loop(0, count, step, 0)

    for k in Z_ORDER:
        w1_copy(k).start()
    steps = ny // 2

    def in_step(i):
        return 2 - lax.div(steps - i, steps) - lax.div(i, steps)

    def source_in(i):
        return lambda u: lax.rem(y + (2 * u - 1) * i + ny, ny)

    def pass_on(t, i):
        below, above = at_y(-i), at_y(i)
        more = t + 2 < ny - 1
        up_copy(t, below).wait_recv()

        @pl.when(more)
        def _():
            up_copy(t + 2, below).start()

        down_copy(t, above).wait_recv()

        @pl.when(more)
        def _():
            down_copy(t + 2, above).start()

    def gather_late(i):
        @pl.when(i >= 3)
        def _():
            absorb(in_step(i - 3), source_in(i - 3))

        @pl.when((i >= 2) & (i <= steps + 2))
        def _():
            collect(in_step(i - 2), source_in(i - 2))

    def ring_step(i, carry):
        @pl.when(i > 0)
        def _():
            pass_on(2 * i - 2, i)

        @pl.when((i > 0) & (i < steps))
        def _():
            pass_on(2 * i - 1, i)

        process(in_step(i), source_in(i))
        gather_late(i)
        return carry

    lax.fori_loop(0, steps + 1, ring_step, 0)

    for copy in fetches[7:]:
        copy.wait()
    fanout = adj_ref.shape[0]
    present = self_ref.shape[1]
    table[nd * cap:, :] = jnp.zeros((8, 128), jnp.float32)
    padded[...] = jnp.full(padded.shape, nd * cap, jnp.int32)
    for j in range(fanout):
        padded[j:j + 1, :present] = jnp.where(deg_ref[...] > j, adj_ref[j], nd * cap)
    padded[fanout:fanout + 1, :present] = self_ref[...]
    my_lanes_half = pl.ds(pl.multiple_of(c * half_rows, 128), half_rows)
    for j in range(fanout + 1):
        line = padded[j:j + 1, my_lanes_half]
        for to in range(nz):
            at = to * (fanout + 1) + j
            lists[at:at + 1, :block] = line[:, block * to:block * to + block]
    to_smem = pltpu.make_async_copy(lists, slots, smem_sem.at[0])
    to_smem.start()
    padded[:1, :] = jnp.ones((1, ROWS), jnp.int32)
    padded[:1, :present] = deg_ref[...]
    inverse = 1.0 / padded[:1, my_lanes_half].astype(jnp.float32)
    scale[...] = jnp.broadcast_to(jnp.broadcast_to(inverse, (8, half_rows)).T[:, :1], scale.shape)

    out_grad = grad_ref[...]
    degree_row = deg_two[...]
    targets = degree_row.shape[1]
    row = lax.broadcasted_iota(jnp.int32, (ROWS, targets), 0)
    counts = jnp.zeros((ROWS, targets), jnp.float32)
    for j in range(fanout):
        listed = jnp.where(degree_row > j, adj_two[j], -1)
        counts = counts + jnp.where(row == listed, 1.0, 0.0)
    degree_row = degree_row.astype(jnp.float32)
    degree = jnp.broadcast_to(degree_row, (8, targets)).T[:, :1]
    grad_agg = contract_lanes(out_grad, w2n[...]) / degree
    high = grad_agg.astype(jnp.bfloat16)
    low = (grad_agg - high.astype(jnp.float32)).astype(jnp.bfloat16)
    both = jnp.concatenate([counts, counts], axis=1).astype(jnp.bfloat16)
    gh_buf[...] = jnp.dot(both, jnp.concatenate([high, low], axis=0), preferred_element_type=jnp.float32)
    gh_buf[:targets, :] += contract_lanes(out_grad, w2s[...])
    counts = counts.T.astype(jnp.bfloat16)

    lax.fori_loop(steps + 1, steps + 4, lambda i, carry: (gather_late(i), carry)[1], 0)

    g_rows = core_rows(c, 32)

    def grad_copy(to):
        return remote(grad_ref.at[g_rows, :], grads.at[d, g_rows, :], g_send.at[0], g_recv.at[0], (to, f))

    some_grads = grads.at[pl.ds(0, nd - 1), pl.ds(0, 32), :]

    to_smem.wait()
    all_in(w1.at[pl.ds(0, nz - 1), :, pl.ds(0, 64), :], w1_recv.at[0])
    w1_over(c).start()

    def row_copy(k):
        to, device = along_z(k)
        return remote(x_out.at[to], x_in.at[z], a_send.at[0], a_recv.at[z], device)

    def row_back(k):
        source, device = along_z(k)
        return remote(x_out.at[source], x_in.at[source], a_send.at[0], a_recv.at[source], device)

    def sum_rows(t, carry):
        odd = lax.rem(t, 2)
        k = nz // 2 + lax.div(t, 2) * (1 - odd) - lax.div(t + 1, 2) * odd
        to = lax.rem(z + k, nz)
        base = to * (fanout + 1)
        for i in range(block):
            own[i:i + 1, :] = table[pl.ds(slots[base + fanout, i], 1), :]
            terms = [table[pl.ds(slots[base + j, i], 1), :] for j in range(fanout)]
            while len(terms) > 1:
                terms = [sum(terms[n:n + 2][1:], terms[n]) for n in range(0, len(terms), 2)]
            total[i:i + 1, :] = terms[0]
        x_out[to, :, :128] = own[...].astype(jnp.bfloat16)
        mean = total[...] * scale[pl.ds(pl.multiple_of(to * block, 8), block), :]
        x_out[to, :, 128:] = mean.astype(jnp.bfloat16)

        @pl.when(k > 0)
        def _():
            row_copy(k).start()

        return carry

    lax.fori_loop(0, nz, sum_rows, 0)
    to_dp_peers(grad_copy)
    grads[d, g_rows, :] = grad_ref[g_rows, :]
    x_in[z] = x_out[z]
    rows_t[...] = x_out[...].reshape(half_rows, 256).astype(jnp.float32).T.astype(jnp.bfloat16)
    w1_over(1 - c).wait_recv()

    pre = jnp.zeros((block, w1.shape[-1]), jnp.float32)
    for k in (0, 5, 4, 6, 3, 7, 2, 1):
        if k > 0:
            row_back(k).wait_recv()
        source = lax.rem(z + k, nz)
        pre = pre + jnp.dot(
            x_in[source], w1[source].reshape(256, w1.shape[-1]), preferred_element_type=jnp.float32
        )
    sig = 1.0 / (1.0 + jnp.exp(-pre))
    my_gh = gh_buf[pl.ds(pl.multiple_of(mine * block, 8), block), :]
    hid[mine] = (pre * sig).astype(jnp.bfloat16)
    gpre[z] = (my_gh * (sig * (1.0 + pre * (1.0 - sig)))).astype(jnp.bfloat16)

    def spread(buf, send_sem, recv_sem, k):
        return remote(buf.at[mine], buf.at[mine], send_sem.at[0], recv_sem.at[0], along_z(k)[1])

    def most(buf):
        return buf.at[pl.ds(0, nz - 1)]

    def hand_over(buf, core, i):
        ours = buf.at[pl.ds(core * nz, nz)]
        return remote(ours, ours, sib_send.at[i], sib_recv.at[i], sibling)

    def gpre_copy(k):
        return remote(gpre.at[z], gpre.at[z], p_send.at[0], p_recv.at[0], along_z(k)[1])

    for k in Z_ORDER:
        spread(hid, h_send, h_recv, k).start()
    for k in Z_ORDER:
        gpre_copy(k).start()
    all_in(most(hid), h_recv.at[0])
    hand_over(hid, c, 1).start()
    all_in(most(gpre), p_recv.at[0])
    sums = jnp.dot(
        rows_t[...], gpre[...].reshape(half_rows, gpre.shape[-1]), preferred_element_type=jnp.float32
    )
    part[...] = sums.reshape(part.shape)

    def part_copy(core):
        return remote(part.at[:, core], part_in, sib_send.at[2], sib_recv.at[2], sibling)

    part_copy(1 - c).start()
    hand_over(hid, 1 - c, 1).wait_recv()

    hidden = hid[...].reshape(ROWS, hid.shape[-1])
    self_hidden = hidden[:targets, :]
    agg_two = jnp.dot(counts, hidden, preferred_element_type=jnp.float32) / degree
    agg_two = agg_two.astype(jnp.bfloat16)
    pair = jnp.concatenate([self_hidden, agg_two], axis=0)
    turned[...] = pair.astype(jnp.float32).T.astype(jnp.bfloat16)
    columns = core_rows(f, 16)

    def w2_copy(to):
        return remote(turned.at[columns, :], w2_in.at[d], q_send.at[0], q_recv.at[0], (to, f))

    to_dp_peers(w2_copy)
    w2_in[d] = turned[columns, :]

    part_copy(c).wait_recv()
    part1[...] = (part[:, c] + part_in[...]).reshape(part1.shape)

    def tile_of(index):
        return (
            pl.ds(pl.multiple_of(lax.div(index, 2) * 8, 8), 8),
            pl.ds(pl.multiple_of(lax.rem(index, 2) * 128, 128), 128),
        )

    my_rows, my_lanes = tile_of(d)

    def w1_sum_copy(to):
        rows, lanes = tile_of(to)
        return remote(part1.at[rows, lanes], in1.at[d], r_send.at[0], r_recv.at[0], (to, f))

    some_tiles = in1.at[pl.ds(0, nd - 1)]
    to_dp_peers(w1_sum_copy)
    in1[d] = part1[my_rows, my_lanes]

    all_in(some_grads, g_recv.at[0])

    def grads_over(core):
        ours = grads.at[:, core_rows(core, 32), :]
        return remote(ours, ours, sib_send.at[3], sib_recv.at[3], sibling)

    grads_over(c).start()
    emb = jnp.dot(self_hidden, w2s[...], preferred_element_type=jnp.float32)
    emb = emb + jnp.dot(agg_two, w2n[...], preferred_element_type=jnp.float32)
    emb_ref[...] = emb.astype(jnp.bfloat16)
    grads_over(1 - c).wait_recv()
    all_in(w2_in.at[pl.ds(0, nd - 1)], q_recv.at[0])
    lane = lax.broadcasted_iota(jnp.int32, (16, 128), 1)
    for p in range(nd // 2):
        first, second = w2_in[2 * p].astype(jnp.float32), w2_in[2 * p + 1].astype(jnp.float32)
        selfs = jnp.where(lane < 64, first, pltpu.roll(second, 64, 1))
        neighs = jnp.where(lane < 64, pltpu.roll(first, 64, 1), second)
        left[:, 128 * p:128 * p + 128] = jnp.concatenate([selfs, neighs], axis=0).astype(jnp.bfloat16)
    total2 = jnp.dot(
        left[...], grads[...].reshape(nd * targets, grads.shape[-1]), preferred_element_type=jnp.float32
    )
    gw2_ref[mine] = total2.astype(jnp.bfloat16)
    for k in Z_ORDER:
        spread(gw2_ref, f_send, f_recv, k).start()

    all_in(some_tiles, r_recv.at[0])
    sum1[...] = jnp.sum(in1[...], axis=0)
    gw1_ref[my_rows, my_lanes] = sum1[...]

    def w1_out(to):
        return remote(sum1, gw1_ref.at[my_rows, my_lanes], b_send.at[0], b_recv.at[0], (to, f))

    to_dp_peers(w1_out)
    all_in(most(gw2_ref), f_recv.at[0])
    hand_over(gw2_ref, c, 4).start()

    all_out(req_in.at[pl.ds(0, nx - 1)], req_send.at[0])
    all_out(blocks.at[pl.ds(0, ny - 1), pl.ds(0, 128), :], up_send.at[0])
    all_out(blocks.at[pl.ds(0, ny - 1), pl.ds(0, 128), :], down_send.at[0])
    all_out(w1.at[pl.ds(0, nz - 1), :, pl.ds(0, 64), :], w1_send.at[0])
    all_out(most(x_out), a_send.at[0])
    all_out(most(hid), h_send.at[0])
    all_out(most(gpre), p_send.at[0])
    all_out(most(gw2_ref), f_send.at[0])
    w1_over(c).wait_send()
    hand_over(hid, c, 1).wait_send()
    part_copy(1 - c).wait_send()
    grads_over(c).wait_send()
    all_out(stage.at[:, pl.ds(0, nx - 1)], x_send.at[0])
    all_out(samp.at[:, core_rows(c, 64), :], pair_send.at[0])
    all_out(some_grads, g_send.at[0])
    all_out(w2_in.at[pl.ds(0, nd - 1)], q_send.at[0])
    all_out(some_tiles, r_send.at[0])
    hand_over(gw2_ref, 1 - c, 4).wait_recv()
    hand_over(gw2_ref, c, 4).wait_send()
    all_in(some_tiles, b_recv.at[0])
    all_out(some_tiles, b_send.at[0])


def finish_kernel(emb_ref, gw1_ref, gw2_ref, out_emb, out_1s, out_1n, out_2s, out_2n):
    out_emb[...] = emb_ref[...]
    out_1s[...] = gw1_ref[:64, :]
    out_1n[...] = gw1_ref[64:, :]
    nz = gw2_ref.shape[0] // 2
    for i in range(2 * nz):
        f = 2 * (i % nz) + i // nz
        out_2s[16 * f:16 * f + 16, :] = gw2_ref[i, :16, :].astype(jnp.float32)
        out_2n[16 * f:16 * f + 16, :] = gw2_ref[i, 16:, :].astype(jnp.float32)


def local(
    nd, nf,
    features, request_rows, self_slots, adj_one, deg_one, adj_two, deg_two,
    w1_self, w1_neigh, w2_self, w2_neigh, out_grad,
):
    vmem = pl.BlockSpec(memory_space=pltpu.VMEM)
    anywhere = pl.BlockSpec(memory_space=pltpu.HBM)
    f32, bf16, i32 = jnp.float32, jnp.bfloat16, jnp.int32
    dma = pltpu.SemaphoreType.DMA
    nx, ny, nz = 4, nd // 4, nf // 2
    block, half = ROWS // nf, ROWS // 2
    adj_one = adj_one.transpose(2, 0, 1)
    adj_two = adj_two.transpose(2, 0, 1)
    lists = nz * (adj_one.shape[0] + 1)
    emb, gw1, gw2 = pl.pallas_call(
        functools.partial(step_kernel, nd, nf),
        out_shape=(
            jax.ShapeDtypeStruct((64, 256), bf16),
            jax.ShapeDtypeStruct((128, 256), f32),
            jax.ShapeDtypeStruct((nf, 32, 256), bf16),
        ),
        in_specs=[anywhere] * 12,
        out_specs=(vmem,) * 3,
        scratch_shapes=[
            pltpu.VMEM((ny, 256, 512), bf16),
            pltpu.VMEM((nd, 512), i32),
            pltpu.VMEM((nx, ny, 512), i32),
            pltpu.VMEM((nx, ny, 512), i32),
            pltpu.VMEM((ny, nx, 64, 512), bf16),
            pltpu.VMEM((nd, 128, 512), bf16),
            pltpu.VMEM((nd * 512 + 8, 128), f32),
            pltpu.VMEM((nz, 2, 128, 256), bf16),
            pltpu.VMEM(adj_one.shape, i32),
            pltpu.VMEM(deg_one.shape, i32),
            pltpu.VMEM(self_slots.shape, i32),
            pltpu.VMEM((16, ROWS), i32),
            pltpu.VMEM((lists, 128), i32),
            pltpu.SMEM((lists, 128), i32),
            pltpu.VMEM((half, 128), f32),
            pltpu.VMEM((block, 128), f32),
            pltpu.VMEM((block, 128), f32),
            pltpu.VMEM(adj_two.shape, i32),
            pltpu.VMEM(deg_two.shape, i32),
            pltpu.VMEM((256, 256), bf16),
            pltpu.VMEM((256, 256), bf16),
            pltpu.VMEM(out_grad.shape, bf16),
            pltpu.VMEM((nz, block, 256), bf16),
            pltpu.VMEM((nz, block, 256), bf16),
            pltpu.VMEM((ROWS, 256), f32),
            pltpu.VMEM((nf, block, 256), bf16),
            pltpu.VMEM((nz, block, 256), bf16),
            pltpu.VMEM((nd, 64, 256), bf16),
            pltpu.VMEM((256, 128), bf16),
            pltpu.VMEM((256, half), bf16),
            pltpu.VMEM((nd, 16, 128), bf16),
            pltpu.VMEM((32, nd * 64), bf16),
            pltpu.VMEM((2, 2, 64, 256), f32),
            pltpu.VMEM((2, 64, 256), f32),
            pltpu.VMEM((128, 256), f32),
            pltpu.VMEM((nd, 8, 128), f32),
            pltpu.VMEM((8, 128), f32),
            dma((11,)),
            dma((1,)), dma((ny - 1,)), dma((1,)), dma((ny - 1,)),
            dma((1,)), dma((1,)), dma((1,)), dma((ny,)), dma((1,)), dma((ny,)),
            dma((1,)), dma((1,)), dma((5,)), dma((5,)),
            dma((1,)), dma((nz,)), dma((1,)), dma((1,)), dma((1,)), dma((1,)),
            dma((1,)), dma((1,)), dma((1,)), dma((1,)),
            dma((1,)), dma((1,)), dma((1,)), dma((1,)),
            dma((1,)), dma((1,)), dma((1,)),
        ],
        compiler_params=pltpu.CompilerParams(
            collective_id=1, has_side_effects=True, vmem_limit_bytes=60 * 1024 * 1024
        ),
        name="train_step",
    )(
        features.T, request_rows[0], w1_self, w1_neigh, adj_one, deg_one, self_slots,
        adj_two, deg_two, w2_self, w2_neigh, out_grad,
    )
    return pl.pallas_call(
        finish_kernel,
        out_shape=(
            jax.ShapeDtypeStruct((64, 256), bf16),
            jax.ShapeDtypeStruct((64, 256), f32),
            jax.ShapeDtypeStruct((64, 256), f32),
            jax.ShapeDtypeStruct((256, 256), f32),
            jax.ShapeDtypeStruct((256, 256), f32),
        ),
        in_specs=[vmem] * 3,
        out_specs=(vmem,) * 5,
        compiler_params=pltpu.CompilerParams(vmem_limit_bytes=60 * 1024 * 1024),
        name="finish",
    )(emb, gw1, gw2)


def solution(mesh):
    return jax.shard_map(
        functools.partial(local, mesh.shape["dp"], mesh.shape["feat"]),
        mesh=mesh,
        in_specs=(
            P("dp", "feat"),
            P("dp", None, None),
            P("dp", None),
            P("dp", None, None),
            P("dp", None),
            P("dp", None, None),
            P("dp", None),
            P("feat", None),
            P("feat", None),
            P(),
            P(),
            P("dp", None),
        ),
        out_specs=(P("dp", None), P("feat", None), P("feat", None), P(), P()),
        check_vma=False,
    )
```

```python
import functools

import jax
import jax.numpy as jnp
from jax import lax
from jax.experimental import pallas as pl
from jax.experimental.pallas import tpu as pltpu
from jax.sharding import PartitionSpec as P

MESH = pl.DeviceIdType.MESH
ROWS = 768


def contract_rows(a, b):
    return lax.dot_general(a, b, (((0,), (0,)), ((), ())), preferred_element_type=jnp.float32)


def contract_lanes(a, b):
    return lax.dot_general(a, b, (((1,), (1,)), ((), ())), preferred_element_type=jnp.float32)


Z_ORDER = (4, 3, 5, 2, 6, 1, 7)


def step_kernel(
    nd, nf,
    feat_any, req_any, w1s_any, w1n_any, adj_any, deg_any, self_any,
    adj_two_any, deg_two_any, w2s_any, w2n_any, grad_any,
    emb_ref, gw1_ref, gw2_ref,
    blocks, req_ref, req_by_x, req_in, stage, samp, table, w1,
    adj_ref, deg_ref, self_ref, padded, lists, slots, scale, own, total,
    adj_two, deg_two, w2s, w2n, grad_ref, counts_ref, degree_ref,
    x_out, x_in, gh_buf, hid, gpre, grads, turned, rows_t, w2_in, left, part, part_in, part1, in1, sum1,
    fetch, up_send, up_recv, down_send, down_recv, req_send, req_recv, x_send, x_recv,
    pair_send, pair_recv, w1_send, w1_recv, sib_send, sib_recv, a_send, a_recv, h_send, h_recv,
    p_send, p_recv, g_send, g_recv, q_send, q_recv, r_send, r_recv, b_send, b_recv,
    f_send, f_recv, smem_sem,
):
    d = lax.axis_index("dp")
    f = lax.axis_index("feat")
    nx, ny, nz = 4, nd // 4, nf // 2
    cap = 512
    x, y = lax.rem(d, nx), lax.div(d, nx)
    z, c = lax.div(f, 2), lax.rem(f, 2)
    block, half_rows = ROWS // nf, ROWS // 2
    mine = c * nz + z
    sibling = (d, 2 * z + 1 - c)

    def at_x(j):
        return lax.rem(x + j, nx)

    def at_y(s):
        return lax.rem(y + s + ny, ny)

    def along_z(k):
        to = lax.rem(z + k, nz)
        return to, (d, 2 * to + c)

    offsets = [(dx, dy) for dy in range(ny) for dx in range(nx) if dx + dy > 0]
    offsets.sort(key=lambda o: -min(o[0], nx - o[0]) - min(o[1], ny - o[1]))

    def to_dp_peers(copy_to):
        for dx, dy in offsets:
            copy_to(at_y(dy) * nx + at_x(dx)).start()

    def remote(src, dst, send_sem, recv_sem, to):
        return pltpu.make_async_remote_copy(
            src_ref=src, dst_ref=dst, send_sem=send_sem, recv_sem=recv_sem,
            device_id=to, device_id_type=MESH,
        )

    def all_in(ref, sem):
        remote(ref, ref, sem, sem, sibling).wait_recv()

    def all_out(ref, sem):
        remote(ref, ref, sem, sem, sibling).wait_send()

    def core_rows(core, size):
        return pl.ds(pl.multiple_of(core * size, 16), size)

    barrier = pltpu.get_barrier_semaphore()

    def greet(to):
        pl.semaphore_signal(barrier, inc=1, device_id=to, device_id_type=MESH)

    sources = [
        (feat_any.at[:, 512 * q:512 * q + 512], blocks.at[y, 64 * q:64 * q + 64, :]) for q in range(4)
    ] + [
        (req_any, req_ref),
        (w1s_any, w1.at[z, 0, core_rows(c, 64), :]),
        (w1n_any, w1.at[z, 1, core_rows(c, 64), :]),
        (adj_any, adj_ref), (deg_any, deg_ref), (self_any, self_ref),
        (adj_two_any, adj_two), (deg_two_any, deg_two),
        (w2s_any, w2s), (w2n_any, w2n), (grad_any, grad_ref),
    ]
    kinds = (0, 0, 0, 0, 1, 2, 2, 3, 4, 5, 6, 7, 8, 9, 10)
    fetches = [pltpu.make_async_copy(src, dst, fetch.at[i]) for i, (src, dst) in zip(kinds, sources)]
    for copy in [fetches[4]] + fetches[:4] + fetches[5:7]:
        copy.start()

    for s in (1, -1):
        greet((at_y(s) * nx + x, f))
    for j in range(1, nx):
        greet((y * nx + at_x(j), f))
    greet(sibling)
    for k in range(1, nz):
        greet(along_z(k)[1])
    pl.semaphore_wait(barrier, 2 + nx - 1 + 1 + nz - 1)

    def req_copy(j):
        to = at_x(j)
        return remote(req_by_x.at[to], req_in.at[x], req_send.at[0], req_recv.at[0], (y * nx + to, f))

    def half(source, h):
        return blocks.at[source, core_rows(h, 128), :]

    def up_copy(t, source):
        part = half(source, lax.rem(t, 2))
        return remote(part, part, up_send.at[0], up_recv.at[t], (at_y(1) * nx + x, f))

    def down_copy(t, source):
        part = half(source, 1 - lax.rem(t, 2))
        return remote(part, part, down_send.at[0], down_recv.at[t], (at_y(-1) * nx + x, f))

    def w1_part(source):
        return w1.at[source, :, core_rows(c, 64), :]

    def w1_copy(k):
        return remote(w1_part(z), w1_part(z), w1_send.at[0], w1_recv.at[0], along_z(k)[1])

    def w1_over(core):
        ours = w1.at[:, :, core_rows(core, 64), :]
        return remote(ours, ours, sib_send.at[0], sib_recv.at[0], sibling)

    def first_copies(t):
        copies = []
        for up, h in ((True, t % 2), (False, 1 - t % 2)):
            for q in (2 * h, 2 * h + 1):
                copies.append(remote(
                    feat_any.at[:, 512 * q:512 * q + 512], blocks.at[y, 64 * q:64 * q + 64, :],
                    (up_send if up else down_send).at[0], (up_recv if up else down_recv).at[t],
                    (at_y(1 if up else -1) * nx + x, f),
                ))
        return copies

    for t in range(2):
        for copy in first_copies(t):
            copy.start()
    for copy in fetches[7:]:
        copy.start()
    fetches[4].wait()
    for owner in range(nd):
        req_by_x[owner % nx, owner // nx:owner // nx + 1, :] = req_ref[owner:owner + 1, :]
    for j in range(1, nx):
        req_copy(j).start()
    pltpu.make_async_copy(blocks.at[y], blocks.at[y], fetch.at[0]).wait()
    pltpu.make_async_copy(w1.at[z, :, core_rows(c, 64), :], w1.at[z, :, core_rows(c, 64), :], fetch.at[2]).wait()
    req_in[x] = req_by_x[x]
    all_in(req_in.at[pl.ds(0, nx - 1)], req_recv.at[0])

    def x_copy(source, j):
        slot = source * nx + x
        return remote(
            stage.at[source, j], samp.at[slot, core_rows(c, 64), :],
            x_send.at[0], x_recv.at[source], (y * nx + at_x(j), f),
        )

    def slots_of(source, count, core):
        return samp.at[pl.ds(source * nx, count), core_rows(core, 64), :]

    def pair_copy(source, core):
        ours = slots_of(source, nx, core)
        return remote(ours, ours, pair_send.at[0], pair_recv.at[source], sibling)

    node = lax.broadcasted_iota(jnp.int32, (512, cap), 0)

    def pick(source, j):
        asked = req_in[at_x(j), pl.ds(source, 1), :]
        low, quarter = asked & 511, asked >> 9
        one_hot = jnp.where(node == low, 1.0, 0.0).astype(jnp.bfloat16)
        rows = jnp.dot(blocks[source], one_hot, preferred_element_type=jnp.float32)
        chosen = rows[192:256, :]
        for q in range(3):
            chosen = jnp.where(quarter == q, rows[64 * q:64 * q + 64, :], chosen)
        return chosen.astype(jnp.bfloat16)

    def process(count, source_of):
        def step(k, carry):
            source = source_of(lax.div(k, nx))
            j = lax.rem(k + 2, nx)
            stage[source, j] = pick(source, j)

            @pl.when(j > 0)
            def _():
                x_copy(source, j).start()

            return carry

        lax.fori_loop(0, count * nx, step, 0)

    def collect(count, source_of):
        def step(u, carry):
            source = source_of(u)
            all_in(slots_of(source, nx - 1, c), x_recv.at[source])
            samp[source * nx + x, core_rows(c, 64), :] = stage[source, 0]
            pair_copy(source, c).start()
            return carry

        lax.fori_loop(0, count, step, 0)

    def absorb(count, source_of):
        def step(u, carry):
            source = source_of(u)
            pair_copy(source, 1 - c).wait_recv()
            for j in range(nx):
                slot = source * nx + j
                here = pl.ds(pl.multiple_of(slot * cap, 8), cap)
                table[here, :] = samp[slot].astype(jnp.float32).T
            return carry

        lax.fori_loop(0, count, step, 0)

    for k in Z_ORDER:
        w1_copy(k).start()
    steps = ny // 2

    def in_step(i):
        return 2 - lax.div(steps - i, steps) - lax.div(i, steps)

    def source_in(i):
        return lambda u: lax.rem(y + (2 * u - 1) * i + ny, ny)

    def pass_on(t, i):
        below, above = at_y(-i), at_y(i)
        more = t + 2 < ny - 1
        up_copy(t, below).wait_recv()

        @pl.when(more)
        def _():
            up_copy(t + 2, below).start()

        down_copy(t, above).wait_recv()

        @pl.when(more)
        def _():
            down_copy(t + 2, above).start()

    def gather_late(i):
        @pl.when(i >= 3)
        def _():
            absorb(in_step(i - 3), source_in(i - 3))

        @pl.when((i >= 2) & (i <= steps + 2))
        def _():
            collect(in_step(i - 2), source_in(i - 2))

    fanout = adj_ref.shape[0]
    present = self_ref.shape[1]
    targets = deg_two.shape[1]
    to_smem = pltpu.make_async_copy(lists, slots, smem_sem.at[0])

    def prepare():
        for copy in fetches[7:]:
            copy.wait()
        table[nd * cap:, :] = jnp.zeros((8, 128), jnp.float32)
        padded[...] = jnp.full(padded.shape, nd * cap, jnp.int32)
        for j in range(fanout):
            padded[j:j + 1, :present] = jnp.where(deg_ref[...] > j, adj_ref[j], nd * cap)
        padded[fanout:fanout + 1, :present] = self_ref[...]
        my_lanes_half = pl.ds(pl.multiple_of(c * half_rows, 128), half_rows)
        for j in range(fanout + 1):
            line = padded[j:j + 1, my_lanes_half]
            for to in range(nz):
                at = to * (fanout + 1) + j
                lists[at:at + 1, :block] = line[:, block * to:block * to + block]
        to_smem.start()
        padded[:1, :] = jnp.ones((1, ROWS), jnp.int32)
        padded[:1, :present] = deg_ref[...]
        inverse = 1.0 / padded[:1, my_lanes_half].astype(jnp.float32)
        scale[...] = jnp.broadcast_to(jnp.broadcast_to(inverse, (8, half_rows)).T[:, :1], scale.shape)

        out_grad = grad_ref[...]
        degree_row = deg_two[...]
        row = lax.broadcasted_iota(jnp.int32, (ROWS, targets), 0)
        counts = jnp.zeros((ROWS, targets), jnp.float32)
        for j in range(fanout):
            listed = jnp.where(degree_row > j, adj_two[j], -1)
            counts = counts + jnp.where(row == listed, 1.0, 0.0)
        degree_row = degree_row.astype(jnp.float32)
        degree = jnp.broadcast_to(degree_row, (8, targets)).T[:, :1]
        degree_ref[...] = jnp.broadcast_to(degree, degree_ref.shape)
        grad_agg = contract_lanes(out_grad, w2n[...]) / degree
        high = grad_agg.astype(jnp.bfloat16)
        low = (grad_agg - high.astype(jnp.float32)).astype(jnp.bfloat16)
        both = jnp.concatenate([counts, counts], axis=1).astype(jnp.bfloat16)
        gh_buf[...] = jnp.dot(both, jnp.concatenate([high, low], axis=0), preferred_element_type=jnp.float32)
        gh_buf[:targets, :] += contract_lanes(out_grad, w2s[...])
        counts_ref[...] = counts.T.astype(jnp.bfloat16)

    def ring_step(i, carry):
        @pl.when(i > 0)
        def _():
            pass_on(2 * i - 2, i)

        @pl.when((i > 0) & (i < steps))
        def _():
            pass_on(2 * i - 1, i)

        process(in_step(i), source_in(i))

        @pl.when(i == 1)
        def _():
            prepare()

        gather_late(i)
        return carry

    lax.fori_loop(0, steps + 1, ring_step, 0)

    lax.fori_loop(steps + 1, steps + 4, lambda i, carry: (gather_late(i), carry)[1], 0)

    g_rows = core_rows(c, 32)

    def grad_copy(to):
        return remote(grad_ref.at[g_rows, :], grads.at[d, g_rows, :], g_send.at[0], g_recv.at[0], (to, f))

    some_grads = grads.at[pl.ds(0, nd - 1), pl.ds(0, 32), :]

    to_smem.wait()
    all_in(w1.at[pl.ds(0, nz - 1), :, pl.ds(0, 64), :], w1_recv.at[0])
    w1_over(c).start()

    def row_copy(k):
        to, device = along_z(k)
        return remote(x_out.at[to], x_in.at[z], a_send.at[0], a_recv.at[z], device)

    def row_back(k):
        source, device = along_z(k)
        return remote(x_out.at[source], x_in.at[source], a_send.at[0], a_recv.at[source], device)

    def sum_rows(t, carry):
        odd = lax.rem(t, 2)
        k = nz // 2 + lax.div(t, 2) * (1 - odd) - lax.div(t + 1, 2) * odd
        to = lax.rem(z + k, nz)
        base = to * (fanout + 1)
        for i in range(block):
            own[i:i + 1, :] = table[pl.ds(slots[base + fanout, i], 1), :]
            terms = [table[pl.ds(slots[base + j, i], 1), :] for j in range(fanout)]
            while len(terms) > 1:
                terms = [sum(terms[n:n + 2][1:], terms[n]) for n in range(0, len(terms), 2)]
            total[i:i + 1, :] = terms[0]
        x_out[to, :, :128] = own[...].astype(jnp.bfloat16)
        mean = total[...] * scale[pl.ds(pl.multiple_of(to * block, 8), block), :]
        x_out[to, :, 128:] = mean.astype(jnp.bfloat16)

        @pl.when(k > 0)
        def _():
            row_copy(k).start()

        return carry

    lax.fori_loop(0, nz, sum_rows, 0)
    to_dp_peers(grad_copy)
    grads[d, g_rows, :] = grad_ref[g_rows, :]
    x_in[z] = x_out[z]
    rows_t[...] = x_out[...].reshape(half_rows, 256).astype(jnp.float32).T.astype(jnp.bfloat16)
    w1_over(1 - c).wait_recv()

    pre = jnp.zeros((block, w1.shape[-1]), jnp.float32)
    for k in (0, 5, 4, 6, 3, 7, 2, 1):
        if k > 0:
            row_back(k).wait_recv()
        source = lax.rem(z + k, nz)
        pre = pre + jnp.dot(
            x_in[source], w1[source].reshape(256, w1.shape[-1]), preferred_element_type=jnp.float32
        )
    sig = 1.0 / (1.0 + jnp.exp(-pre))
    my_gh = gh_buf[pl.ds(pl.multiple_of(mine * block, 8), block), :]
    hid[mine] = (pre * sig).astype(jnp.bfloat16)
    gpre[z] = (my_gh * (sig * (1.0 + pre * (1.0 - sig)))).astype(jnp.bfloat16)

    def spread(buf, send_sem, recv_sem, k):
        return remote(buf.at[mine], buf.at[mine], send_sem.at[0], recv_sem.at[0], along_z(k)[1])

    def most(buf):
        return buf.at[pl.ds(0, nz - 1)]

    def hand_over(buf, core, i):
        ours = buf.at[pl.ds(core * nz, nz)]
        return remote(ours, ours, sib_send.at[i], sib_recv.at[i], sibling)

    def gpre_copy(k):
        return remote(gpre.at[z], gpre.at[z], p_send.at[0], p_recv.at[0], along_z(k)[1])

    for k in Z_ORDER:
        spread(hid, h_send, h_recv, k).start()
    for k in Z_ORDER:
        gpre_copy(k).start()
    all_in(most(hid), h_recv.at[0])
    hand_over(hid, c, 1).start()
    all_in(most(gpre), p_recv.at[0])
    sums = jnp.dot(
        rows_t[...], gpre[...].reshape(half_rows, gpre.shape[-1]), preferred_element_type=jnp.float32
    )
    part[...] = sums.reshape(part.shape)

    def part_copy(core):
        return remote(part.at[:, core], part_in, sib_send.at[2], sib_recv.at[2], sibling)

    part_copy(1 - c).start()
    hand_over(hid, 1 - c, 1).wait_recv()

    hidden = hid[...].reshape(ROWS, hid.shape[-1])
    self_hidden = hidden[:targets, :]
    agg_two = jnp.dot(counts_ref[...], hidden, preferred_element_type=jnp.float32) / degree_ref[...]
    agg_two = agg_two.astype(jnp.bfloat16)
    pair = jnp.concatenate([self_hidden, agg_two], axis=0)
    turned[...] = pair.astype(jnp.float32).T.astype(jnp.bfloat16)
    columns = core_rows(f, 16)

    def w2_copy(to):
        return remote(turned.at[columns, :], w2_in.at[d], q_send.at[0], q_recv.at[0], (to, f))

    to_dp_peers(w2_copy)
    w2_in[d] = turned[columns, :]

    part_copy(c).wait_recv()
    part1[...] = (part[:, c] + part_in[...]).reshape(part1.shape)

    def tile_of(index):
        return (
            pl.ds(pl.multiple_of(lax.div(index, 2) * 8, 8), 8),
            pl.ds(pl.multiple_of(lax.rem(index, 2) * 128, 128), 128),
        )

    my_rows, my_lanes = tile_of(d)

    def w1_sum_copy(to):
        rows, lanes = tile_of(to)
        return remote(part1.at[rows, lanes], in1.at[d], r_send.at[0], r_recv.at[0], (to, f))

    some_tiles = in1.at[pl.ds(0, nd - 1)]
    to_dp_peers(w1_sum_copy)
    in1[d] = part1[my_rows, my_lanes]

    all_in(some_grads, g_recv.at[0])

    def grads_over(core):
        ours = grads.at[:, core_rows(core, 32), :]
        return remote(ours, ours, sib_send.at[3], sib_recv.at[3], sibling)

    grads_over(c).start()
    emb = jnp.dot(self_hidden, w2s[...], preferred_element_type=jnp.float32)
    emb = emb + jnp.dot(agg_two, w2n[...], preferred_element_type=jnp.float32)
    emb_ref[...] = emb.astype(jnp.bfloat16)
    grads_over(1 - c).wait_recv()
    all_in(w2_in.at[pl.ds(0, nd - 1)], q_recv.at[0])
    lane = lax.broadcasted_iota(jnp.int32, (16, 128), 1)
    for p in range(nd // 2):
        first, second = w2_in[2 * p].astype(jnp.float32), w2_in[2 * p + 1].astype(jnp.float32)
        selfs = jnp.where(lane < 64, first, pltpu.roll(second, 64, 1))
        neighs = jnp.where(lane < 64, pltpu.roll(first, 64, 1), second)
        left[:, 128 * p:128 * p + 128] = jnp.concatenate([selfs, neighs], axis=0).astype(jnp.bfloat16)
    total2 = jnp.dot(
        left[...], grads[...].reshape(nd * targets, grads.shape[-1]), preferred_element_type=jnp.float32
    )
    gw2_ref[mine] = total2.astype(jnp.bfloat16)
    for k in Z_ORDER:
        spread(gw2_ref, f_send, f_recv, k).start()

    all_in(some_tiles, r_recv.at[0])
    sum1[...] = jnp.sum(in1[...], axis=0)
    gw1_ref[my_rows, my_lanes] = sum1[...]

    def w1_out(to):
        return remote(sum1, gw1_ref.at[my_rows, my_lanes], b_send.at[0], b_recv.at[0], (to, f))

    to_dp_peers(w1_out)
    all_in(most(gw2_ref), f_recv.at[0])
    hand_over(gw2_ref, c, 4).start()

    all_out(req_in.at[pl.ds(0, nx - 1)], req_send.at[0])
    all_out(blocks.at[pl.ds(0, ny - 1), pl.ds(0, 128), :], up_send.at[0])
    all_out(blocks.at[pl.ds(0, ny - 1), pl.ds(0, 128), :], down_send.at[0])
    all_out(w1.at[pl.ds(0, nz - 1), :, pl.ds(0, 64), :], w1_send.at[0])
    all_out(most(x_out), a_send.at[0])
    all_out(most(hid), h_send.at[0])
    all_out(most(gpre), p_send.at[0])
    all_out(most(gw2_ref), f_send.at[0])
    w1_over(c).wait_send()
    hand_over(hid, c, 1).wait_send()
    part_copy(1 - c).wait_send()
    grads_over(c).wait_send()
    all_out(stage.at[:, pl.ds(0, nx - 1)], x_send.at[0])
    all_out(samp.at[:, core_rows(c, 64), :], pair_send.at[0])
    all_out(some_grads, g_send.at[0])
    all_out(w2_in.at[pl.ds(0, nd - 1)], q_send.at[0])
    all_out(some_tiles, r_send.at[0])
    hand_over(gw2_ref, 1 - c, 4).wait_recv()
    hand_over(gw2_ref, c, 4).wait_send()
    all_in(some_tiles, b_recv.at[0])
    all_out(some_tiles, b_send.at[0])


def finish_kernel(emb_ref, gw1_ref, gw2_ref, out_emb, out_1s, out_1n, out_2s, out_2n):
    out_emb[...] = emb_ref[...]
    out_1s[...] = gw1_ref[:64, :]
    out_1n[...] = gw1_ref[64:, :]
    nz = gw2_ref.shape[0] // 2
    for i in range(2 * nz):
        f = 2 * (i % nz) + i // nz
        out_2s[16 * f:16 * f + 16, :] = gw2_ref[i, :16, :].astype(jnp.float32)
        out_2n[16 * f:16 * f + 16, :] = gw2_ref[i, 16:, :].astype(jnp.float32)


def local(
    nd, nf,
    features, request_rows, self_slots, adj_one, deg_one, adj_two, deg_two,
    w1_self, w1_neigh, w2_self, w2_neigh, out_grad,
):
    vmem = pl.BlockSpec(memory_space=pltpu.VMEM)
    anywhere = pl.BlockSpec(memory_space=pltpu.HBM)
    f32, bf16, i32 = jnp.float32, jnp.bfloat16, jnp.int32
    dma = pltpu.SemaphoreType.DMA
    nx, ny, nz = 4, nd // 4, nf // 2
    block, half = ROWS // nf, ROWS // 2
    adj_one = adj_one.transpose(2, 0, 1)
    adj_two = adj_two.transpose(2, 0, 1)
    lists = nz * (adj_one.shape[0] + 1)
    emb, gw1, gw2 = pl.pallas_call(
        functools.partial(step_kernel, nd, nf),
        out_shape=(
            jax.ShapeDtypeStruct((64, 256), bf16),
            jax.ShapeDtypeStruct((128, 256), f32),
            jax.ShapeDtypeStruct((nf, 32, 256), bf16),
        ),
        in_specs=[anywhere] * 12,
        out_specs=(vmem,) * 3,
        scratch_shapes=[
            pltpu.VMEM((ny, 256, 512), bf16),
            pltpu.VMEM((nd, 512), i32),
            pltpu.VMEM((nx, ny, 512), i32),
            pltpu.VMEM((nx, ny, 512), i32),
            pltpu.VMEM((ny, nx, 64, 512), bf16),
            pltpu.VMEM((nd, 128, 512), bf16),
            pltpu.VMEM((nd * 512 + 8, 128), f32),
            pltpu.VMEM((nz, 2, 128, 256), bf16),
            pltpu.VMEM(adj_one.shape, i32),
            pltpu.VMEM(deg_one.shape, i32),
            pltpu.VMEM(self_slots.shape, i32),
            pltpu.VMEM((16, ROWS), i32),
            pltpu.VMEM((lists, 128), i32),
            pltpu.SMEM((lists, 128), i32),
            pltpu.VMEM((half, 128), f32),
            pltpu.VMEM((block, 128), f32),
            pltpu.VMEM((block, 128), f32),
            pltpu.VMEM(adj_two.shape, i32),
            pltpu.VMEM(deg_two.shape, i32),
            pltpu.VMEM((256, 256), bf16),
            pltpu.VMEM((256, 256), bf16),
            pltpu.VMEM(out_grad.shape, bf16),
            pltpu.VMEM((64, ROWS), bf16),
            pltpu.VMEM((64, 256), f32),
            pltpu.VMEM((nz, block, 256), bf16),
            pltpu.VMEM((nz, block, 256), bf16),
            pltpu.VMEM((ROWS, 256), f32),
            pltpu.VMEM((nf, block, 256), bf16),
            pltpu.VMEM((nz, block, 256), bf16),
            pltpu.VMEM((nd, 64, 256), bf16),
            pltpu.VMEM((256, 128), bf16),
            pltpu.VMEM((256, half), bf16),
            pltpu.VMEM((nd, 16, 128), bf16),
            pltpu.VMEM((32, nd * 64), bf16),
            pltpu.VMEM((2, 2, 64, 256), f32),
            pltpu.VMEM((2, 64, 256), f32),
            pltpu.VMEM((128, 256), f32),
            pltpu.VMEM((nd, 8, 128), f32),
            pltpu.VMEM((8, 128), f32),
            dma((11,)),
            dma((1,)), dma((ny - 1,)), dma((1,)), dma((ny - 1,)),
            dma((1,)), dma((1,)), dma((1,)), dma((ny,)), dma((1,)), dma((ny,)),
            dma((1,)), dma((1,)), dma((5,)), dma((5,)),
            dma((1,)), dma((nz,)), dma((1,)), dma((1,)), dma((1,)), dma((1,)),
            dma((1,)), dma((1,)), dma((1,)), dma((1,)),
            dma((1,)), dma((1,)), dma((1,)), dma((1,)),
            dma((1,)), dma((1,)), dma((1,)),
        ],
        compiler_params=pltpu.CompilerParams(
            collective_id=1, has_side_effects=True, vmem_limit_bytes=60 * 1024 * 1024
        ),
        name="train_step",
    )(
        features.T, request_rows[0], w1_self, w1_neigh, adj_one, deg_one, self_slots,
        adj_two, deg_two, w2_self, w2_neigh, out_grad,
    )
    return pl.pallas_call(
        finish_kernel,
        out_shape=(
            jax.ShapeDtypeStruct((64, 256), bf16),
            jax.ShapeDtypeStruct((64, 256), f32),
            jax.ShapeDtypeStruct((64, 256), f32),
            jax.ShapeDtypeStruct((256, 256), f32),
            jax.ShapeDtypeStruct((256, 256), f32),
        ),
        in_specs=[vmem] * 3,
        out_specs=(vmem,) * 5,
        compiler_params=pltpu.CompilerParams(vmem_limit_bytes=60 * 1024 * 1024),
        name="finish",
    )(emb, gw1, gw2)


def solution(mesh):
    return jax.shard_map(
        functools.partial(local, mesh.shape["dp"], mesh.shape["feat"]),
        mesh=mesh,
        in_specs=(
            P("dp", "feat"),
            P("dp", None, None),
            P("dp", None),
            P("dp", None, None),
            P("dp", None),
            P("dp", None, None),
            P("dp", None),
            P("feat", None),
            P("feat", None),
            P(),
            P(),
            P("dp", None),
        ),
        out_specs=(P("dp", None), P("feat", None), P("feat", None), P(), P()),
        check_vma=False,
    )
```

```python
import functools

import jax
import jax.numpy as jnp
from jax import lax
from jax.experimental import pallas as pl
from jax.experimental.pallas import tpu as pltpu
from jax.sharding import PartitionSpec as P

MESH = pl.DeviceIdType.MESH
ROWS = 768


def contract_rows(a, b):
    return lax.dot_general(a, b, (((0,), (0,)), ((), ())), preferred_element_type=jnp.float32)


def contract_lanes(a, b):
    return lax.dot_general(a, b, (((1,), (1,)), ((), ())), preferred_element_type=jnp.float32)


Z_ORDER = (4, 3, 5, 2, 6, 1, 7)


def step_kernel(
    nd, nf,
    feat_any, req_any, w1s_any, w1n_any, adj_any, deg_any, self_any,
    adj_two_any, deg_two_any, w2s_any, w2n_any, grad_any,
    emb_ref, gw1_ref, gw2_ref,
    blocks, req_ref, req_by_x, req_in, stage, samp, table, w1,
    adj_ref, deg_ref, self_ref, padded, lists, slots, scale, own, total,
    adj_two, deg_two, w2s, w2n, grad_ref, counts_ref, degree_ref,
    x_out, x_in, gh_buf, hid, gpre, grads, turned, rows_t, w2_in, left, part, part_in, part1, in1, sum1,
    fetch, up_send, up_recv, down_send, down_recv, req_send, req_recv, x_send, x_recv,
    pair_send, pair_recv, w1_send, w1_recv, sib_send, sib_recv, a_send, a_recv, h_send, h_recv,
    p_send, p_recv, g_send, g_recv, q_send, q_recv, r_send, r_recv, b_send, b_recv,
    f_send, f_recv, smem_sem,
):
    d = lax.axis_index("dp")
    f = lax.axis_index("feat")
    nx, ny, nz = 4, nd // 4, nf // 2
    cap = 512
    x, y = lax.rem(d, nx), lax.div(d, nx)
    z, c = lax.div(f, 2), lax.rem(f, 2)
    block, half_rows = ROWS // nf, ROWS // 2
    mine = c * nz + z
    sibling = (d, 2 * z + 1 - c)

    def at_x(j):
        return lax.rem(x + j, nx)

    def at_y(s):
        return lax.rem(y + s + ny, ny)

    def along_z(k):
        to = lax.rem(z + k, nz)
        return to, (d, 2 * to + c)

    offsets = [(dx, dy) for dy in range(ny) for dx in range(nx) if dx + dy > 0]
    offsets.sort(key=lambda o: -min(o[0], nx - o[0]) - min(o[1], ny - o[1]))

    def to_dp_peers(copy_to):
        for dx, dy in offsets:
            copy_to(at_y(dy) * nx + at_x(dx)).start()

    def remote(src, dst, send_sem, recv_sem, to):
        return pltpu.make_async_remote_copy(
            src_ref=src, dst_ref=dst, send_sem=send_sem, recv_sem=recv_sem,
            device_id=to, device_id_type=MESH,
        )

    def all_in(ref, sem):
        remote(ref, ref, sem, sem, sibling).wait_recv()

    def all_out(ref, sem):
        remote(ref, ref, sem, sem, sibling).wait_send()

    def core_rows(core, size):
        return pl.ds(pl.multiple_of(core * size, 16), size)

    barrier = pltpu.get_barrier_semaphore()

    def greet(to):
        pl.semaphore_signal(barrier, inc=1, device_id=to, device_id_type=MESH)

    sources = [
        (feat_any.at[:, 512 * q:512 * q + 512], blocks.at[y, 64 * q:64 * q + 64, :]) for q in range(4)
    ] + [
        (req_any, req_ref),
        (w1s_any, w1.at[z, 0, core_rows(c, 64), :]),
        (w1n_any, w1.at[z, 1, core_rows(c, 64), :]),
        (adj_any, adj_ref), (deg_any, deg_ref), (self_any, self_ref),
        (adj_two_any, adj_two), (deg_two_any, deg_two),
        (w2s_any, w2s), (w2n_any, w2n), (grad_any, grad_ref),
    ]
    kinds = (0, 0, 0, 0, 1, 2, 2, 3, 4, 5, 6, 7, 8, 9, 10)
    fetches = [pltpu.make_async_copy(src, dst, fetch.at[i]) for i, (src, dst) in zip(kinds, sources)]
    for copy in [fetches[4]] + fetches[:4] + fetches[5:7]:
        copy.start()

    for s in (1, -1):
        greet((at_y(s) * nx + x, f))
    for j in range(1, nx):
        greet((y * nx + at_x(j), f))
    greet(sibling)
    for k in range(1, nz):
        greet(along_z(k)[1])
    pl.semaphore_wait(barrier, 2 + nx - 1 + 1 + nz - 1)

    def req_copy(j):
        to = at_x(j)
        return remote(req_by_x.at[to], req_in.at[x], req_send.at[0], req_recv.at[0], (y * nx + to, f))

    def half(source, h):
        return blocks.at[source, core_rows(h, 128), :]

    def up_copy(t, source):
        part = half(source, lax.rem(t, 2))
        return remote(part, part, up_send.at[0], up_recv.at[t], (at_y(1) * nx + x, f))

    def down_copy(t, source):
        part = half(source, 1 - lax.rem(t, 2))
        return remote(part, part, down_send.at[0], down_recv.at[t], (at_y(-1) * nx + x, f))

    def w1_part(source):
        return w1.at[source, :, core_rows(c, 64), :]

    def w1_copy(k):
        return remote(w1_part(z), w1_part(z), w1_send.at[0], w1_recv.at[0], along_z(k)[1])

    def w1_over(core):
        ours = w1.at[:, :, core_rows(core, 64), :]
        return remote(ours, ours, sib_send.at[0], sib_recv.at[0], sibling)

    def first_copies(t):
        copies = []
        for up, h in ((True, t % 2), (False, 1 - t % 2)):
            for q in (2 * h, 2 * h + 1):
                copies.append(remote(
                    feat_any.at[:, 512 * q:512 * q + 512], blocks.at[y, 64 * q:64 * q + 64, :],
                    (up_send if up else down_send).at[0], (up_recv if up else down_recv).at[t],
                    (at_y(1 if up else -1) * nx + x, f),
                ))
        return copies

    for t in range(2):
        for copy in first_copies(t):
            copy.start()
    for copy in fetches[7:]:
        copy.start()
    fetches[4].wait()
    for owner in range(nd):
        req_by_x[owner % nx, owner // nx:owner // nx + 1, :] = req_ref[owner:owner + 1, :]
    for j in range(1, nx):
        req_copy(j).start()
    pltpu.make_async_copy(blocks.at[y], blocks.at[y], fetch.at[0]).wait()
    pltpu.make_async_copy(w1.at[z, :, core_rows(c, 64), :], w1.at[z, :, core_rows(c, 64), :], fetch.at[2]).wait()
    req_in[x] = req_by_x[x]
    all_in(req_in.at[pl.ds(0, nx - 1)], req_recv.at[0])

    def x_copy(source, j):
        slot = source * nx + x
        return remote(
            stage.at[source, j], samp.at[slot, core_rows(c, 64), :],
            x_send.at[0], x_recv.at[source], (y * nx + at_x(j), f),
        )

    def slots_of(source, count, core):
        return samp.at[pl.ds(source * nx, count), core_rows(core, 64), :]

    def pair_copy(source, core):
        ours = slots_of(source, nx, core)
        return remote(ours, ours, pair_send.at[0], pair_recv.at[source], sibling)

    node = lax.broadcasted_iota(jnp.int32, (512, cap), 0)

    def pick(source, j):
        asked = req_in[at_x(j), pl.ds(source, 1), :]
        low, quarter = asked & 511, asked >> 9
        one_hot = jnp.where(node == low, 1.0, 0.0).astype(jnp.bfloat16)
        rows = jnp.dot(blocks[source], one_hot, preferred_element_type=jnp.float32)
        chosen = rows[192:256, :]
        for q in range(3):
            chosen = jnp.where(quarter == q, rows[64 * q:64 * q + 64, :], chosen)
        return chosen.astype(jnp.bfloat16)

    def process(count, source_of):
        def step(k, carry):
            source = source_of(lax.div(k, nx))
            late = lax.div(lax.rem(k, nx), 2)
            j = (2 + lax.rem(k, nx)) * (1 - late) + (3 - lax.rem(k, nx)) * late
            stage[source, j] = pick(source, j)

            @pl.when(j > 0)
            def _():
                x_copy(source, j).start()

            return carry

        lax.fori_loop(0, count * nx, step, 0)

    def collect(count, source_of):
        def step(u, carry):
            source = source_of(u)
            all_in(slots_of(source, nx - 1, c), x_recv.at[source])
            samp[source * nx + x, core_rows(c, 64), :] = stage[source, 0]
            pair_copy(source, c).start()
            return carry

        lax.fori_loop(0, count, step, 0)

    def absorb(count, source_of):
        def step(u, carry):
            source = source_of(u)
            pair_copy(source, 1 - c).wait_recv()
            for j in range(nx):
                slot = source * nx + j
                here = pl.ds(pl.multiple_of(slot * cap, 8), cap)
                table[here, :] = samp[slot].astype(jnp.float32).T
            return carry

        lax.fori_loop(0, count, step, 0)

    for k in Z_ORDER:
        w1_copy(k).start()
    steps = ny // 2

    def in_step(i):
        return 2 - lax.div(steps - i, steps) - lax.div(i, steps)

    def source_in(i):
        return lambda u: lax.rem(y + (2 * u - 1) * i + ny, ny)

    def pass_on(t, i):
        below, above = at_y(-i), at_y(i)
        more = t + 2 < ny - 1
        up_copy(t, below).wait_recv()

        @pl.when(more)
        def _():
            up_copy(t + 2, below).start()

        down_copy(t, above).wait_recv()

        @pl.when(more)
        def _():
            down_copy(t + 2, above).start()

    def gather_late(i):
        @pl.when(i >= 3)
        def _():
            absorb(in_step(i - 3), source_in(i - 3))

        @pl.when((i >= 2) & (i <= steps + 2))
        def _():
            collect(in_step(i - 2), source_in(i - 2))

    fanout = adj_ref.shape[0]
    present = self_ref.shape[1]
    targets = deg_two.shape[1]
    to_smem = pltpu.make_async_copy(lists, slots, smem_sem.at[0])

    def prepare():
        for copy in fetches[7:]:
            copy.wait()
        table[nd * cap:, :] = jnp.zeros((8, 128), jnp.float32)
        padded[...] = jnp.full(padded.shape, nd * cap, jnp.int32)
        for j in range(fanout):
            padded[j:j + 1, :present] = jnp.where(deg_ref[...] > j, adj_ref[j], nd * cap)
        padded[fanout:fanout + 1, :present] = self_ref[...]
        my_lanes_half = pl.ds(pl.multiple_of(c * half_rows, 128), half_rows)
        for j in range(fanout + 1):
            line = padded[j:j + 1, my_lanes_half]
            for to in range(nz):
                at = to * (fanout + 1) + j
                lists[at:at + 1, :block] = line[:, block * to:block * to + block]
        to_smem.start()
        padded[:1, :] = jnp.ones((1, ROWS), jnp.int32)
        padded[:1, :present] = deg_ref[...]
        inverse = 1.0 / padded[:1, my_lanes_half].astype(jnp.float32)
        scale[...] = jnp.broadcast_to(jnp.broadcast_to(inverse, (8, half_rows)).T[:, :1], scale.shape)

        out_grad = grad_ref[...]
        degree_row = deg_two[...]
        row = lax.broadcasted_iota(jnp.int32, (ROWS, targets), 0)
        counts = jnp.zeros((ROWS, targets), jnp.float32)
        for j in range(fanout):
            listed = jnp.where(degree_row > j, adj_two[j], -1)
            counts = counts + jnp.where(row == listed, 1.0, 0.0)
        degree_row = degree_row.astype(jnp.float32)
        degree = jnp.broadcast_to(degree_row, (8, targets)).T[:, :1]
        degree_ref[...] = jnp.broadcast_to(degree, degree_ref.shape)
        grad_agg = contract_lanes(out_grad, w2n[...]) / degree
        high = grad_agg.astype(jnp.bfloat16)
        low = (grad_agg - high.astype(jnp.float32)).astype(jnp.bfloat16)
        both = jnp.concatenate([counts, counts], axis=1).astype(jnp.bfloat16)
        gh_buf[...] = jnp.dot(both, jnp.concatenate([high, low], axis=0), preferred_element_type=jnp.float32)
        gh_buf[:targets, :] += contract_lanes(out_grad, w2s[...])
        counts_ref[...] = counts.T.astype(jnp.bfloat16)

    def ring_step(i, carry):
        @pl.when(i > 0)
        def _():
            pass_on(2 * i - 2, i)

        @pl.when((i > 0) & (i < steps))
        def _():
            pass_on(2 * i - 1, i)

        process(in_step(i), source_in(i))

        @pl.when(i == 1)
        def _():
            prepare()

        gather_late(i)
        return carry

    lax.fori_loop(0, steps + 1, ring_step, 0)

    lax.fori_loop(steps + 1, steps + 4, lambda i, carry: (gather_late(i), carry)[1], 0)

    g_rows = core_rows(c, 32)

    def grad_copy(to):
        return remote(grad_ref.at[g_rows, :], grads.at[d, g_rows, :], g_send.at[0], g_recv.at[0], (to, f))

    some_grads = grads.at[pl.ds(0, nd - 1), pl.ds(0, 32), :]

    to_smem.wait()
    all_in(w1.at[pl.ds(0, nz - 1), :, pl.ds(0, 64), :], w1_recv.at[0])
    w1_over(c).start()

    def row_copy(k):
        to, device = along_z(k)
        return remote(x_out.at[to], x_in.at[z], a_send.at[0], a_recv.at[z], device)

    def row_back(k):
        source, device = along_z(k)
        return remote(x_out.at[source], x_in.at[source], a_send.at[0], a_recv.at[source], device)

    def sum_rows(t, carry):
        odd = lax.rem(t, 2)
        k = nz // 2 + lax.div(t, 2) * (1 - odd) - lax.div(t + 1, 2) * odd
        to = lax.rem(z + k, nz)
        base = to * (fanout + 1)
        for i in range(block):
            own[i:i + 1, :] = table[pl.ds(slots[base + fanout, i], 1), :]
            terms = [table[pl.ds(slots[base + j, i], 1), :] for j in range(fanout)]
            while len(terms) > 1:
                terms = [sum(terms[n:n + 2][1:], terms[n]) for n in range(0, len(terms), 2)]
            total[i:i + 1, :] = terms[0]
        x_out[to, :, :128] = own[...].astype(jnp.bfloat16)
        mean = total[...] * scale[pl.ds(pl.multiple_of(to * block, 8), block), :]
        x_out[to, :, 128:] = mean.astype(jnp.bfloat16)

        @pl.when(k > 0)
        def _():
            row_copy(k).start()

        return carry

    lax.fori_loop(0, nz, sum_rows, 0)
    x_in[z] = x_out[z]
    rows_t[...] = x_out[...].reshape(half_rows, 256).astype(jnp.float32).T.astype(jnp.bfloat16)
    w1_over(1 - c).wait_recv()

    pre = jnp.zeros((block, w1.shape[-1]), jnp.float32)
    for k in (0, 5, 4, 6, 3, 7, 2, 1):
        if k > 0:
            row_back(k).wait_recv()
        source = lax.rem(z + k, nz)
        pre = pre + jnp.dot(
            x_in[source], w1[source].reshape(256, w1.shape[-1]), preferred_element_type=jnp.float32
        )
    sig = 1.0 / (1.0 + jnp.exp(-pre))
    my_gh = gh_buf[pl.ds(pl.multiple_of(mine * block, 8), block), :]
    hid[mine] = (pre * sig).astype(jnp.bfloat16)
    gpre[z] = (my_gh * (sig * (1.0 + pre * (1.0 - sig)))).astype(jnp.bfloat16)

    def spread(buf, send_sem, recv_sem, k):
        return remote(buf.at[mine], buf.at[mine], send_sem.at[0], recv_sem.at[0], along_z(k)[1])

    def most(buf):
        return buf.at[pl.ds(0, nz - 1)]

    def hand_over(buf, core, i):
        ours = buf.at[pl.ds(core * nz, nz)]
        return remote(ours, ours, sib_send.at[i], sib_recv.at[i], sibling)

    def gpre_copy(k):
        return remote(gpre.at[z], gpre.at[z], p_send.at[0], p_recv.at[0], along_z(k)[1])

    for k in Z_ORDER:
        spread(hid, h_send, h_recv, k).start()
    for k in Z_ORDER:
        gpre_copy(k).start()
    to_dp_peers(grad_copy)
    grads[d, g_rows, :] = grad_ref[g_rows, :]
    all_in(most(hid), h_recv.at[0])
    hand_over(hid, c, 1).start()
    all_in(most(gpre), p_recv.at[0])
    sums = jnp.dot(
        rows_t[...], gpre[...].reshape(half_rows, gpre.shape[-1]), preferred_element_type=jnp.float32
    )
    part[...] = sums.reshape(part.shape)

    def part_copy(core):
        return remote(part.at[:, core], part_in, sib_send.at[2], sib_recv.at[2], sibling)

    part_copy(1 - c).start()
    hand_over(hid, 1 - c, 1).wait_recv()

    hidden = hid[...].reshape(ROWS, hid.shape[-1])
    self_hidden = hidden[:targets, :]
    agg_two = jnp.dot(counts_ref[...], hidden, preferred_element_type=jnp.float32) / degree_ref[...]
    agg_two = agg_two.astype(jnp.bfloat16)
    pair = jnp.concatenate([self_hidden, agg_two], axis=0)
    turned[...] = pair.astype(jnp.float32).T.astype(jnp.bfloat16)
    columns = core_rows(f, 16)

    def w2_copy(to):
        return remote(turned.at[columns, :], w2_in.at[d], q_send.at[0], q_recv.at[0], (to, f))

    to_dp_peers(w2_copy)
    w2_in[d] = turned[columns, :]

    part_copy(c).wait_recv()
    part1[...] = (part[:, c] + part_in[...]).reshape(part1.shape)

    def tile_of(index):
        return (
            pl.ds(pl.multiple_of(lax.div(index, 2) * 8, 8), 8),
            pl.ds(pl.multiple_of(lax.rem(index, 2) * 128, 128), 128),
        )

    my_rows, my_lanes = tile_of(d)

    def w1_sum_copy(to):
        rows, lanes = tile_of(to)
        return remote(part1.at[rows, lanes], in1.at[d], r_send.at[0], r_recv.at[0], (to, f))

    some_tiles = in1.at[pl.ds(0, nd - 1)]
    to_dp_peers(w1_sum_copy)
    in1[d] = part1[my_rows, my_lanes]

    all_in(some_grads, g_recv.at[0])

    def grads_over(core):
        ours = grads.at[:, core_rows(core, 32), :]
        return remote(ours, ours, sib_send.at[3], sib_recv.at[3], sibling)

    grads_over(c).start()
    emb = jnp.dot(self_hidden, w2s[...], preferred_element_type=jnp.float32)
    emb = emb + jnp.dot(agg_two, w2n[...], preferred_element_type=jnp.float32)
    emb_ref[...] = emb.astype(jnp.bfloat16)
    grads_over(1 - c).wait_recv()
    all_in(w2_in.at[pl.ds(0, nd - 1)], q_recv.at[0])
    lane = lax.broadcasted_iota(jnp.int32, (16, 128), 1)
    for p in range(nd // 2):
        first, second = w2_in[2 * p].astype(jnp.float32), w2_in[2 * p + 1].astype(jnp.float32)
        selfs = jnp.where(lane < 64, first, pltpu.roll(second, 64, 1))
        neighs = jnp.where(lane < 64, pltpu.roll(first, 64, 1), second)
        left[:, 128 * p:128 * p + 128] = jnp.concatenate([selfs, neighs], axis=0).astype(jnp.bfloat16)
    total2 = jnp.dot(
        left[...], grads[...].reshape(nd * targets, grads.shape[-1]), preferred_element_type=jnp.float32
    )
    gw2_ref[mine] = total2.astype(jnp.bfloat16)
    for k in Z_ORDER:
        spread(gw2_ref, f_send, f_recv, k).start()

    all_in(some_tiles, r_recv.at[0])
    sum1[...] = jnp.sum(in1[...], axis=0)
    gw1_ref[my_rows, my_lanes] = sum1[...]

    def w1_out(to):
        return remote(sum1, gw1_ref.at[my_rows, my_lanes], b_send.at[0], b_recv.at[0], (to, f))

    to_dp_peers(w1_out)
    all_in(most(gw2_ref), f_recv.at[0])
    hand_over(gw2_ref, c, 4).start()

    all_out(req_in.at[pl.ds(0, nx - 1)], req_send.at[0])
    all_out(blocks.at[pl.ds(0, ny - 1), pl.ds(0, 128), :], up_send.at[0])
    all_out(blocks.at[pl.ds(0, ny - 1), pl.ds(0, 128), :], down_send.at[0])
    all_out(w1.at[pl.ds(0, nz - 1), :, pl.ds(0, 64), :], w1_send.at[0])
    all_out(most(x_out), a_send.at[0])
    all_out(most(hid), h_send.at[0])
    all_out(most(gpre), p_send.at[0])
    all_out(most(gw2_ref), f_send.at[0])
    w1_over(c).wait_send()
    hand_over(hid, c, 1).wait_send()
    part_copy(1 - c).wait_send()
    grads_over(c).wait_send()
    all_out(stage.at[:, pl.ds(0, nx - 1)], x_send.at[0])
    all_out(samp.at[:, core_rows(c, 64), :], pair_send.at[0])
    all_out(some_grads, g_send.at[0])
    all_out(w2_in.at[pl.ds(0, nd - 1)], q_send.at[0])
    all_out(some_tiles, r_send.at[0])
    hand_over(gw2_ref, 1 - c, 4).wait_recv()
    hand_over(gw2_ref, c, 4).wait_send()
    all_in(some_tiles, b_recv.at[0])
    all_out(some_tiles, b_send.at[0])


def finish_kernel(emb_ref, gw1_ref, gw2_ref, out_emb, out_1s, out_1n, out_2s, out_2n):
    out_emb[...] = emb_ref[...]
    out_1s[...] = gw1_ref[:64, :]
    out_1n[...] = gw1_ref[64:, :]
    nz = gw2_ref.shape[0] // 2
    for i in range(2 * nz):
        f = 2 * (i % nz) + i // nz
        out_2s[16 * f:16 * f + 16, :] = gw2_ref[i, :16, :].astype(jnp.float32)
        out_2n[16 * f:16 * f + 16, :] = gw2_ref[i, 16:, :].astype(jnp.float32)


def local(
    nd, nf,
    features, request_rows, self_slots, adj_one, deg_one, adj_two, deg_two,
    w1_self, w1_neigh, w2_self, w2_neigh, out_grad,
):
    vmem = pl.BlockSpec(memory_space=pltpu.VMEM)
    anywhere = pl.BlockSpec(memory_space=pltpu.HBM)
    f32, bf16, i32 = jnp.float32, jnp.bfloat16, jnp.int32
    dma = pltpu.SemaphoreType.DMA
    nx, ny, nz = 4, nd // 4, nf // 2
    block, half = ROWS // nf, ROWS // 2
    adj_one = adj_one.transpose(2, 0, 1)
    adj_two = adj_two.transpose(2, 0, 1)
    lists = nz * (adj_one.shape[0] + 1)
    emb, gw1, gw2 = pl.pallas_call(
        functools.partial(step_kernel, nd, nf),
        out_shape=(
            jax.ShapeDtypeStruct((64, 256), bf16),
            jax.ShapeDtypeStruct((128, 256), f32),
            jax.ShapeDtypeStruct((nf, 32, 256), bf16),
        ),
        in_specs=[anywhere] * 12,
        out_specs=(vmem,) * 3,
        scratch_shapes=[
            pltpu.VMEM((ny, 256, 512), bf16),
            pltpu.VMEM((nd, 512), i32),
            pltpu.VMEM((nx, ny, 512), i32),
            pltpu.VMEM((nx, ny, 512), i32),
            pltpu.VMEM((ny, nx, 64, 512), bf16),
            pltpu.VMEM((nd, 128, 512), bf16),
            pltpu.VMEM((nd * 512 + 8, 128), f32),
            pltpu.VMEM((nz, 2, 128, 256), bf16),
            pltpu.VMEM(adj_one.shape, i32),
            pltpu.VMEM(deg_one.shape, i32),
            pltpu.VMEM(self_slots.shape, i32),
            pltpu.VMEM((16, ROWS), i32),
            pltpu.VMEM((lists, 128), i32),
            pltpu.SMEM((lists, 128), i32),
            pltpu.VMEM((half, 128), f32),
            pltpu.VMEM((block, 128), f32),
            pltpu.VMEM((block, 128), f32),
            pltpu.VMEM(adj_two.shape, i32),
            pltpu.VMEM(deg_two.shape, i32),
            pltpu.VMEM((256, 256), bf16),
            pltpu.VMEM((256, 256), bf16),
            pltpu.VMEM(out_grad.shape, bf16),
            pltpu.VMEM((64, ROWS), bf16),
            pltpu.VMEM((64, 256), f32),
            pltpu.VMEM((nz, block, 256), bf16),
            pltpu.VMEM((nz, block, 256), bf16),
            pltpu.VMEM((ROWS, 256), f32),
            pltpu.VMEM((nf, block, 256), bf16),
            pltpu.VMEM((nz, block, 256), bf16),
            pltpu.VMEM((nd, 64, 256), bf16),
            pltpu.VMEM((256, 128), bf16),
            pltpu.VMEM((256, half), bf16),
            pltpu.VMEM((nd, 16, 128), bf16),
            pltpu.VMEM((32, nd * 64), bf16),
            pltpu.VMEM((2, 2, 64, 256), f32),
            pltpu.VMEM((2, 64, 256), f32),
            pltpu.VMEM((128, 256), f32),
            pltpu.VMEM((nd, 8, 128), f32),
            pltpu.VMEM((8, 128), f32),
            dma((11,)),
            dma((1,)), dma((ny - 1,)), dma((1,)), dma((ny - 1,)),
            dma((1,)), dma((1,)), dma((1,)), dma((ny,)), dma((1,)), dma((ny,)),
            dma((1,)), dma((1,)), dma((5,)), dma((5,)),
            dma((1,)), dma((nz,)), dma((1,)), dma((1,)), dma((1,)), dma((1,)),
            dma((1,)), dma((1,)), dma((1,)), dma((1,)),
            dma((1,)), dma((1,)), dma((1,)), dma((1,)),
            dma((1,)), dma((1,)), dma((1,)),
        ],
        compiler_params=pltpu.CompilerParams(
            collective_id=1, has_side_effects=True, vmem_limit_bytes=60 * 1024 * 1024
        ),
        name="train_step",
    )(
        features.T, request_rows[0], w1_self, w1_neigh, adj_one, deg_one, self_slots,
        adj_two, deg_two, w2_self, w2_neigh, out_grad,
    )
    return pl.pallas_call(
        finish_kernel,
        out_shape=(
            jax.ShapeDtypeStruct((64, 256), bf16),
            jax.ShapeDtypeStruct((64, 256), f32),
            jax.ShapeDtypeStruct((64, 256), f32),
            jax.ShapeDtypeStruct((256, 256), f32),
            jax.ShapeDtypeStruct((256, 256), f32),
        ),
        in_specs=[vmem] * 3,
        out_specs=(vmem,) * 5,
        compiler_params=pltpu.CompilerParams(vmem_limit_bytes=60 * 1024 * 1024),
        name="finish",
    )(emb, gw1, gw2)


def solution(mesh):
    return jax.shard_map(
        functools.partial(local, mesh.shape["dp"], mesh.shape["feat"]),
        mesh=mesh,
        in_specs=(
            P("dp", "feat"),
            P("dp", None, None),
            P("dp", None),
            P("dp", None, None),
            P("dp", None),
            P("dp", None, None),
            P("dp", None),
            P("feat", None),
            P("feat", None),
            P(),
            P(),
            P("dp", None),
        ),
        out_specs=(P("dp", None), P("feat", None), P("feat", None), P(), P()),
        check_vma=False,
    )
```
